32 devices in a mesh: fsdp: 8 (over y, x, core), sp: 4 (over z).
Axes of the slice: x: 2, y: 2, z: 4, core: 2. Of those that a mesh axis runs over, the one named last changes fastest.
Arguments:
- inputs: bfloat16 [8, 1536, 1024], P('fsdp', 'sp'), may hold values from -6 to 6
- segments: int32 [8, 1536], P('fsdp', 'sp'), may hold values from 0 to 4, as said below
- enc_states: bfloat16 [8, 1024, 1024], P('fsdp', 'sp'), may hold values from -6 to 6
- adapter_pick: int32 [8], P('fsdp'), may hold values from 0 to 7
- qkv_weights: bfloat16 [1, 6, 1024, 1024], P(None, None, 'fsdp'), may hold values from -0.1875 to 0.1875
- out_weights: bfloat16 [1, 2, 1024, 1024], P(None, None, 'fsdp'), may hold values from -0.75 to 0.75
- mlp_in: bfloat16 [1, 1024, 4096], P(None, 'fsdp'), may hold values from -0.1875 to 0.1875
- mlp_out: bfloat16 [1, 4096, 1024], P(None, 'fsdp'), may hold values from -0.09375 to 0.09375
- proj_down: bfloat16 [1, 8, 8, 16, 1024], replicated, may hold values from -0.1875 to 0.1875
- proj_up: bfloat16 [1, 8, 8, 16, 1024], replicated, may hold values from -0.75 to 0.75
- fc1_down: bfloat16 [1, 8, 16, 1024], replicated, may hold values from -0.1875 to 0.1875
- fc1_up: bfloat16 [1, 8, 16, 4096], replicated, may hold values from -0.75 to 0.75
- fc2_down: bfloat16 [1, 8, 16, 4096], replicated, may hold values from -0.09375 to 0.09375
- fc2_up: bfloat16 [1, 8, 16, 1024], replicated, may hold values from -0.75 to 0.75
- cotangent: bfloat16 [8, 1536, 1024], P('fsdp', 'sp'), may hold values from -6 to 6
Outputs:
- output: bfloat16 [8, 1536, 1024], P('fsdp', 'sp')
- input_grad: float32 [8, 1536, 1024], P('fsdp', 'sp')
- memory_grad: float32 [8, 1024, 1024], P('fsdp', 'sp')
- proj_down_grad: float32 [1, 8, 8, 16, 1024], replicated
- proj_up_grad: float32 [1, 8, 8, 16, 1024], replicated
- fc1_down_grad: float32 [1, 8, 16, 1024], replicated
- fc1_up_grad: float32 [1, 8, 16, 4096], replicated
- fc2_down_grad: float32 [1, 8, 16, 4096], replicated
- fc2_up_grad: float32 [1, 8, 16, 1024], replicated
The draws below stay inside these ranges and needn't reach their ends.
Inputs may be any that keep to these rules, and one draw needn't show every extreme that they name: `segments`: segment numbers never fall along a sequence; segment 2 starts within the first 384 tokens of every sequence and ends within its last 384; the last token is in segment 4.
All inputs are finite; a program needn't handle non-finite values.
Results may differ from the reference program's by a relative error of at most 0.025.
The reference program's roundings to bfloat16 on the way count: a program that leaves them out, or rounds other values in their place, can miss the bound.
Values may be sent and summed in bfloat16 or wider, within the bound.
No kernel may reach another device: no remote copies, remote signals or barrier semaphores. Data moves between devices by JAX's collectives and lax.ppermute only.
A program may use at most 192 MiB of HBM per device.

```python
import jax
import jax.numpy as jnp
from jax import lax

D = 1024
FF = 4096
HEADS = 16
HEAD = 64
RANK = 16
ADAPTERS = 8
LAYERS = 1
TOK_DEV = 384
ENC = 1024
SEQ_LEN = 1536
SEQS = 8


def draw_segments(key, part):
    key = jax.random.fold_in(key, 7)
    early_key, late_key = jax.random.split(key)
    early = jax.random.randint(early_key, (SEQS, 2), 1, TOK_DEV)
    late = jax.random.randint(late_key, (SEQS, 2), SEQ_LEN - TOK_DEV + 1, SEQ_LEN)
    bounds = jnp.concatenate([early, late], axis=1)
    positions = jnp.arange(SEQ_LEN)
    return jnp.sum((positions[None, :, None] >= bounds[:, None, :]).astype(jnp.int32), axis=-1).astype(jnp.int32)


def set_ends(values, key, least, high):
    dims = values.shape
    place = [jax.random.randint(jax.random.fold_in(key, axis), (), 0, dims[axis]) for axis in range(len(dims))]
    values = values.at[tuple(place)].set(least)
    longest = dims.index(max(dims))
    place[longest] = (place[longest] + 1) % dims[longest]
    return values.at[tuple(place)].set(high)


def block_levels(rng, dims, cuts, least, largest):
    level, own = 1.0, jax.random.fold_in(rng, 6)
    for dim, shards_of in cuts:
        heights = jnp.exp(jax.random.uniform(jax.random.fold_in(own, dim), (shards_of,), jnp.float32, least / len(cuts), largest / len(cuts)))
        level = level * jnp.repeat(heights, dims[dim] // shards_of).reshape([-1 if axis == dim else 1 for axis in range(len(dims))])
    return level


def normal_values(stream_key, extent, spread, reach, cuts=(), kind=jnp.bfloat16):
    values = spread * jax.random.normal(stream_key, extent, jnp.float32)
    if cuts:
        values = values * block_levels(stream_key, extent, cuts, -0.22, 0.18)
    return jnp.clip(values, -reach, reach).astype(kind)


def setup_inputs(seed: int = 0) -> dict:
    key_list = jax.random.split(jax.random.key(seed), 16)
    inputs = normal_values(key_list[0], (SEQS, SEQ_LEN, D), 1.0, 6.0, ((0, 8), (1, 4)))
    segments = draw_segments(jax.random.fold_in(key_list[15], 71), 0)
    enc_states = normal_values(key_list[2], (SEQS, ENC, D), 1.0, 6.0, ((0, 8), (1, 4)))
    adapter_pick = set_ends(jax.random.randint(key_list[3], (SEQS,), 0, ADAPTERS), jax.random.fold_in(key_list[3], 1), 0, ADAPTERS - 1).astype(jnp.int32)
    qkv_weights = normal_values(key_list[4], (LAYERS, 6, D, D), D ** -0.5, 0.1875, ((2, 8),))
    out_weights = normal_values(key_list[5], (LAYERS, 2, D, D), (D // 16) ** -0.5, 0.75, ((2, 8),))
    mlp_in = normal_values(key_list[6], (LAYERS, D, FF), D ** -0.5, 0.1875, ((1, 8),))
    mlp_out = normal_values(key_list[7], (LAYERS, FF, D), FF ** -0.5, 0.09375, ((1, 8),))
    proj_down = normal_values(key_list[8], (LAYERS, 8, ADAPTERS, RANK, D), D ** -0.5, 0.1875)
    proj_up = normal_values(key_list[9], (LAYERS, 8, ADAPTERS, RANK, D), (4 * RANK) ** -0.5, 0.75)
    fc1_down = normal_values(key_list[10], (LAYERS, ADAPTERS, RANK, D), D ** -0.5, 0.1875)
    fc1_up = normal_values(key_list[11], (LAYERS, ADAPTERS, RANK, FF), (4 * RANK) ** -0.5, 0.75)
    fc2_down = normal_values(key_list[12], (LAYERS, ADAPTERS, RANK, FF), FF ** -0.5, 0.09375)
    fc2_up = normal_values(key_list[13], (LAYERS, ADAPTERS, RANK, D), (4 * RANK) ** -0.5, 0.75)
    cotangent = normal_values(key_list[14], (SEQS, SEQ_LEN, D), 1.0, 6.0, ((0, 8), (1, 4)))
    return {"inputs": inputs, "segments": segments, "enc_states": enc_states, "adapter_pick": adapter_pick, "qkv_weights": qkv_weights, "out_weights": out_weights, "mlp_in": mlp_in, "mlp_out": mlp_out, "proj_down": proj_down, "proj_up": proj_up, "fc1_down": fc1_down, "fc1_up": fc1_up, "fc2_down": fc2_down, "fc2_up": fc2_up, "cotangent": cotangent}


@jax.custom_vjp
def low(v):
    return lax.optimization_barrier(v.astype(jnp.bfloat16)).astype(jnp.float32)

@jax.custom_vjp
def low_back(v):
    return v

def low_keep(v):
    return (low(v), None)

def low_pass(kept, grad):
    return (grad,)

def back_keep(v):
    return (v, None)

def back_low(kept, grad):
    return (low(grad),)
low.defvjp(low_keep, low_pass)
low_back.defvjp(back_keep, back_low)

def narrow_both(values):
    return low_back(low(values))

def matmul(left, right):
    return jnp.dot(left, right, precision=lax.Precision.HIGHEST)

def project(rows_in, weight, down_proj, up_proj):
    hidden = narrow_both(matmul(rows_in, down_proj.T))
    return matmul(rows_in, weight) + matmul(hidden, up_proj)

def normalize(values):
    centered = values - lax.optimization_barrier(jnp.mean(values, -1, keepdims=True))
    variance = lax.optimization_barrier(jnp.mean(centered * centered, -1, keepdims=True))
    return centered * lax.rsqrt(variance + 1e-05)

def attend(queries, key_rows, value_rows, seg_ids, causal):
    length = queries.shape[0]
    block_rows = min(512, length)
    block_count = length // block_rows
    heads_q = queries.reshape(block_count, block_rows, HEADS, HEAD)
    heads_k = key_rows.reshape(-1, HEADS, HEAD)
    heads_v = value_rows.reshape(-1, HEADS, HEAD)
    key_pos = jnp.arange(key_rows.shape[0]).astype(jnp.int32)

    def run_block(packed):
        block_q, first_row = packed
        scores = low_back(jnp.einsum('qhd,khd->hqk', block_q, heads_k, precision=lax.Precision.HIGHEST) * HEAD ** (-0.5))
        if causal:
            query_pos = first_row + jnp.arange(block_rows).astype(jnp.int32)
            query_seg = lax.dynamic_slice_in_dim(seg_ids, first_row, block_rows)
            allowed = (query_seg[:, None] == seg_ids[None, :]) & (key_pos[None, :] <= query_pos[:, None])
            scores = jnp.where(allowed[None], scores, -1e+30)
        row_max = lax.optimization_barrier(jnp.max(scores, -1, keepdims=True))
        weights_exp = jnp.exp(scores - row_max)
        chances = low(weights_exp / lax.optimization_barrier(jnp.sum(weights_exp, -1, keepdims=True)))
        return jnp.einsum('hqk,khd->qhd', chances, heads_v, precision=lax.Precision.HIGHEST)
    starts = (jnp.arange(block_count) * block_rows).astype(jnp.int32)
    outputs = lax.map(jax.checkpoint(run_block), (heads_q, starts))
    return outputs.reshape(length, HEADS * HEAD)

def layer_forward(stream, memory_low, frozen, tables, seg_ids):
    w_in, w_out, w_up, w_down = frozen
    adapt_down, adapt_up, first_down, first_up, second_down, second_up = tables
    stream_low = low(stream)
    queries = narrow_both(project(stream_low, w_in[0], adapt_down[0], adapt_up[0]))
    key_rows = narrow_both(project(stream_low, w_in[1], adapt_down[1], adapt_up[1]))
    value_rows = narrow_both(project(stream_low, w_in[2], adapt_down[2], adapt_up[2]))
    attended = narrow_both(attend(queries, key_rows, value_rows, seg_ids, True))
    branch = low_back(project(attended, w_out[0], adapt_down[6], adapt_up[6]))
    first_norm = normalize(stream + branch)
    first_low = low(first_norm)
    cross_q = narrow_both(project(first_low, w_in[3], adapt_down[3], adapt_up[3]))
    cross_k = narrow_both(project(memory_low, w_in[4], adapt_down[4], adapt_up[4]))
    cross_v = narrow_both(project(memory_low, w_in[5], adapt_down[5], adapt_up[5]))
    crossed = narrow_both(attend(cross_q, cross_k, cross_v, seg_ids, False))
    branch = low_back(project(crossed, w_out[1], adapt_down[7], adapt_up[7]))
    second_norm = normalize(first_norm + branch)
    pre_act = low_back(project(low(second_norm), w_up, first_down, first_up))
    activated = low(jax.nn.gelu(pre_act, approximate=False))
    branch = low_back(project(activated, w_down, second_down, second_up))
    return normalize(second_norm + branch)

def sequence_forward(stream, memory, tables, seg_ids, pick, frozen):
    picked = (pick == jnp.arange(ADAPTERS)).astype(jnp.float32)
    high = lax.Precision.HIGHEST
    chosen = (jnp.einsum('a,lpard->lprd', picked, tables[0], precision=high), jnp.einsum('a,lpard->lprd', picked, tables[1], precision=high), jnp.einsum('a,lard->lrd', picked, tables[2], precision=high), jnp.einsum('a,lard->lrd', picked, tables[3], precision=high), jnp.einsum('a,lard->lrd', picked, tables[4], precision=high), jnp.einsum('a,lard->lrd', picked, tables[5], precision=high))
    memory_low = low(memory)
    for layer_at in range(LAYERS):
        layer_frozen = tuple((w[layer_at] for w in frozen))
        layer_tables = tuple((t[layer_at] for t in chosen))
        stream = layer_forward(stream, memory_low, layer_frozen, layer_tables, seg_ids)
    return stream

def reference(inputs, segments, enc_states, adapter_pick, qkv_weights, out_weights, mlp_in, mlp_out, proj_down, proj_up, fc1_down, fc1_up, fc2_down, fc2_up, cotangent):
    frozen = tuple((w.astype(jnp.float32) for w in (qkv_weights, out_weights, mlp_in, mlp_out)))
    tables = tuple((t.astype(jnp.float32) for t in (proj_down, proj_up, fc1_down, fc1_up, fc2_down, fc2_up)))

    def per_sequence(totals, item):
        stream, memory, seg_ids, pick, grad_out = item

        def forward(stream_in, memory_in, tables_in):
            return sequence_forward(stream_in, memory_in, tables_in, seg_ids, pick, frozen)
        result, pullback = jax.vjp(forward, stream.astype(jnp.float32), memory.astype(jnp.float32), tables)
        grad_stream, grad_memory, grad_tables = pullback(grad_out.astype(jnp.float32))
        totals = jax.tree.map(jnp.add, totals, grad_tables)
        return (totals, (result.astype(jnp.bfloat16), grad_stream, grad_memory))
    zeros = tuple((jnp.zeros_like(t) for t in tables))
    totals, stacked = lax.scan(per_sequence, zeros, (inputs, enc_states, segments, adapter_pick, cotangent))
    return (stacked[0], stacked[1], stacked[2], totals[0], totals[1], totals[2], totals[3], totals[4], totals[5])
```

```python
import functools

import jax
import jax.numpy as jnp
from jax import lax
from jax.experimental import pallas as pl
from jax.experimental.pallas import tpu as pltpu
from jax.sharding import Mesh
from jax.sharding import PartitionSpec as P

HEAD = 64
PAIR = 2 * HEAD
LANES = 128
NORM_EPS = 1e-05
FAR = -1e30
SEG_KINDS = 5
SEG_LANE = 3
F32 = jnp.float32
BF16 = jnp.bfloat16
VMEM = 60 * 1024 * 1024


def dot(left, right, dims):
    return lax.dot_general(left, right, ((dims[0], dims[1]), ((), ())), preferred_element_type=F32)


def nn(left, right):
    return dot(left, right, ((1,), (0,)))


def nt(left, right):
    return dot(left, right, ((1,), (1,)))


def tn(left, right):
    return dot(left, right, ((0,), (0,)))


def lane_of(rows):
    return lax.broadcasted_iota(jnp.int32, (rows, LANES), 1)


def split_pair(rows):
    low = lane_of(rows.shape[0]) < HEAD
    zero = jnp.zeros_like(rows)
    return jnp.concatenate([jnp.where(low, rows, zero), jnp.where(low, zero, rows)], axis=0)


def join_pair(rows):
    half = rows.shape[0] // 2
    return jnp.where(lane_of(half) < HEAD, rows[:half], rows[half:])


def three_terms(column):
    high = column.astype(BF16)
    rest = column - high.astype(F32)
    mid = rest.astype(BF16)
    low = (rest - mid.astype(F32)).astype(BF16)
    return high, mid, low


def spread_terms(terms, rest):
    lane = lane_of(terms[0].shape[0])
    out = rest
    for at, term in enumerate(terms):
        out = jnp.where(lane == at, term, out)
    return out


def attend_kernel(blocks, block, causal, s_ref, q_ref, qaug_ref, k_ref, v_ref, kaug_ref, out_ref, aug_ref, m_ref, l_ref, acc_ref):
    rows = q_ref.shape[0]
    q = q_ref[...] * jnp.asarray(HEAD**-0.5, BF16)
    qaug = qaug_ref[...]
    qaug2 = jnp.concatenate([qaug, qaug], axis=0)
    qa = jnp.concatenate([split_pair(q), qaug2], axis=1)

    def scores_of(at):
        keys = jnp.concatenate([k_ref[at * block : (at + 1) * block], kaug_ref[at * block : (at + 1) * block]], axis=1)
        return nt(qa, keys)

    scores = scores_of(0)
    if causal:
        row = lax.broadcasted_iota(jnp.int32, (rows, block), 0)
        col = lax.broadcasted_iota(jnp.int32, (rows, block), 1)
        keep = col <= row
        scores = jnp.where(jnp.concatenate([keep, keep], axis=0), scores, FAR)
    top = jnp.max(scores, axis=1, keepdims=True)
    weights = jnp.exp(scores - top)
    m_ref[...] = top
    l_ref[...] = jnp.sum(weights, axis=1, keepdims=True)
    acc_ref[...] = nn(weights.astype(BF16), v_ref[0:block])

    def more(at):
        scores = scores_of(at)
        old = m_ref[...]
        top = jnp.maximum(old, jnp.max(scores, axis=1, keepdims=True))
        scale = jnp.exp(old - top)
        weights = jnp.exp(scores - top)
        m_ref[...] = top
        l_ref[...] = l_ref[...] * scale + jnp.sum(weights, axis=1, keepdims=True)
        acc_ref[...] = acc_ref[...] * scale + nn(weights.astype(BF16), v_ref[at * block : (at + 1) * block])

    for at in range(1, blocks):
        if causal:
            pl.when(s_ref[0] >= at)(functools.partial(more, at))
        else:
            more(at)
    total = l_ref[...]
    out_ref[...] = join_pair(acc_ref[...] / total).astype(BF16)
    lse = m_ref[...] + jnp.log(total)
    aug_ref[0] = spread_terms(three_terms(-lse), qaug2)


def attend(place, queries, qaug, keys, values, kaug, block, causal):
    rows, width = queries.shape
    total = keys.shape[0]
    pairs = width // PAIR
    kernel = functools.partial(attend_kernel, total // block, block, causal)
    return pl.pallas_call(
        kernel,
        grid_spec=pltpu.PrefetchScalarGridSpec(
            num_scalar_prefetch=1,
            grid=(pairs,),
            in_specs=[
                pl.BlockSpec((rows, PAIR), lambda h, s: (0, h)),
                pl.BlockSpec((rows, LANES), lambda h, s: (0, 0)),
                pl.BlockSpec((total, PAIR), lambda h, s: (0, h)),
                pl.BlockSpec((total, PAIR), lambda h, s: (0, h)),
                pl.BlockSpec((total, LANES), lambda h, s: (0, 0)),
            ],
            out_specs=[
                pl.BlockSpec((rows, PAIR), lambda h, s: (0, h)),
                pl.BlockSpec((1, 2 * rows, LANES), lambda h, s: (h, 0, 0)),
            ],
            scratch_shapes=[
                pltpu.VMEM((2 * rows, 1), F32),
                pltpu.VMEM((2 * rows, 1), F32),
                pltpu.VMEM((2 * rows, PAIR), F32),
            ],
        ),
        out_shape=[
            jax.ShapeDtypeStruct((rows, width), BF16),
            jax.ShapeDtypeStruct((pairs, 2 * rows, LANES), BF16),
        ],
        compiler_params=pltpu.CompilerParams(vmem_limit_bytes=VMEM),
        cost_estimate=pl.CostEstimate(flops=4 * rows * total * width, bytes_accessed=4 * total * width, transcendentals=rows * total * width // HEAD),
    )(place, queries, qaug, keys, values, kaug)


def attend_back_kernel(blocks, block, causal, s_ref, q_ref, aug_ref, k_ref, v_ref, kaug_ref, do_ref, o_ref, dq_ref, dk_ref, dv_ref, acc_ref):
    rows = q_ref.shape[0]
    q = split_pair(q_ref[...] * jnp.asarray(HEAD**-0.5, BF16))
    grads = do_ref[...]
    dot_rows = grads.astype(F32) * o_ref[...].astype(F32)
    low = lane_of(rows) < HEAD
    delta = jnp.concatenate(
        [
            jnp.sum(jnp.where(low, dot_rows, 0.0), axis=1, keepdims=True),
            jnp.sum(jnp.where(low, 0.0, dot_rows), axis=1, keepdims=True),
        ],
        axis=0,
    )
    grads = split_pair(grads)
    qa = jnp.concatenate([q, aug_ref[0]], axis=1)
    ga = jnp.concatenate([grads, spread_terms(three_terms(-delta), jnp.zeros((2 * rows, LANES), BF16))], axis=1)

    def one(at, first):
        span = slice(at * block, (at + 1) * block)
        kaug = kaug_ref[span]
        keys = k_ref[span]
        scores = nt(jnp.concatenate([keys, kaug], axis=1), qa)
        if causal and first:
            row = lax.broadcasted_iota(jnp.int32, (block, rows), 0)
            col = lax.broadcasted_iota(jnp.int32, (block, rows), 1)
            keep = row <= col
            scores = jnp.where(jnp.concatenate([keep, keep], axis=1), scores, FAR)
        chances = jnp.exp(scores)
        slopes = nt(jnp.concatenate([v_ref[span], kaug], axis=1), ga)
        low_slopes = (chances * slopes).astype(BF16)
        dv_ref[span] = nn(chances.astype(BF16), grads).astype(BF16)
        dk_ref[span] = nn(low_slopes, q).astype(BF16)
        part = tn(low_slopes, keys)
        if first:
            acc_ref[...] = part
        else:
            acc_ref[...] += part

    def none(at):
        span = slice(at * block, (at + 1) * block)
        dv_ref[span] = jnp.zeros((block, PAIR), BF16)
        dk_ref[span] = jnp.zeros((block, PAIR), BF16)

    one(0, True)
    for at in range(1, blocks):
        if causal:
            pl.when(s_ref[0] >= at)(functools.partial(one, at, False))
            pl.when(s_ref[0] < at)(functools.partial(none, at))
        else:
            one(at, False)
    dq_ref[...] = (join_pair(acc_ref[...]) * HEAD**-0.5).astype(BF16)


def attend_back(place, queries, aug, keys, values, kaug, grads, outs, block, causal):
    rows, width = queries.shape
    total = keys.shape[0]
    pairs = width // PAIR
    kernel = functools.partial(attend_back_kernel, total // block, block, causal)
    by_head = pl.BlockSpec((rows, PAIR), lambda h, s: (0, h))
    keys_by_head = pl.BlockSpec((total, PAIR), lambda h, s: (0, h))
    return pl.pallas_call(
        kernel,
        grid_spec=pltpu.PrefetchScalarGridSpec(
            num_scalar_prefetch=1,
            grid=(pairs,),
            in_specs=[
                by_head,
                pl.BlockSpec((1, 2 * rows, LANES), lambda h, s: (h, 0, 0)),
                keys_by_head,
                keys_by_head,
                pl.BlockSpec((total, LANES), lambda h, s: (0, 0)),
                by_head,
                by_head,
            ],
            out_specs=[by_head, keys_by_head, keys_by_head],
            scratch_shapes=[pltpu.VMEM((2 * rows, PAIR), F32)],
        ),
        out_shape=[
            jax.ShapeDtypeStruct((rows, width), BF16),
            jax.ShapeDtypeStruct((total, width), BF16),
            jax.ShapeDtypeStruct((total, width), BF16),
        ],
        compiler_params=pltpu.CompilerParams(vmem_limit_bytes=VMEM),
        cost_estimate=pl.CostEstimate(flops=10 * rows * total * width, bytes_accessed=8 * total * width, transcendentals=rows * total * width // HEAD),
    )(place, queries, aug, keys, values, kaug, grads, outs)


def project(rows_low, weight, down, up):
    hidden = nt(rows_low, down).astype(BF16)
    return nn(rows_low, weight) + nn(hidden, up), hidden


def project_back(grad_low, rows_low, hidden, weight, down, up):
    grad_hidden = nt(grad_low, up).astype(BF16)
    grad_rows = nt(grad_low, weight) + nn(grad_hidden, down)
    return grad_rows, tn(grad_hidden, rows_low), tn(hidden, grad_low)


def normalize(values):
    centered = values - jnp.mean(values, -1, keepdims=True)
    inv_std = lax.rsqrt(jnp.mean(centered * centered, -1, keepdims=True) + NORM_EPS)
    return centered * inv_std, inv_std


def normalize_back(grads, normed, inv_std):
    return inv_std * (grads - jnp.mean(grads, -1, keepdims=True) - normed * jnp.mean(grads * normed, -1, keepdims=True))


def gelu_value(values):
    return 0.5 * values * (1.0 + lax.erf(values * 0.7071067811865476))


def gelu_slope(values):
    return 0.5 * (1.0 + lax.erf(values * 0.7071067811865476)) + values * jnp.exp(-0.5 * values * values) * 0.3989422804014327


def make_shards(mesh):
    chips, cores, span = mesh.shape["chip"], mesh.shape["core"], mesh.shape["sp"]
    plane = ("chip", "core")

    def up(values):
        return lax.ppermute(values, "sp", [(i, i + 1) for i in range(span - 1)])

    def down(values):
        return lax.ppermute(values, "sp", [(i + 1, i) for i in range(span - 1)])

    def turn(values, by):
        return lax.ppermute(values, "sp", [(i, (i + by) % span) for i in range(span)])

    def gather_plane(values):
        return lax.all_gather(values, plane, axis=0, tiled=True)

    def shards(
        inputs,
        segments,
        enc_states,
        adapter_pick,
        qkv_weights,
        out_weights,
        mlp_in,
        mlp_out,
        proj_down,
        proj_up,
        fc1_down,
        fc1_up,
        fc2_down,
        fc2_up,
        cotangent,
    ):
        x_low = inputs[0]
        mem_own = enc_states[0]
        seg_own = segments[0]
        pick = adapter_pick[0]
        place = lax.axis_index("sp").astype(jnp.int32)[None]
        tokens, width = x_low.shape
        rank = proj_down.shape[3]

        blocks, seg_blocks, mems = [x_low], [seg_own], [mem_own]
        for _ in range(1, span):
            blocks.append(up(blocks[-1]))
            seg_blocks.append(up(seg_blocks[-1]))
        for by in range(1, span):
            mems.append(turn(mem_own, by))
        x_all = jnp.concatenate(blocks, axis=0)
        seg_all = jnp.concatenate(seg_blocks, axis=0)
        mem_all = jnp.concatenate(mems, axis=0)

        lane = jnp.arange(LANES, dtype=jnp.int32)[None, :]
        in_seg = (lane >= SEG_LANE) & (lane < SEG_LANE + SEG_KINDS)
        q_aug = jnp.where(in_seg & (lane - SEG_LANE == seg_own[:, None]), 1.0, 0.0).astype(BF16)
        k_aug = jnp.where(lane < SEG_LANE, 1.0, jnp.where(in_seg & (lane - SEG_LANE != seg_all[:, None]), FAR, 0.0)).astype(BF16)
        q_aug_free = jnp.zeros((tokens, LANES), BF16)
        k_aug_free = jnp.broadcast_to(jnp.where(lane < SEG_LANE, 1.0, 0.0), (mem_all.shape[0], LANES)).astype(BF16)

        a_proj = lax.dynamic_index_in_dim(proj_down[0], pick, 1, False)
        b_proj = lax.dynamic_index_in_dim(proj_up[0], pick, 1, False)
        a_fc1 = lax.dynamic_index_in_dim(fc1_down[0], pick, 0, False)
        b_fc1 = lax.dynamic_index_in_dim(fc1_up[0], pick, 0, False)
        a_fc2 = lax.dynamic_index_in_dim(fc2_down[0], pick, 0, False)
        b_fc2 = lax.dynamic_index_in_dim(fc2_up[0], pick, 0, False)

        w_self = [gather_plane(qkv_weights[0, p]) for p in range(6)]
        w_out = [gather_plane(out_weights[0, p]) for p in range(2)]
        w_up = gather_plane(mlp_in[0])
        w_down = gather_plane(mlp_out[0])

        q, r_q = project(x_low, w_self[0], a_proj[0], b_proj[0])
        k, r_k = project(x_all, w_self[1], a_proj[1], b_proj[1])
        v, r_v = project(x_all, w_self[2], a_proj[2], b_proj[2])
        q, k, v = q.astype(BF16), k.astype(BF16), v.astype(BF16)
        o, aug = attend(place, q, q_aug, k, v, k_aug, tokens, True)
        branch, r_so = project(o, w_out[0], a_proj[6], b_proj[6])
        h1, std1 = normalize(x_low.astype(F32) + branch)
        h1_low = h1.astype(BF16)
        kc, r_kc = project(mem_all, w_self[4], a_proj[4], b_proj[4])
        vc, r_vc = project(mem_all, w_self[5], a_proj[5], b_proj[5])
        kc, vc = kc.astype(BF16), vc.astype(BF16)
        qc, r_cq = project(h1_low, w_self[3], a_proj[3], b_proj[3])
        qc = qc.astype(BF16)
        mem_block = min(512, mem_all.shape[0])
        oc, aug_c = attend(place, qc, q_aug_free, kc, vc, k_aug_free, mem_block, False)
        branch, r_co = project(oc, w_out[1], a_proj[7], b_proj[7])
        h2, std2 = normalize(h1 + branch)
        h2_low = h2.astype(BF16)
        pre, r_fc1 = project(h2_low, w_up, a_fc1, b_fc1)
        g = gelu_value(pre).astype(BF16)
        branch, r_fc2 = project(g, w_down, a_fc2, b_fc2)
        y, std3 = normalize(h2 + branch)

        d3 = normalize_back(cotangent[0].astype(F32), y, std3)
        dg, da_fc2, db_fc2 = project_back(d3.astype(BF16), g, r_fc2, w_down, a_fc2, b_fc2)
        dpre = (dg * gelu_slope(pre)).astype(BF16)
        dh2, da_fc1, db_fc1 = project_back(dpre, h2_low, r_fc1, w_up, a_fc1, b_fc1)
        d2 = normalize_back(d3 + dh2, h2, std2)
        doc, da_co, db_co = project_back(d2.astype(BF16), oc, r_co, w_out[1], a_proj[7], b_proj[7])
        dqc, dkc, dvc = attend_back(place, qc, aug_c, kc, vc, k_aug_free, doc.astype(BF16), oc, mem_block, False)
        dh1, da_cq, db_cq = project_back(dqc, h1_low, r_cq, w_self[3], a_proj[3], b_proj[3])
        dmem_k, da_kc, db_kc = project_back(dkc, mem_all, r_kc, w_self[4], a_proj[4], b_proj[4])
        dmem_v, da_vc, db_vc = project_back(dvc, mem_all, r_vc, w_self[5], a_proj[5], b_proj[5])
        dmem_parts = (dmem_k + dmem_v).reshape(span, -1, width)
        dmem = dmem_parts[0]
        for by in range(1, span):
            dmem = dmem + turn(dmem_parts[by].astype(BF16), -by).astype(F32)
        d1 = normalize_back(d2 + dh1, h1, std1)
        do, da_so, db_so = project_back(d1.astype(BF16), o, r_so, w_out[0], a_proj[6], b_proj[6])
        dq, dk, dv = attend_back(place, q, aug, k, v, k_aug, do.astype(BF16), o, tokens, True)
        dx_q, da_q, db_q = project_back(dq, x_low, r_q, w_self[0], a_proj[0], b_proj[0])
        dx_k, da_k, db_k = project_back(dk, x_all, r_k, w_self[1], a_proj[1], b_proj[1])
        dx_v, da_v, db_v = project_back(dv, x_all, r_v, w_self[2], a_proj[2], b_proj[2])
        dx_parts = (dx_k + dx_v).reshape(span, tokens, width)
        dx = dx_parts[span - 1]
        for at in reversed(range(span - 1)):
            dx = dx_parts[at] + down(dx.astype(BF16)).astype(F32)
        dx = d1 + dx_q + dx

        def everywhere(parts):
            sizes = [p.size // width for p in parts]
            flat = jnp.concatenate([p.reshape(-1, width) for p in parts], axis=0)
            flat = lax.psum(flat.astype(BF16), "sp")
            return lax.all_gather(flat, plane, axis=0, tiled=False), sizes

        picks = lax.all_gather(adapter_pick, plane, axis=0, tiled=True)
        mlp_parts = (da_fc1, db_fc1, da_fc2, db_fc2)
        proj_parts = [da_q, da_k, da_v, da_cq, da_kc, da_vc, da_so, da_co, db_q, db_k, db_v, db_cq, db_kc, db_vc, db_so, db_co]
        flat, sizes = everywhere(list(mlp_parts) + proj_parts)
        hot = (picks[None, :] == jnp.arange(proj_down.shape[2], dtype=jnp.int32)[:, None]).astype(F32)
        wide = jnp.sum(hot[:, :, None, None] * flat.astype(F32)[None], axis=1)
        outs, at = [], 0
        for size, like in zip(sizes[:4], (fc1_down, fc1_up, fc2_down, fc2_up)):
            outs.append(wide[:, at : at + size].reshape(like.shape))
            at += size
        kinds = 8 * rank
        total_down = wide[:, at : at + kinds].reshape(-1, 8, rank, width).transpose(1, 0, 2, 3)[None]
        total_up = wide[:, at + kinds : at + 2 * kinds].reshape(-1, 8, rank, width).transpose(1, 0, 2, 3)[None]
        return (y.astype(BF16)[None], dx[None], dmem[None], total_down, total_up, *outs)

    return shards


def solution(mesh):
    count = mesh.shape["fsdp"]
    fine = Mesh(mesh.devices.reshape(count // 2, 2, mesh.shape["sp"]), ("chip", "core", "sp"))
    fsdp = ("chip", "core")
    row = P(fsdp, "sp", None)
    return jax.shard_map(
        make_shards(fine),
        mesh=fine,
        in_specs=(
            row,
            P(fsdp, "sp"),
            row,
            P(fsdp),
            P(None, None, fsdp, None),
            P(None, None, fsdp, None),
            P(None, fsdp, None),
            P(None, fsdp, None),
            P(),
            P(),
            P(),
            P(),
            P(),
            P(),
            row,
        ),
        out_specs=(row, row, row, P(), P(), P(), P(), P(), P()),
        check_vma=False,
    )
```

```python
import functools

import jax
import jax.numpy as jnp
from jax import lax
from jax.experimental import pallas as pl
from jax.experimental.pallas import tpu as pltpu
from jax.sharding import Mesh
from jax.sharding import PartitionSpec as P

HEAD = 64
PAIR = 2 * HEAD
RANK = 16
AUG = 16
TERMS = 3
SEG_KINDS = 5
COLS = 256
NORM_EPS = 1e-05
FAR = -1e30
SCALE = HEAD**-0.5
F32 = jnp.float32
BF16 = jnp.bfloat16
ANY = pl.BlockSpec(memory_space=pltpu.HBM)
WHOLE = pl.BlockSpec(memory_space=pltpu.VMEM)


def dot(left, right, left_dim, right_dim):
    return lax.dot_general(left, right, (((left_dim,), (right_dim,)), ((), ())), preferred_element_type=F32)


def nn(left, right):
    return dot(left, right, 1, 0)


def nt(left, right):
    return dot(left, right, 1, 1)


def tn(left, right):
    return dot(left, right, 0, 0)


def params(mib):
    return pltpu.CompilerParams(vmem_limit_bytes=mib * 1024 * 1024)


def cost(flops, moved, exps=0):
    return pl.CostEstimate(flops=int(flops), bytes_accessed=int(moved), transcendentals=int(exps))


def each(total, size, body, unroll=4):
    def step(at, carry):
        body(pl.ds(pl.multiple_of(at * size, size), size))
        return carry

    lax.fori_loop(0, total // size, step, 0, unroll=min(unroll, total // size))


def fetch(refs, layout, own, rows, part, target, sems):
    copies = []
    for ref, entries in zip(refs, layout):
        for source, flip, who, first, count in entries:
            low, high = max(first, part * rows), min(first + count, (part + 1) * rows)
            if low < high:
                shard = own ^ who if flip else who
                copies.append(
                    pltpu.make_async_copy(
                        ref.at[pl.ds(source + low - first, high - low)],
                        target.at[pl.ds(pl.multiple_of(shard * rows + (low - part * rows), 16), high - low)],
                        sems.at[len(copies)],
                    )
                )
    return copies


def start_all(copies):
    for copy in copies:
        copy.start()


def wait_all(copies):
    for copy in copies:
        copy.wait()


def low_half(shape, axis):
    return lax.broadcasted_iota(jnp.int32, shape, axis) < HEAD


def split_pair(rows):
    low = low_half(rows.shape, 1)
    zero = jnp.zeros_like(rows)
    return jnp.concatenate([jnp.where(low, rows, zero), jnp.where(low, zero, rows)], axis=0)


def split_pair_t(cols):
    low = low_half(cols.shape, 0)
    zero = jnp.zeros_like(cols)
    return jnp.concatenate([jnp.where(low, cols, zero), jnp.where(low, zero, cols)], axis=1)


def join_pair_t(cols):
    half = cols.shape[1] // 2
    return jnp.where(low_half((PAIR, half), 0), cols[:, :half], cols[:, half:])


def turned(rows):
    return rows.astype(F32).T


def term_rows(row, rest):
    high = row.astype(BF16).astype(F32)
    mid = (row - high).astype(BF16).astype(F32)
    low = row - high - mid
    at = lax.broadcasted_iota(jnp.int32, rest.shape, 0)
    return jnp.where(at == 0, high, jnp.where(at == 1, mid, jnp.where(at == 2, low, rest))).astype(BF16)


def causal_scores(scores):
    keys, columns = scores.shape
    row = lax.broadcasted_iota(jnp.int32, (keys, columns // 2), 0)
    col = lax.broadcasted_iota(jnp.int32, (keys, columns // 2), 1)
    keep = row <= col
    return jnp.where(jnp.concatenate([keep, keep], axis=1), scores, FAR)


def out_slopes(grads, outs):
    gt = turned(grads)
    products = gt * turned(outs)
    delta = jnp.concatenate([jnp.sum(products[:HEAD], axis=0, keepdims=True), jnp.sum(products[HEAD:], axis=0, keepdims=True)], axis=1)
    rest = jnp.zeros((AUG, delta.shape[1]), F32)
    return jnp.concatenate([split_pair_t(gt.astype(BF16)), term_rows(-delta, rest)], axis=0)


def block_back(keys, values, kaug, qa, ga, q, grads, diagonal):
    scores = nn(jnp.concatenate([keys, kaug], axis=1), qa)
    if diagonal:
        scores = causal_scores(scores)
    chances = jnp.exp(scores)
    slopes = nn(jnp.concatenate([values, kaug], axis=1), ga)
    low_slopes = (chances * slopes).astype(BF16)
    grad_values = nn(chances.astype(BF16), grads).astype(BF16)
    grad_keys = nn(low_slopes, q).astype(BF16)
    grad_q = join_pair_t(nn(turned(keys).astype(BF16), low_slopes))
    return grad_q, grad_keys, grad_values


def slope_rows(ga_ref, do_ref, o_ref):
    for at in range(ga_ref.shape[0]):
        cols = slice(at * PAIR, (at + 1) * PAIR)
        ga_ref[at] = out_slopes(do_ref[:, cols], o_ref[:, cols])


def adapter_spec(first, count, width):
    return pl.BlockSpec((1, count, 1, RANK, width), lambda *at: (0, first // count, at[-1][2], 0, 0))


def mlp_adapter_spec(width):
    return pl.BlockSpec((1, 1, RANK, width), lambda *at: (0, at[-1][2], 0, 0))


def low_rank(rows, table):
    return nt(rows, table).astype(BF16)


class Gathered:
    def __init__(self, arrays, layout, rows):
        self.arrays, self.layout, self.rows = arrays, layout, rows
        self.count = sum(len(entries) for entries in layout)

    def bring(self, refs, own, part, target, sems):
        return fetch(refs, self.layout, own, self.rows, part, target, sems)

    def specs(self):
        return [ANY] * len(self.arrays)

    def sems(self, parts):
        return pltpu.SemaphoreType.DMA((parts, self.count))


def project_into(out_ref, rows, weight, hidden, up):
    def body(cols):
        out_ref[:, cols] = (nn(rows, weight[:, cols]) + nn(hidden, up(cols))).astype(out_ref.dtype)

    each(out_ref.shape[1], COLS, body)


class Gathered:
    def __init__(self, arrays, layout, rows):
        self.arrays, self.layout, self.rows = arrays, layout, rows
        self.count = sum(len(entries) for entries in layout)

    def bring(self, refs, own, part, target, sems):
        return fetch(refs, self.layout, own, self.rows, part, target, sems)

    def specs(self):
        return [ANY] * len(self.arrays)

    def sems(self, parts):
        return pltpu.SemaphoreType.DMA((parts, self.count))


def project_into(out_ref, rows, weight, hidden, up):
    def body(cols):
        out_ref[:, cols] = (nn(rows, weight[:, cols]) + nn(hidden, up(cols))).astype(out_ref.dtype)

    each(out_ref.shape[1], COLS, body)


class Step:
    def __init__(self, name, w, parts, at, first, last, causal):
        self.name, self.w, self.parts, self.at, self.first, self.last, self.causal = name, w, parts, at, first, last, causal
        self.diagonal = causal and at == 0

    def active(self, sc_ref):
        return sc_ref[0] >= self.at if self.causal and self.at else None

    def when(self, sc_ref, condition=None):
        conditions = [c for c in (self.active(sc_ref), condition) if c is not None]
        if not conditions:
            return lambda body: body()
        return pl.when(conditions[0] if len(conditions) == 1 else conditions[0] & conditions[1])


def head_cols():
    return pl.ds(pl.multiple_of(pl.program_id(0) * PAIR, PAIR), PAIR)


def attend_step_kernel(step, count, sc_ref, *refs):
    refs = list(refs)
    make_q = step.causal and step.first

    def take(number):
        return [refs.pop(0) for _ in range(number)]

    xs = take(count)
    a_ref, b_ref, kaug_ref = take(3)
    q_ref = take(1)[0] if step.first and not make_q else None
    seg_ref = take(1)[0] if step.first else None
    qa_in, acc_in, m_in = (None, None, None) if step.first else take(3)
    pieces = take(len(step.w.arrays))
    q_out = take(1)[0] if make_q else None
    k_out, v_out, r_out = take(3)
    o_out, qa_out = None, None
    if step.first:
        qa_out = take(1)[0]
    if step.last:
        o_out, qa_out, w_ref, k_all, v_all, sems, acc_ref, m_ref = take(8)
    else:
        acc_ref, m_ref, w_ref, k_all, v_all, sems = take(6)
        acc_ref, m_ref = acc_ref.at[0], m_ref.at[0]
    q_all = take(1)[0] if make_q else None
    parts = step.parts
    kinds = len(parts)

    @step.when(sc_ref, pl.program_id(0) == 0)
    def _():
        copies = [step.w.bring(pieces, sc_ref[1], part, w_ref.at[at], sems.at[at]) for at, part in enumerate(parts)]
        for part in copies:
            start_all(part)
        low = 0
        tables = a_ref[...].reshape(-1, a_ref.shape[-1])
        for x_ref in xs:
            x = x_ref[...]
            span = pl.ds(low, x.shape[0])
            low += x.shape[0]
            hidden = low_rank(x, tables)
            r_out[span, :] = hidden
            outs = [k_all, v_all]
            if make_q:
                outs.insert(0, q_all)
            for at, out in enumerate(outs):
                slot = at + a_ref.shape[1] - len(outs)
                own = hidden[:, slot * RANK : (slot + 1) * RANK]
                if x_ref is xs[0]:
                    wait_all(copies[at])

                def body(cols, at=at, slot=slot, own=own, out=out):
                    out[span, cols] = (nn(x, w_ref[at, :, cols]) + nn(own, b_ref[0, slot, 0, :, cols])).astype(BF16)

                each(out.shape[1], COLS, body)

    @step.when(sc_ref)
    def _():
        cols = head_cols()
        keys, values = k_all[:, cols], v_all[:, cols]
        k_out[...] = keys
        v_out[...] = values
        if step.first:
            q = q_all[:, cols] if make_q else q_ref[...]
            if make_q:
                q_out[...] = q
            seg = seg_ref[...]
            qt = split_pair_t((turned(q) * SCALE).astype(BF16))
            qa = jnp.concatenate([qt, jnp.concatenate([seg, seg], axis=1).astype(BF16)], axis=0)
            if not step.last:
                qa_out[0] = qa
        else:
            qa = qa_in[0]
        scores = nn(jnp.concatenate([keys, kaug_ref[...]], axis=1), qa)
        if step.diagonal:
            scores = causal_scores(scores)
        top = jnp.max(scores, axis=0, keepdims=True)
        vt = jnp.concatenate([turned(values).astype(BF16), jnp.ones((16, keys.shape[0]), BF16)], axis=0)
        if step.first:
            acc_ref[...] = nn(vt, jnp.exp(scores - top).astype(BF16))
        else:
            old = m_in[0, 0:1]
            top = jnp.maximum(old, top)
            acc_ref[...] = acc_in[0] * jnp.exp(old - top) + nn(vt, jnp.exp(scores - top).astype(BF16))
        m_ref[...] = jnp.broadcast_to(top, m_ref.shape)

    if step.active(sc_ref) is not None:

        @pl.when(jnp.logical_not(step.active(sc_ref)))
        def _():
            acc_ref[...] = acc_in[0]
            m_ref[...] = m_in[0]

    if step.last:
        total = acc_ref[PAIR : PAIR + 1]
        o_out[...] = join_pair_t(acc_ref[:PAIR] / total).T.astype(BF16)
        lse = m_ref[0:1] + jnp.log(total)
        qa = qa_in[0]
        qa_out[0] = jnp.concatenate([qa[:PAIR], term_rows(-lse, qa[PAIR:].astype(F32))], axis=0)


def attend_step(step, scalars, xs, tokens, block_rows, proj_down, proj_up, kaug, q, seg, state):
    width = xs[0].shape[1]
    pairs = width // PAIR
    keys = block_rows * len(xs)
    make_q = step.causal and step.first
    kinds = len(step.parts)
    slots = 3 if step.causal else 2
    by_head = pl.BlockSpec((tokens, PAIR), lambda h, s: (0, h))
    keys_by_head = pl.BlockSpec((keys, PAIR), lambda h, s: (0, h))
    extended = pl.BlockSpec((1, PAIR + AUG, 2 * tokens), lambda h, s: (h, 0, 0))
    m_spec = pl.BlockSpec((1, 8, 2 * tokens), lambda h, s: (h, 0, 0))
    adapters = adapter_spec(0 if step.causal else 4, slots, width)
    q_shape = jax.ShapeDtypeStruct((tokens, width), BF16)
    kv_shape = jax.ShapeDtypeStruct((keys, width), BF16)
    qa_shape = jax.ShapeDtypeStruct((pairs, PAIR + AUG, 2 * tokens), BF16)
    state_shapes = [jax.ShapeDtypeStruct((pairs, PAIR + 16, 2 * tokens), F32), jax.ShapeDtypeStruct((pairs, 8, 2 * tokens), F32)]
    in_specs = [pl.BlockSpec((block_rows, width), lambda h, s: (0, 0))] * len(xs)
    in_specs += [adapters, adapters, pl.BlockSpec((keys, AUG), lambda h, s: (0, 0))]
    args = [*xs, proj_down, proj_up, kaug]
    if step.first and not make_q:
        in_specs.append(by_head)
        args.append(q)
    if step.first:
        in_specs.append(pl.BlockSpec((AUG, tokens), lambda h, s: (0, 0)))
        args.append(seg)
    else:
        in_specs += [extended, extended, m_spec]
        args += state
    out_specs = [keys_by_head, keys_by_head, pl.BlockSpec((keys, slots * RANK), lambda h, s: (0, 0))]
    out_shape = [kv_shape, kv_shape, jax.ShapeDtypeStruct((keys, slots * RANK), BF16)]
    if make_q:
        out_specs.insert(0, by_head)
        out_shape.insert(0, q_shape)
    scratch = [pltpu.VMEM((kinds, width, width), BF16), pltpu.VMEM((keys, width), BF16), pltpu.VMEM((keys, width), BF16), step.w.sems(kinds)]
    if step.first:
        out_specs.append(extended)
        out_shape.append(qa_shape)
    if step.last:
        out_specs += [by_head, extended]
        out_shape += [q_shape, qa_shape]
        scratch += [pltpu.VMEM((PAIR + 16, 2 * tokens), F32), pltpu.VMEM((8, 2 * tokens), F32)]
    else:
        out_specs += [extended, m_spec]
        out_shape += state_shapes
    if make_q:
        scratch.append(pltpu.VMEM((tokens, width), BF16))
    call = pl.pallas_call(
        functools.partial(attend_step_kernel, step, len(xs)),
        grid_spec=pltpu.PrefetchScalarGridSpec(
            num_scalar_prefetch=1, grid=(pairs,), in_specs=in_specs + step.w.specs(), out_specs=out_specs, scratch_shapes=scratch
        ),
        out_shape=out_shape,
        name=step.name,
        compiler_params=params(60),
        cost_estimate=cost(4 * tokens * keys * width + 2 * kinds * keys * width * width, 20 * tokens * width, tokens * keys * width // HEAD),
    )
    return list(call(scalars, *args, *step.w.arrays))


def back_step_kernel(step, count, sc_ref, *refs):
    refs = list(refs)

    def take(number):
        return [refs.pop(0) for _ in range(number)]

    qa_ref, ga_ref, q_ref, do_ref, k_ref, v_ref, kaug_ref, r_ref, a_ref, b_ref = take(10)
    xs = take(count)
    dqt_in, sums_in = (None, None) if step.first else take(2)
    query = step.causal and step.last
    d1_ref = take(1)[0] if query else None
    pieces = take(len(step.w.arrays))
    dq_all = None
    if query:
        base_ref, grads_ref, w_ref, dk_all, dv_all, sems, dq_all = refs
    elif step.last:
        own_ref, part_ref, dq_ref, grads_ref, w_ref, dk_all, dv_all, sems = refs
    else:
        part_ref, dqt_ref, sums_ref, w_ref, dk_all, dv_all, sems = refs
    h = pl.program_id(0)
    final = h == pl.num_programs(0) - 1
    width = a_ref.shape[-1]
    parts = step.parts
    slots = a_ref.shape[1]

    def weights():
        return [step.w.bring(pieces, sc_ref[1], part, w_ref.at[at], sems.at[at]) for at, part in enumerate(parts)]

    @step.when(sc_ref, h == 0)
    def _():
        for part in weights():
            start_all(part)

    @step.when(sc_ref)
    def _():
        q = split_pair(q_ref[...] * jnp.asarray(SCALE, BF16))
        grad_q, grad_keys, grad_values = block_back(
            k_ref[...], v_ref[...], kaug_ref[...], qa_ref[0], ga_ref[0], q, split_pair(do_ref[...]), step.diagonal
        )
        cols = head_cols()
        dk_all[:, cols] = grad_keys
        dv_all[:, cols] = grad_values
        if not step.first:
            grad_q = grad_q + dqt_in[0]
        if query:
            dq_all[:, cols] = (grad_q * SCALE).T.astype(BF16)
        elif step.last:
            dq_ref[...] = (grad_q * SCALE).T.astype(BF16)
        else:
            dqt_ref[0] = grad_q

    if step.active(sc_ref) is not None:

        @pl.when(jnp.logical_not(step.active(sc_ref)))
        def _():
            dqt_ref[0] = jnp.zeros_like(dqt_ref[0]) if step.first else dqt_in[0]

            @pl.when(final)
            def _():
                part_ref[...] = jnp.zeros_like(part_ref)
                sums_ref[...] = jnp.zeros_like(sums_ref) if step.first else sums_in[...]

    @step.when(sc_ref, final)
    def _():
        grads = [dq_all, dk_all, dv_all] if query else [dk_all, dv_all]
        shift = slots - len(grads)
        drs, dbs = [], []
        hidden = r_ref[...]
        for at, grad_ref in enumerate(grads):
            slot = at + shift
            grad = grad_ref[...]
            drs.append(low_rank(grad, b_ref[0, slot, 0]))
            dbs.append(tn(hidden[:, slot * RANK : (slot + 1) * RANK], grad))
        dr = jnp.concatenate(drs, axis=1)
        low, da = 0, None
        for x_ref in xs:
            part = tn(dr[low : low + x_ref.shape[0]], x_ref[...])
            da = part if da is None else da + part
            low += x_ref.shape[0]
        olds = [None] * 4 if step.first else [sums_in[at * RANK : (at + 1) * RANK] for at in range(4)]
        if query:
            olds = [None, *olds[:2], None, *olds[2:]]
        total = [da[at * RANK : (at + 1) * RANK] for at in range(len(grads))] + dbs
        target = grads_ref if step.last else sums_ref
        for at, (new, old) in enumerate(zip(total, olds)):
            target[at * RANK : (at + 1) * RANK] = (new if old is None else new + old).astype(target.dtype)
        for part in weights():
            wait_all(part)
        rows = dk_all.shape[0]
        own = rows // count if step.last and not query else 0

        def body(cols):
            table = a_ref[0, shift:, 0, :, cols].reshape(len(grads) * RANK, COLS)
            value = nn(dr, table)
            for at, grad_ref in enumerate(grads):
                value = value + nt(grad_ref[...], w_ref[at, cols, :])
            if query:
                base_ref[:, cols] = value + d1_ref[:, cols]
            elif step.last:
                own_ref[:, cols] = value[:own]
                part_ref[:, cols] = value[own:].astype(BF16)
            else:
                part_ref[:, cols] = value.astype(BF16)

        each(width, COLS, body)


def back_step(step, scalars, qa, ga, q, do, k, v, kaug, r, xs, block_rows, proj_down, proj_up, state, d1):
    tokens, width = q.shape
    pairs = width // PAIR
    keys = k.shape[0]
    slots = 3 if step.causal else 2
    query = step.causal and step.last
    by_head = pl.BlockSpec((tokens, PAIR), lambda h, s: (0, h))
    keys_by_head = pl.BlockSpec((keys, PAIR), lambda h, s: (0, h))
    extended = pl.BlockSpec((1, PAIR + AUG, 2 * tokens), lambda h, s: (h, 0, 0))
    dqt_spec = pl.BlockSpec((1, PAIR, tokens), lambda h, s: (h, 0, 0))

    def whole(rows):
        return pl.BlockSpec((rows, width), lambda h, s: (0, 0))

    adapters = adapter_spec(0 if step.causal else 4, slots, width)
    in_specs = [
        extended,
        extended,
        by_head,
        by_head,
        keys_by_head,
        keys_by_head,
        pl.BlockSpec((keys, AUG), lambda h, s: (0, 0)),
        pl.BlockSpec((keys, slots * RANK), lambda h, s: (0, 0)),
        adapters,
        adapters,
        *[whole(block_rows)] * len(xs),
    ]
    args = [qa, ga, q, do, k, v, kaug, r, proj_down, proj_up, *xs]
    if not step.first:
        in_specs += [dqt_spec, whole(4 * RANK)]
        args += state
    scratch = [pltpu.VMEM((len(step.parts), width, width), BF16), pltpu.VMEM((keys, width), BF16), pltpu.VMEM((keys, width), BF16)]
    scratch.append(step.w.sems(len(step.parts)))
    if query:
        in_specs.append(whole(tokens))
        args.append(d1)
        scratch.append(pltpu.VMEM((tokens, width), BF16))
        out_specs = [whole(tokens), whole(6 * RANK)]
        out_shape = [jax.ShapeDtypeStruct((tokens, width), F32), jax.ShapeDtypeStruct((6 * RANK, width), BF16)]
    elif step.last:
        rest = keys - block_rows
        out_specs = [whole(block_rows), whole(rest), by_head, whole(4 * RANK)]
        out_shape = [
            jax.ShapeDtypeStruct((block_rows, width), F32),
            jax.ShapeDtypeStruct((rest, width), BF16),
            jax.ShapeDtypeStruct((tokens, width), BF16),
            jax.ShapeDtypeStruct((4 * RANK, width), BF16),
        ]
    else:
        out_specs = [whole(keys), dqt_spec, whole(4 * RANK)]
        out_shape = [
            jax.ShapeDtypeStruct((keys, width), BF16),
            jax.ShapeDtypeStruct((pairs, PAIR, tokens), F32),
            jax.ShapeDtypeStruct((4 * RANK, width), F32),
        ]
    return pl.pallas_call(
        functools.partial(back_step_kernel, step, len(xs)),
        grid_spec=pltpu.PrefetchScalarGridSpec(
            num_scalar_prefetch=1, grid=(pairs,), in_specs=in_specs + step.w.specs(), out_specs=out_specs, scratch_shapes=scratch
        ),
        out_shape=out_shape,
        name=step.name,
        compiler_params=params(60),
        cost_estimate=cost(10 * tokens * keys * width + 4 * keys * width * width, 24 * tokens * width, tokens * keys * width // HEAD),
    )(scalars, *args, *step.w.arrays)


ROWS = 64


def normalize_rows(u_ref, norm_ref, low_ref, std_ref):
    def body(rows):
        values = u_ref[rows, :]
        centered = values - jnp.mean(values, -1, keepdims=True)
        inv_std = lax.rsqrt(jnp.mean(centered * centered, -1, keepdims=True) + NORM_EPS)
        normed = centered * inv_std
        norm_ref[rows, :] = normed
        low_ref[rows, :] = normed.astype(BF16)
        std_ref[rows, :] = inv_std

    each(u_ref.shape[0], ROWS, body)


def normalize_back(grads, normed, inv_std):
    return inv_std * (grads - jnp.mean(grads, -1, keepdims=True) - normed * jnp.mean(grads * normed, -1, keepdims=True))


def mid_kernel(w, part, query, sc_ref, o_ref, x_ref, a_ref, b_ref, aq_ref, bq_ref, *refs):
    pieces, refs = refs[: len(w.arrays)], refs[len(w.arrays) :]
    if query:
        norm_ref, low_ref, std_ref, r_ref, q_ref, w_ref, u_ref, sems = refs
    else:
        norm_ref, low_ref, std_ref, r_ref, w_ref, u_ref, sems = refs
    width = x_ref.shape[1]
    first = w.bring(pieces, sc_ref[1], part, w_ref.at[0], sems.at[0])
    start_all(first)
    if query:
        second = w.bring(pieces, sc_ref[1], 2, w_ref.at[1], sems.at[1])
        start_all(second)
    o = o_ref[...]
    hidden = low_rank(o, a_ref[0, 0, 0])
    r_ref[:, :RANK] = hidden
    wait_all(first)

    def body(cols):
        u_ref[:, cols] = x_ref[:, cols].astype(F32) + nn(o, w_ref[0, :, cols]) + nn(hidden, b_ref[0, 0, 0, :, cols])

    each(width, COLS, body)
    normalize_rows(u_ref, norm_ref, low_ref, std_ref)
    if query:
        low = low_ref[...]
        hidden_q = low_rank(low, aq_ref[0, 0, 0])
        r_ref[:, RANK:] = hidden_q
        wait_all(second)
        project_into(q_ref, low, w_ref.at[1], hidden_q, lambda cols: bq_ref[0, 0, 0, :, cols])


def mid(name, scalars, outs, residual, part, proj, query, proj_down, proj_up, w):
    rows, width = outs.shape
    shapes = [
        jax.ShapeDtypeStruct((rows, width), F32),
        jax.ShapeDtypeStruct((rows, width), BF16),
        jax.ShapeDtypeStruct((rows, 1), F32),
        jax.ShapeDtypeStruct((rows, 2 * RANK if query else RANK), BF16),
    ]
    if query:
        shapes.append(jax.ShapeDtypeStruct((rows, width), BF16))
    spec, spec_q = adapter_spec(proj, 1, width), adapter_spec(3, 1, width)
    return pl.pallas_call(
        functools.partial(mid_kernel, w, part, query),
        grid_spec=pltpu.PrefetchScalarGridSpec(
            num_scalar_prefetch=1,
            grid=(1,),
            in_specs=[WHOLE, WHOLE, spec, spec, spec_q, spec_q, *w.specs()],
            out_specs=[WHOLE] * len(shapes),
            scratch_shapes=[pltpu.VMEM((2, width, width), BF16), pltpu.VMEM((rows, width), F32), w.sems(2)],
        ),
        out_shape=shapes,
        name=name,
        compiler_params=params(60),
        cost_estimate=cost(4 * rows * width * width, 12 * rows * width + 4 * width * width),
    )(scalars, outs, residual, proj_down, proj_up, proj_down, proj_up, *w.arrays)


def gelu_kernel(w, sc_ref, x_ref, a_ref, b_ref, *refs):
    pieces, (g_ref, slope_ref, r_ref, w_ref, sems) = refs[: len(w.arrays)], refs[len(w.arrays) :]
    copies = w.bring(pieces, sc_ref[1], 0, w_ref, sems.at[0])
    start_all(copies)
    x = x_ref[...]
    hidden = low_rank(x, a_ref[0, 0])
    r_ref[...] = hidden
    wait_all(copies)

    def body(cols):
        pre = nn(x, w_ref[:, cols]) + nn(hidden, b_ref[0, 0, :, cols])
        phi = 0.5 * (1.0 + lax.erf(pre * 0.7071067811865476))
        g_ref[:, cols] = (pre * phi).astype(BF16)
        slope_ref[:, cols] = (phi + pre * jnp.exp(-0.5 * pre * pre) * 0.3989422804014327).astype(BF16)

    each(g_ref.shape[1], COLS, body)


def gelu_up(scalars, x, down, up, w):
    rows, width = x.shape
    wide = up.shape[3]
    return pl.pallas_call(
        functools.partial(gelu_kernel, w),
        grid_spec=pltpu.PrefetchScalarGridSpec(
            num_scalar_prefetch=1,
            grid=(1,),
            in_specs=[WHOLE, mlp_adapter_spec(width), mlp_adapter_spec(wide), *w.specs()],
            out_specs=[WHOLE] * 3,
            scratch_shapes=[pltpu.VMEM((width, wide), BF16), w.sems(1)],
        ),
        out_shape=[
            jax.ShapeDtypeStruct((rows, wide), BF16),
            jax.ShapeDtypeStruct((rows, wide), BF16),
            jax.ShapeDtypeStruct((rows, RANK), BF16),
        ],
        name="gelu_up",
        compiler_params=params(60),
        cost_estimate=cost(2 * rows * width * wide, 2 * width * wide + 4 * rows * wide, 2 * rows * wide),
    )(scalars, x, down, up, *w.arrays)


FC_ROWS = {"da1": 0, "db1": 16, "da2": 80, "db2": 144, "da_co": 160, "db_co": 176, "pick": 192}
FC_TOTAL = 208


def mlp_kernel(w_up, w_down, w_mid, sc_ref, g_ref, slope_ref, h2_ref, h2_low_ref, std2_ref, cot_ref, r1_ref, rco_ref, oc_ref,
               a1_ref, b1_ref, a2_ref, b2_ref, a7_ref, b7_ref, *refs):
    ups, refs = refs[: len(w_up.arrays)], refs[len(w_up.arrays) :]
    downs, refs = refs[: len(w_down.arrays)], refs[len(w_down.arrays) :]
    mids, refs = refs[: len(w_mid.arrays)], refs[len(w_mid.arrays) :]
    y_ref, d2_ref, doc_ref, gac_ref, grads_ref, w1, w2, wco, u, low, dpre, sem1, sem2, sem3 = refs
    rows, width = h2_ref.shape
    wide = g_ref.shape[1]
    own = sc_ref[1]
    copies2 = w_down.bring(downs, own, 0, w2, sem2.at[0])
    copies1 = w_up.bring(ups, own, 0, w1, sem1.at[0])
    copies3 = w_mid.bring(mids, own, 1, wco, sem3.at[0])
    start_all(copies2)
    start_all(copies1)
    start_all(copies3)
    g = g_ref[...]
    r2 = low_rank(g, a2_ref[0, 0])
    wait_all(copies2)

    def second(cols):
        u[:, cols] = h2_ref[:, cols] + nn(g_ref[...], w2[:, cols]) + nn(r2, b2_ref[0, 0, :, cols])

    each(width, COLS, second)

    def third(at):
        values = u[at, :]
        centered = values - jnp.mean(values, -1, keepdims=True)
        inv_std = lax.rsqrt(jnp.mean(centered * centered, -1, keepdims=True) + NORM_EPS)
        normed = centered * inv_std
        y_ref[at, :] = normed.astype(BF16)
        d3 = normalize_back(cot_ref[at, :].astype(F32), normed, inv_std)
        u[at, :] = d3
        low[at, :] = d3.astype(BF16)

    each(rows, ROWS, third)
    d3_low = low[...]
    grads_ref[pl.ds(FC_ROWS["db2"], RANK), :] = tn(r2, d3_low).astype(BF16)
    dr2 = low_rank(d3_low, b2_ref[0, 0])
    r1 = r1_ref[...]
    run = 2 * COLS
    runs = width // run

    def slopes(at, carry):
        cols = pl.ds(pl.multiple_of(at * run, run), run)
        down_rows = nt(low[...], w2[cols, :]) + nn(dr2, a2_ref[0, 0, :, cols])
        part = (down_rows * slope_ref[:, cols].astype(F32)).astype(BF16)
        dpre[:, cols] = part
        row = pl.multiple_of((at // runs) * RANK, RANK)
        place = pl.ds(pl.multiple_of((at % runs) * run, run), run)
        grads_ref[pl.ds(FC_ROWS["da2"] + row, RANK), place] = tn(dr2, g_ref[:, cols]).astype(BF16)
        grads_ref[pl.ds(FC_ROWS["db1"] + row, RANK), place] = tn(r1, part).astype(BF16)
        return carry

    lax.fori_loop(0, wide // run, slopes, 0)
    dr1 = low_rank(dpre[...], b1_ref[0, 0])
    grads_ref[pl.ds(FC_ROWS["da1"], RANK), :] = tn(dr1, h2_low_ref[...]).astype(BF16)
    wait_all(copies1)

    def first(cols):
        u[:, cols] += nt(dpre[...], w1[cols, :]) + nn(dr1, a1_ref[0, 0, :, cols])

    each(width, COLS, first)

    def norm(at):
        d2 = normalize_back(u[at, :], h2_ref[at, :], std2_ref[at, :])
        d2_ref[at, :] = d2
        low[at, :] = d2.astype(BF16)

    each(rows, ROWS, norm)
    wait_all(copies3)
    d2_low = low[...]
    grads_ref[pl.ds(FC_ROWS["db_co"], RANK), :] = tn(rco_ref[...], d2_low).astype(BF16)
    drc = low_rank(d2_low, b7_ref[0, 0, 0])
    grads_ref[pl.ds(FC_ROWS["da_co"], RANK), :] = tn(drc, oc_ref[...]).astype(BF16)

    def cross(cols):
        doc_ref[:, cols] = (nt(low[...], wco[cols, :]) + nn(drc, a7_ref[0, 0, 0, :, cols])).astype(BF16)

    each(width, COLS, cross)
    slope_rows(gac_ref, doc_ref, oc_ref)
    mine = jnp.where(sc_ref[0] == 0, sc_ref[2], 0).astype(F32)
    grads_ref[pl.ds(FC_ROWS["pick"], 16), :] = jnp.full((16, width), mine, F32).astype(BF16)


def mlp(scalars, g, slope, h2, h2_low, std2, cot, r1, rco, oc, fc1_down, fc1_up, fc2_down, fc2_up, proj_down, proj_up, w_up, w_down, w_mid):
    rows, width = h2.shape
    wide = g.shape[1]
    return pl.pallas_call(
        functools.partial(mlp_kernel, w_up, w_down, w_mid),
        grid_spec=pltpu.PrefetchScalarGridSpec(
            num_scalar_prefetch=1,
            grid=(1,),
            in_specs=[
                *[WHOLE] * 9,
                mlp_adapter_spec(width),
                mlp_adapter_spec(wide),
                mlp_adapter_spec(wide),
                mlp_adapter_spec(width),
                adapter_spec(7, 1, width),
                adapter_spec(7, 1, width),
                *w_up.specs(),
                *w_down.specs(),
                *w_mid.specs(),
            ],
            out_specs=[WHOLE] * 5,
            scratch_shapes=[
                pltpu.VMEM((width, wide), BF16),
                pltpu.VMEM((wide, width), BF16),
                pltpu.VMEM((width, width), BF16),
                pltpu.VMEM((rows, width), F32),
                pltpu.VMEM((rows, width), BF16),
                pltpu.VMEM((rows, wide), BF16),
                w_up.sems(1),
                w_down.sems(1),
                w_mid.sems(1),
            ],
        ),
        out_shape=[
            jax.ShapeDtypeStruct((rows, width), BF16),
            jax.ShapeDtypeStruct((rows, width), F32),
            jax.ShapeDtypeStruct((rows, width), BF16),
            jax.ShapeDtypeStruct((width // PAIR, PAIR + AUG, 2 * rows), BF16),
            jax.ShapeDtypeStruct((FC_TOTAL, width), BF16),
        ],
        name="mlp",
        compiler_params=params(60),
        cost_estimate=cost(6 * rows * width * wide, 4 * width * wide + 4 * rows * wide),
    )(scalars, g, slope, h2, h2_low, std2, cot, r1, rco, oc, fc1_down, fc1_up, fc2_down, fc2_up, proj_down, proj_up,
      *w_up.arrays, *w_down.arrays, *w_mid.arrays)


def mid_back_kernel(w, sc_ref, dqc_ref, d2_ref, h1_ref, h1_low_ref, std1_ref, r_ref, o_ref, aq_ref, bq_ref, a_ref, b_ref, *refs):
    pieces, refs = refs[: len(w.arrays)], refs[len(w.arrays) :]
    d1_ref, do_ref, ga_ref, grads_ref, w_ref, low, sems = refs
    rows, width = d2_ref.shape
    first = w.bring(pieces, sc_ref[1], 2, w_ref.at[1], sems.at[1])
    second = w.bring(pieces, sc_ref[1], 0, w_ref.at[0], sems.at[0])
    start_all(first)
    start_all(second)
    dqc = dqc_ref[...]
    drq = low_rank(dqc, bq_ref[0, 0, 0])
    grads_ref[0:RANK, :] = tn(drq, h1_low_ref[...]).astype(BF16)
    grads_ref[2 * RANK : 3 * RANK, :] = tn(r_ref[:, RANK:], dqc).astype(BF16)
    wait_all(first)

    def query(cols):
        d1_ref[:, cols] = d2_ref[:, cols] + nt(dqc_ref[...], w_ref[1, cols, :]) + nn(drq, aq_ref[0, 0, 0, :, cols])

    each(width, COLS, query)

    def norm(at):
        d1 = normalize_back(d1_ref[at, :], h1_ref[at, :], std1_ref[at, :])
        d1_ref[at, :] = d1
        low[at, :] = d1.astype(BF16)

    each(rows, ROWS, norm)
    wait_all(second)
    d1_low = low[...]
    dr = low_rank(d1_low, b_ref[0, 0, 0])
    grads_ref[RANK : 2 * RANK, :] = tn(dr, o_ref[...]).astype(BF16)
    grads_ref[3 * RANK :, :] = tn(r_ref[:, :RANK], d1_low).astype(BF16)

    def out(cols):
        do_ref[:, cols] = (nt(low[...], w_ref[0, cols, :]) + nn(dr, a_ref[0, 0, 0, :, cols])).astype(BF16)

    each(width, COLS, out)

    slope_rows(ga_ref, do_ref, o_ref)


def mid_back(scalars, dqc, d2, h1, h1_low, std1, r, o, proj_down, proj_up, w):
    rows, width = d2.shape
    spec, spec_q = adapter_spec(6, 1, width), adapter_spec(3, 1, width)
    return pl.pallas_call(
        functools.partial(mid_back_kernel, w),
        grid_spec=pltpu.PrefetchScalarGridSpec(
            num_scalar_prefetch=1,
            grid=(1,),
            in_specs=[*[WHOLE] * 7, spec_q, spec_q, spec, spec, *w.specs()],
            out_specs=[WHOLE] * 4,
            scratch_shapes=[pltpu.VMEM((2, width, width), BF16), pltpu.VMEM((rows, width), BF16), w.sems(2)],
        ),
        out_shape=[
            jax.ShapeDtypeStruct((rows, width), F32),
            jax.ShapeDtypeStruct((rows, width), BF16),
            jax.ShapeDtypeStruct((width // PAIR, PAIR + AUG, 2 * rows), BF16),
            jax.ShapeDtypeStruct((4 * RANK, width), BF16),
        ],
        name="mid_back",
        compiler_params=params(60),
        cost_estimate=cost(4 * rows * width * width, 20 * rows * width + 4 * width * width),
    )(scalars, dqc, d2, h1, h1_low, std1, r, o, proj_down, proj_up, proj_down, proj_up, *w.arrays)


def add_picked(picks_ref, sequences, out, source, first=0):
    adapters, view = out
    for adapter in range(adapters):
        view(adapter)[...] = jnp.zeros(view(adapter).shape, F32)
    for at in range(sequences):
        target = view(picks_ref[first + at])
        target[...] += source(at).astype(F32)


def fc_total_kernel(picks_ref, g_ref, a1_ref, b1_ref, a2_ref, b2_ref):
    sequences, _, width = g_ref.shape
    adapters = a1_ref.shape[1]

    def put(out_ref, col, row):
        def view(adapter):
            return out_ref.at[0, adapter, :, pl.ds(col, width)]

        add_picked(picks_ref, sequences, (adapters, view), lambda at: g_ref[at, pl.ds(row, RANK), :])

    for out_ref, name in ((a1_ref, "da1"), (b1_ref, "db1"), (a2_ref, "da2"), (b2_ref, "db2")):
        for at in range(out_ref.shape[3] // width):
            put(out_ref, at * width, FC_ROWS[name] + at * RANK)


def fc_total(picks, gathered, shapes):
    return pl.pallas_call(
        fc_total_kernel,
        grid_spec=pltpu.PrefetchScalarGridSpec(
            num_scalar_prefetch=1, grid=(1,), in_specs=[WHOLE], out_specs=[WHOLE] * 4
        ),
        out_shape=[jax.ShapeDtypeStruct(s, F32) for s in shapes],
        name="fc_total",
        compiler_params=params(60),
        cost_estimate=cost(0, 8 * 160 * 1024 * 6),
    )(picks, gathered)


PROJ_ROWS = {
    0: (2, 0, 48),
    1: (2, 16, 64),
    2: (2, 32, 80),
    3: (1, 0, 32),
    4: (1, 64, 96),
    5: (1, 80, 112),
    6: (1, 16, 48),
    7: (0, FC_ROWS["da_co"], FC_ROWS["db_co"]),
}


def proj_total_kernel(picks_ref, g0_ref, g1_ref, g2_ref, down_ref, up_ref):
    adapters = down_ref.shape[2]
    for proj, (source, down_row, up_row) in PROJ_ROWS.items():
        g_ref = (g0_ref, g1_ref, g2_ref)[source]

        @pl.when(pl.program_id(0) == proj)
        def _(g_ref=g_ref, down_row=down_row, up_row=up_row, source=source):
            for out_ref, row in ((down_ref, down_row), (up_ref, up_row)):
                add_picked(
                    picks_ref, g_ref.shape[0], (adapters, lambda adapter, out_ref=out_ref: out_ref.at[0, 0, adapter]),
                    lambda at, row=row: g_ref[at, pl.ds(row, RANK), :], g_ref.shape[0] if source == 2 else 0,
                )


def proj_total(picks, g0, g1, g2, shape):
    block = pl.BlockSpec((1, 1, *shape[2:]), lambda p, s: (0, p, 0, 0, 0))
    return pl.pallas_call(
        proj_total_kernel,
        grid_spec=pltpu.PrefetchScalarGridSpec(
            num_scalar_prefetch=1, grid=(shape[1],), in_specs=[WHOLE] * 3, out_specs=[block] * 2
        ),
        out_shape=[jax.ShapeDtypeStruct(shape, F32)] * 2,
        name="proj_total",
        compiler_params=params(60),
        cost_estimate=cost(0, 8 * 256 * 1024 * 6),
    )(picks, g0, g1, g2)


class Gathering:
    def __init__(self, shard, parts, across, sibling):
        self.shard, self.parts, self.across, self.sibling = shard, parts, across, sibling
        self.half = shard.shape[0] // 2

    def begin(self):
        self.x, self.y = self.across(self.shard, 1), self.across(self.shard, 2)
        self.own = self.sibling(self.shard)

    def forward(self):
        self.xy, self.yx = self.across(self.x[: self.half], 2), self.across(self.y[self.half :], 1)
        self.sx, self.sy = self.sibling(self.x), self.sibling(self.y)

    def share(self):
        self.sxy, self.syx = self.sibling(self.xy), self.sibling(self.yx)

    def result(self):
        rows, half = self.shard.shape[0], self.half
        arrays = [self.shard, self.own, self.x, self.sx, self.y, self.sy, self.xy, self.sxy, self.yx, self.syx]
        layout = [[(0, True, who, 0, rows)] for who in range(6)]
        layout += [[(0, True, who, 0, half)] for who in (6, 7)]
        layout += [[(0, True, who, half, rows - half)] for who in (6, 7)]
        return Gathered(arrays, layout, rows // self.parts)


class Whole:
    def __init__(self, shard, parts, shards, gather):
        self.shard, self.parts, self.shards, self.gather = shard, parts, shards, gather
        self.x = self.y = self.xy = self.yx = shard

    def begin(self):
        self.whole = self.gather(self.shard)

    def forward(self):
        pass

    def share(self):
        pass

    def result(self):
        rows = self.shard.shape[0]
        return Gathered([self.whole], [[(at * rows, False, at, 0, rows) for at in range(self.shards)]], rows // self.parts)


def make_shards(mesh):
    chips, span = mesh.shape["chip"], mesh.shape["sp"]
    plane = ("chip", "core")

    def tie(*values):
        return lax.optimization_barrier(values)

    def up(values):
        return lax.ppermute(values, "sp", [(i, i + 1) for i in range(span - 1)])

    def down(values):
        return lax.ppermute(values, "sp", [(i + 1, i) for i in range(span - 1)])

    def turn(values, by):
        return lax.ppermute(values, "sp", [(i, (i + by) % span) for i in range(span)])

    def swap(values, bit):
        return lax.ppermute(values, "sp", [(i, i ^ bit) for i in range(span)])

    def across(values, bit):
        return lax.ppermute(values, "chip", [(i, i ^ bit) for i in range(chips)])

    def sibling(values):
        return lax.ppermute(values, "core", [(0, 1), (1, 0)])

    def gathering(shard, parts):
        if chips == 4:
            return Gathering(shard, parts, across, sibling)
        return Whole(shard, parts, 2 * chips, lambda v: lax.all_gather(v, plane, axis=0, tiled=True))

    def everywhere(flat):
        flat = lax.psum(flat, "sp")
        return lax.all_gather(flat, plane, axis=0, tiled=False), flat

    def everywhere_now(flat):
        bit = 1
        while bit < span:
            flat = (flat.astype(F32) + swap(flat, bit).astype(F32)).astype(BF16)
            bit *= 2
        flat, bit = flat[None], 1
        while bit < chips:
            flat = jnp.concatenate([flat, across(flat, bit)], axis=0)
            bit *= 2
        return jnp.concatenate([flat, sibling(flat)], axis=0)

    order = [2 * at for at in range(chips)] + [2 * at + 1 for at in range(chips)]

    def shards(
        inputs,
        segments,
        enc_states,
        adapter_pick,
        qkv_weights,
        out_weights,
        mlp_in,
        mlp_out,
        proj_down,
        proj_up,
        fc1_down,
        fc1_up,
        fc2_down,
        fc2_up,
        cotangent,
    ):
        x_low = inputs[0]
        memory = enc_states[0]
        tokens, width = x_low.shape
        mem_rows = memory.shape[0]
        own = lax.axis_index("chip") * 2 + lax.axis_index("core")
        scalars = jnp.stack([lax.axis_index("sp"), own, adapter_pick[0]]).astype(jnp.int32)
        tables = (proj_down, proj_up)

        a = gathering(qkv_weights[0, :3].reshape(-1, width), 3)
        b = gathering(jnp.concatenate([out_weights[0].reshape(-1, width), qkv_weights[0, 3:].reshape(-1, width)], axis=0), 5)
        c, d = gathering(mlp_in[0], 1), gathering(mlp_out[0], 1)

        seg_row = jnp.pad(segments.astype(BF16), ((0, 15), (0, width - tokens)))
        ext = [jnp.concatenate([x_low, seg_row], axis=0)]
        lane = jnp.arange(AUG, dtype=jnp.int32)
        kinds = (lane >= TERMS) & (lane < TERMS + SEG_KINDS)
        q_seg = (kinds[:, None] & (lane[:, None] - TERMS == segments)).astype(F32)
        free_seg = jnp.zeros((AUG, tokens), F32)

        def key_aug(block):
            seg = block[tokens, :tokens].astype(jnp.int32)
            return jnp.where(lane[None] < TERMS, 1.0, jnp.where(kinds[None] & (lane[None] - TERMS != seg[:, None]), FAR, 0.0)).astype(BF16)

        half = span // 2
        halves = [range(half), range(half, span)]
        free_aug = jnp.broadcast_to((lane[None] < TERMS).astype(BF16), (half * mem_rows, AUG))

        ext.append(up(ext[0]))
        a.begin()
        downs, ups = [memory], [memory]
        downs.append(down(memory))
        ext[1], a.x, a.y, b.shard, downs[1] = tie(ext[1], a.x, a.y, b.shard, downs[1])
        ext.append(up(ext[1]))
        a.forward()
        b.begin()
        downs.append(down(downs[1]))
        a.xy, a.yx, downs[2] = tie(a.xy, a.yx, downs[2])
        a.share()
        while len(downs) < span:
            downs.append(down(downs[-1]))
        w_a = a.result()

        state, ks, vs, rs, augs = None, [], [], [], []
        q = qa = o = None
        for at in range(span):
            step = Step(f"self_{at}", w_a, (0, 1, 2) if at == 0 else (1, 2), at, at == 0, at == span - 1, True)
            augs.append(key_aug(ext[at]))
            out = attend_step(step, scalars, [ext[at]], tokens, tokens, *tables, augs[at], None, q_seg, state)
            if at == 0:
                q = out.pop(0)
            ks.append(out.pop(0))
            vs.append(out.pop(0))
            rs.append(out.pop(0))
            if at == 0:
                qa = out.pop(0)
            if at < span - 1:
                state = [qa, *out]
            else:
                o, qa = out
            if at == 0:
                state[1], b.x, b.y, c.shard, ext[2] = tie(state[1], b.x, b.y, c.shard, ext[2])
                b.forward()
                c.begin()
                while len(ext) < span:
                    ext.append(up(ext[-1]))
            if at == 1:
                state[1], b.xy, b.yx = tie(state[1], b.xy, b.yx)
                b.share()
            if at == span - 2:
                state[1], ext[-1], ups[0] = tie(state[1], ext[-1], ups[0])
                ups.append(up(ups[0]))
        o, c.x, c.y, d.shard, ups[1] = tie(o, c.x, c.y, d.shard, ups[1])
        ups.append(up(ups[1]))
        c.forward()
        d.begin()
        w_b = b.result()
        h1, h1_low, std1, r_mid, qc = mid("mid", scalars, o, x_low, 0, 6, True, *tables, w_b)
        qc, c.xy, c.yx, ups[2] = tie(qc, c.xy, c.yx, ups[2])
        c.share()
        while len(ups) < span:
            ups.append(up(ups[-1]))
        w_c = c.result()
        mems = [memory] + [ups[at] + downs[span - at] for at in range(1, span)]
        state, kcs, vcs, rcs, oc = None, [], [], [], None
        for at, slots in enumerate(halves):
            step = Step(f"cross_{at}", w_b, (3, 4), at, at == 0, at == 1, False)
            out = attend_step(step, scalars, [mems[i] for i in slots], tokens, mem_rows, *tables, free_aug, qc, free_seg, state)
            kcs.append(out.pop(0))
            vcs.append(out.pop(0))
            rcs.append(out.pop(0))
            if at == 0:
                state = out
                state[1], d.x, d.y = tie(state[1], d.x, d.y)
                d.forward()
            else:
                oc, qca = out
        oc, d.xy, d.yx = tie(oc, d.xy, d.yx)
        d.share()
        w_d = d.result()
        h2, h2_low, std2, r_co = mid("mid_cross", scalars, oc, h1, 1, 7, False, *tables, w_b)
        g, slope, r_fc1 = gelu_up(scalars, h2_low, fc1_down, fc1_up, w_c)
        y, d2, doc, gac, fc_grads = mlp(
            scalars, g, slope, h2, h2_low, std2, cotangent[0], r_fc1, r_co, oc,
            fc1_down, fc1_up, fc2_down, fc2_up, *tables, w_c, w_d, w_b,
        )
        g0, summed = everywhere(fc_grads)
        picks = g0[:, FC_ROWS["pick"], 0].astype(jnp.int32)

        state, dmem_parts, dqc, cross_grads, dmem = None, {}, None, None, None
        for at in (1, 0):
            step = Step(f"cross_back_{at}", w_b, (3, 4), at, at == 1, at == 0, False)
            out = back_step(step, scalars, qca, gac, qc, doc, kcs[at], vcs[at], free_aug, rcs[at], [mems[i] for i in halves[at]], mem_rows, *tables, state, None)
            if at:
                part, *state = out
                sent = list(halves[at])
            else:
                dmem, part, dqc, cross_grads = out
                sent = list(halves[at])[1:]
            for i, slot in enumerate(sent):
                dmem_parts[slot] = turn(part[i * mem_rows : (i + 1) * mem_rows], -slot)
        d1, do, ga, mid_grads = mid_back(scalars, dqc, d2, h1, h1_low, std1, r_mid, o, *tables, w_b)
        other, summed = tie(jnp.concatenate([mid_grads, cross_grads], axis=0), summed)
        g1, _ = everywhere(other)

        state, moving = None, None
        for at in reversed(range(span)):
            step = Step(f"self_back_{at}", w_a, (0, 1, 2) if at == 0 else (1, 2), at, at == span - 1, at == 0, True)
            out = back_step(step, scalars, qa, ga, q, do, ks[at], vs[at], augs[at], rs[at], [ext[at]], tokens, *tables, state, d1)
            if at == 0:
                dx, qkv_grads = out
                dx = dx + down(moving).astype(F32)
            else:
                part, *state = out
                moving = part if moving is None else (part.astype(F32) + down(moving).astype(F32)).astype(BF16)
        for part in dmem_parts.values():
            dmem = dmem + part.astype(F32)
        fcs = fc_total(picks, g0, (fc1_down.shape, fc1_up.shape, fc2_down.shape, fc2_up.shape))
        g2 = everywhere_now(qkv_grads)
        near = picks[own ^ jnp.array(order, jnp.int32)]
        projs = proj_total(jnp.concatenate([picks, near]), g0, g1, g2, proj_down.shape)
        return (y[None], dx[None], dmem[None], *projs, *fcs)

    return shards


def solution(mesh):
    count = mesh.shape["fsdp"]
    fine = Mesh(mesh.devices.reshape(count // 2, 2, mesh.shape["sp"]), ("chip", "core", "sp"))
    fsdp = ("chip", "core")
    row = P(fsdp, "sp", None)
    return jax.shard_map(
        make_shards(fine),
        mesh=fine,
        in_specs=(
            row,
            P(fsdp, "sp"),
            row,
            P(fsdp),
            P(None, None, fsdp, None),
            P(None, None, fsdp, None),
            P(None, fsdp, None),
            P(None, fsdp, None),
            P(),
            P(),
            P(),
            P(),
            P(),
            P(),
            row,
        ),
        out_specs=(row, row, row, P(), P(), P(), P(), P(), P()),
        check_vma=False,
    )
```

```python
import functools

import jax
import jax.numpy as jnp
from jax import lax
from jax.experimental import pallas as pl
from jax.experimental.pallas import tpu as pltpu
from jax.sharding import Mesh
from jax.sharding import PartitionSpec as P

HEAD = 64
PAIR = 2 * HEAD
RANK = 16
AUG = 16
TERMS = 3
SEG_KINDS = 5
COLS = 256
NORM_EPS = 1e-05
FAR = -1e30
SCALE = HEAD**-0.5
F32 = jnp.float32
BF16 = jnp.bfloat16
ANY = pl.BlockSpec(memory_space=pltpu.HBM)
WHOLE = pl.BlockSpec(memory_space=pltpu.VMEM)


def dot(left, right, left_dim, right_dim):
    return lax.dot_general(left, right, (((left_dim,), (right_dim,)), ((), ())), preferred_element_type=F32)


def nn(left, right):
    return dot(left, right, 1, 0)


def nt(left, right):
    return dot(left, right, 1, 1)


def tn(left, right):
    return dot(left, right, 0, 0)


def params(mib):
    return pltpu.CompilerParams(vmem_limit_bytes=mib * 1024 * 1024)


def cost(us):
    return pl.CostEstimate(flops=int(us * 1.15e9), bytes_accessed=0, transcendentals=0)


def each(total, size, body, unroll=4):
    def step(at, carry):
        body(pl.ds(pl.multiple_of(at * size, size), size))
        return carry

    lax.fori_loop(0, total // size, step, 0, unroll=min(unroll, total // size))


def fetch(refs, layout, own, rows, part, target, sems):
    copies = []
    for ref, entries in zip(refs, layout):
        for source, flip, who, first, count in entries:
            low, high = max(first, part * rows), min(first + count, (part + 1) * rows)
            if low < high:
                shard = own ^ who if flip else who
                copies.append(
                    pltpu.make_async_copy(
                        ref.at[pl.ds(source + low - first, high - low)],
                        target.at[pl.ds(pl.multiple_of(shard * rows + (low - part * rows), 16), high - low)],
                        sems.at[len(copies)],
                    )
                )
    return copies


def start_all(copies):
    for copy in copies:
        copy.start()


def wait_all(copies):
    for copy in copies:
        copy.wait()


def low_half(shape, axis):
    return lax.broadcasted_iota(jnp.int32, shape, axis) < HEAD


def split_pair(rows):
    low = low_half(rows.shape, 1)
    zero = jnp.zeros_like(rows)
    return jnp.concatenate([jnp.where(low, rows, zero), jnp.where(low, zero, rows)], axis=0)


def split_pair_t(cols):
    low = low_half(cols.shape, 0)
    zero = jnp.zeros_like(cols)
    return jnp.concatenate([jnp.where(low, cols, zero), jnp.where(low, zero, cols)], axis=1)


def join_pair_t(cols):
    half = cols.shape[1] // 2
    return jnp.where(low_half((PAIR, half), 0), cols[:, :half], cols[:, half:])


def turned(rows):
    return rows.astype(F32).T


def term_rows(row, rest):
    high = row.astype(BF16).astype(F32)
    mid = (row - high).astype(BF16).astype(F32)
    low = row - high - mid
    at = lax.broadcasted_iota(jnp.int32, rest.shape, 0)
    return jnp.where(at == 0, high, jnp.where(at == 1, mid, jnp.where(at == 2, low, rest))).astype(BF16)


def causal_scores(scores):
    keys, columns = scores.shape
    row = lax.broadcasted_iota(jnp.int32, (keys, columns // 2), 0)
    col = lax.broadcasted_iota(jnp.int32, (keys, columns // 2), 1)
    keep = row <= col
    return jnp.where(jnp.concatenate([keep, keep], axis=1), scores, FAR)


def out_slopes(grads, outs):
    gt = turned(grads)
    products = gt * turned(outs)
    delta = jnp.concatenate([jnp.sum(products[:HEAD], axis=0, keepdims=True), jnp.sum(products[HEAD:], axis=0, keepdims=True)], axis=1)
    rest = jnp.zeros((AUG, delta.shape[1]), F32)
    return jnp.concatenate([split_pair_t(gt.astype(BF16)), term_rows(-delta, rest)], axis=0)


def block_back(keys, values, kaug, qa, ga, q, grads, diagonal):
    scores = nn(jnp.concatenate([keys, kaug], axis=1), qa)
    if diagonal:
        scores = causal_scores(scores)
    chances = jnp.exp(scores)
    slopes = nn(jnp.concatenate([values, kaug], axis=1), ga)
    low_slopes = (chances * slopes).astype(BF16)
    grad_values = nn(chances.astype(BF16), grads).astype(BF16)
    grad_keys = nn(low_slopes, q).astype(BF16)
    grad_q = join_pair_t(nn(turned(keys).astype(BF16), low_slopes))
    return grad_q, grad_keys, grad_values


def slope_rows(ga_ref, do_ref, o_ref):
    for at in range(ga_ref.shape[0]):
        cols = slice(at * PAIR, (at + 1) * PAIR)
        ga_ref[at] = out_slopes(do_ref[:, cols], o_ref[:, cols])


def adapter_spec(first, count, width):
    return pl.BlockSpec((1, count, 1, RANK, width), lambda *at: (0, first // count, at[-1][2], 0, 0))


def mlp_adapter_spec(width):
    return pl.BlockSpec((1, 1, RANK, width), lambda *at: (0, at[-1][2], 0, 0))


def low_rank(rows, table):
    return nt(rows, table).astype(BF16)


class Gathered:
    def __init__(self, arrays, layout, rows):
        self.arrays, self.layout, self.rows = arrays, layout, rows
        self.count = sum(len(entries) for entries in layout)

    def bring(self, refs, own, part, target, sems):
        return fetch(refs, self.layout, own, self.rows, part, target, sems)

    def specs(self):
        return [ANY] * len(self.arrays)

    def sems(self, parts):
        return pltpu.SemaphoreType.DMA((parts, self.count))


def project_into(out_ref, rows, weight, hidden, up):
    def body(cols):
        out_ref[:, cols] = (nn(rows, weight[:, cols]) + nn(hidden, up(cols))).astype(out_ref.dtype)

    each(out_ref.shape[1], COLS, body)


class Gathered:
    def __init__(self, arrays, layout, rows):
        self.arrays, self.layout, self.rows = arrays, layout, rows
        self.count = sum(len(entries) for entries in layout)

    def bring(self, refs, own, part, target, sems):
        return fetch(refs, self.layout, own, self.rows, part, target, sems)

    def specs(self):
        return [ANY] * len(self.arrays)

    def sems(self, parts):
        return pltpu.SemaphoreType.DMA((parts, self.count))


def project_into(out_ref, rows, weight, hidden, up):
    def body(cols):
        out_ref[:, cols] = (nn(rows, weight[:, cols]) + nn(hidden, up(cols))).astype(out_ref.dtype)

    each(out_ref.shape[1], COLS, body)


class Step:
    def __init__(self, name, w, parts, at, first, last, causal):
        self.name, self.w, self.parts, self.at, self.first, self.last, self.causal = name, w, parts, at, first, last, causal
        self.diagonal = causal and at == 0

    def active(self, sc_ref):
        return sc_ref[0] >= self.at if self.causal and self.at else None

    def when(self, sc_ref, condition=None):
        conditions = [c for c in (self.active(sc_ref), condition) if c is not None]
        if not conditions:
            return lambda body: body()
        return pl.when(conditions[0] if len(conditions) == 1 else conditions[0] & conditions[1])


def head_cols():
    return pl.ds(pl.multiple_of(pl.program_id(0) * PAIR, PAIR), PAIR)


def attend_step_kernel(step, count, sc_ref, *refs):
    refs = list(refs)
    make_q = step.causal and step.first

    def take(number):
        return [refs.pop(0) for _ in range(number)]

    xs = take(count)
    a_ref, b_ref, kaug_ref = take(3)
    q_ref = take(1)[0] if step.first and not make_q else None
    seg_ref = take(1)[0] if step.first else None
    qa_in, acc_in, m_in = (None, None, None) if step.first else take(3)
    pieces = take(len(step.w.arrays))
    q_out = take(1)[0] if make_q else None
    k_out, v_out, r_out = take(3)
    o_out, qa_out = None, None
    if step.first:
        qa_out = take(1)[0]
    if step.last:
        o_out, qa_out, w_ref, k_all, v_all, sems, acc_ref, m_ref = take(8)
    else:
        acc_ref, m_ref, w_ref, k_all, v_all, sems = take(6)
        acc_ref, m_ref = acc_ref.at[0], m_ref.at[0]
    q_all = take(1)[0] if make_q else None
    parts = step.parts
    kinds = len(parts)

    @step.when(sc_ref, pl.program_id(0) == 0)
    def _():
        copies = [step.w.bring(pieces, sc_ref[1], part, w_ref.at[at], sems.at[at]) for at, part in enumerate(parts)]
        for part in copies:
            start_all(part)
        low = 0
        tables = a_ref[...].reshape(-1, a_ref.shape[-1])
        for x_ref in xs:
            x = x_ref[...]
            span = pl.ds(low, x.shape[0])
            low += x.shape[0]
            hidden = low_rank(x, tables)
            r_out[span, :] = hidden
            outs = [k_all, v_all]
            if make_q:
                outs.insert(0, q_all)
            for at, out in enumerate(outs):
                slot = at + a_ref.shape[1] - len(outs)
                own = hidden[:, slot * RANK : (slot + 1) * RANK]
                if x_ref is xs[0]:
                    wait_all(copies[at])

                def body(cols, at=at, slot=slot, own=own, out=out):
                    out[span, cols] = (nn(x, w_ref[at, :, cols]) + nn(own, b_ref[0, slot, 0, :, cols])).astype(BF16)

                each(out.shape[1], COLS, body)

    @step.when(sc_ref)
    def _():
        cols = head_cols()
        keys, values = k_all[:, cols], v_all[:, cols]
        k_out[...] = keys
        v_out[...] = values
        if step.first:
            q = q_all[:, cols] if make_q else q_ref[...]
            if make_q:
                q_out[...] = q
            seg = seg_ref[...]
            qt = split_pair_t((turned(q) * SCALE).astype(BF16))
            qa = jnp.concatenate([qt, jnp.concatenate([seg, seg], axis=1).astype(BF16)], axis=0)
            if not step.last:
                qa_out[0] = qa
        else:
            qa = qa_in[0]
        scores = nn(jnp.concatenate([keys, kaug_ref[...]], axis=1), qa)
        if step.diagonal:
            scores = causal_scores(scores)
        top = jnp.max(scores, axis=0, keepdims=True)
        vt = jnp.concatenate([turned(values).astype(BF16), jnp.ones((16, keys.shape[0]), BF16)], axis=0)
        if step.first:
            acc_ref[...] = nn(vt, jnp.exp(scores - top).astype(BF16))
        else:
            old = m_in[0, 0:1]
            top = jnp.maximum(old, top)
            acc_ref[...] = acc_in[0] * jnp.exp(old - top) + nn(vt, jnp.exp(scores - top).astype(BF16))
        m_ref[...] = jnp.broadcast_to(top, m_ref.shape)

    if step.active(sc_ref) is not None:

        @pl.when(jnp.logical_not(step.active(sc_ref)))
        def _():
            acc_ref[...] = acc_in[0]
            m_ref[...] = m_in[0]

    if step.last:
        total = acc_ref[PAIR : PAIR + 1]
        o_out[...] = join_pair_t(acc_ref[:PAIR] / total).T.astype(BF16)
        lse = m_ref[0:1] + jnp.log(total)
        qa = qa_in[0]
        qa_out[0] = jnp.concatenate([qa[:PAIR], term_rows(-lse, qa[PAIR:].astype(F32))], axis=0)


def attend_step(step, scalars, xs, tokens, block_rows, proj_down, proj_up, kaug, q, seg, state):
    width = xs[0].shape[1]
    pairs = width // PAIR
    keys = block_rows * len(xs)
    make_q = step.causal and step.first
    kinds = len(step.parts)
    slots = 3 if step.causal else 2
    by_head = pl.BlockSpec((tokens, PAIR), lambda h, s: (0, h))
    keys_by_head = pl.BlockSpec((keys, PAIR), lambda h, s: (0, h))
    extended = pl.BlockSpec((1, PAIR + AUG, 2 * tokens), lambda h, s: (h, 0, 0))
    m_spec = pl.BlockSpec((1, 8, 2 * tokens), lambda h, s: (h, 0, 0))
    adapters = adapter_spec(0 if step.causal else 4, slots, width)
    q_shape = jax.ShapeDtypeStruct((tokens, width), BF16)
    kv_shape = jax.ShapeDtypeStruct((keys, width), BF16)
    qa_shape = jax.ShapeDtypeStruct((pairs, PAIR + AUG, 2 * tokens), BF16)
    state_shapes = [jax.ShapeDtypeStruct((pairs, PAIR + 16, 2 * tokens), F32), jax.ShapeDtypeStruct((pairs, 8, 2 * tokens), F32)]
    in_specs = [pl.BlockSpec((block_rows, width), lambda h, s: (0, 0))] * len(xs)
    in_specs += [adapters, adapters, pl.BlockSpec((keys, AUG), lambda h, s: (0, 0))]
    args = [*xs, proj_down, proj_up, kaug]
    if step.first and not make_q:
        in_specs.append(by_head)
        args.append(q)
    if step.first:
        in_specs.append(pl.BlockSpec((AUG, tokens), lambda h, s: (0, 0)))
        args.append(seg)
    else:
        in_specs += [extended, extended, m_spec]
        args += state
    out_specs = [keys_by_head, keys_by_head, pl.BlockSpec((keys, slots * RANK), lambda h, s: (0, 0))]
    out_shape = [kv_shape, kv_shape, jax.ShapeDtypeStruct((keys, slots * RANK), BF16)]
    if make_q:
        out_specs.insert(0, by_head)
        out_shape.insert(0, q_shape)
    scratch = [pltpu.VMEM((kinds, width, width), BF16), pltpu.VMEM((keys, width), BF16), pltpu.VMEM((keys, width), BF16), step.w.sems(kinds)]
    if step.first:
        out_specs.append(extended)
        out_shape.append(qa_shape)
    if step.last:
        out_specs += [by_head, extended]
        out_shape += [q_shape, qa_shape]
        scratch += [pltpu.VMEM((PAIR + 16, 2 * tokens), F32), pltpu.VMEM((8, 2 * tokens), F32)]
    else:
        out_specs += [extended, m_spec]
        out_shape += state_shapes
    if make_q:
        scratch.append(pltpu.VMEM((tokens, width), BF16))
    call = pl.pallas_call(
        functools.partial(attend_step_kernel, step, len(xs)),
        grid_spec=pltpu.PrefetchScalarGridSpec(
            num_scalar_prefetch=1, grid=(pairs,), in_specs=in_specs + step.w.specs(), out_specs=out_specs, scratch_shapes=scratch
        ),
        out_shape=out_shape,
        name=step.name,
        compiler_params=params(60),
        cost_estimate=cost(15),
    )
    return list(call(scalars, *args, *step.w.arrays))


def back_step_kernel(step, count, sc_ref, *refs):
    refs = list(refs)

    def take(number):
        return [refs.pop(0) for _ in range(number)]

    qa_ref, ga_ref, q_ref, do_ref, k_ref, v_ref, kaug_ref, r_ref, a_ref, b_ref = take(10)
    xs = take(count)
    dqt_in, sums_in = (None, None) if step.first else take(2)
    query = step.causal and step.last
    d1_ref = take(1)[0] if query else None
    pieces = take(len(step.w.arrays))
    dq_all = None
    if query:
        base_ref, grads_ref, w_ref, dk_all, dv_all, sems, dq_all = refs
    elif step.last:
        own_ref, part_ref, dq_ref, grads_ref, w_ref, dk_all, dv_all, sems = refs
    else:
        part_ref, dqt_ref, sums_ref, w_ref, dk_all, dv_all, sems = refs
    h = pl.program_id(0)
    final = h == pl.num_programs(0) - 1
    width = a_ref.shape[-1]
    parts = step.parts
    slots = a_ref.shape[1]

    def weights():
        return [step.w.bring(pieces, sc_ref[1], part, w_ref.at[at], sems.at[at]) for at, part in enumerate(parts)]

    @step.when(sc_ref, h == 0)
    def _():
        for part in weights():
            start_all(part)

    @step.when(sc_ref)
    def _():
        q = split_pair(q_ref[...] * jnp.asarray(SCALE, BF16))
        grad_q, grad_keys, grad_values = block_back(
            k_ref[...], v_ref[...], kaug_ref[...], qa_ref[0], ga_ref[0], q, split_pair(do_ref[...]), step.diagonal
        )
        cols = head_cols()
        dk_all[:, cols] = grad_keys
        dv_all[:, cols] = grad_values
        if not step.first:
            grad_q = grad_q + dqt_in[0]
        if query:
            dq_all[:, cols] = (grad_q * SCALE).T.astype(BF16)
        elif step.last:
            dq_ref[...] = (grad_q * SCALE).T.astype(BF16)
        else:
            dqt_ref[0] = grad_q

    if step.active(sc_ref) is not None:

        @pl.when(jnp.logical_not(step.active(sc_ref)))
        def _():
            dqt_ref[0] = jnp.zeros_like(dqt_ref[0]) if step.first else dqt_in[0]

            @pl.when(final)
            def _():
                part_ref[...] = jnp.zeros_like(part_ref)
                sums_ref[...] = jnp.zeros_like(sums_ref) if step.first else sums_in[...]

    @step.when(sc_ref, final)
    def _():
        grads = [dq_all, dk_all, dv_all] if query else [dk_all, dv_all]
        shift = slots - len(grads)
        drs, dbs = [], []
        hidden = r_ref[...]
        for at, grad_ref in enumerate(grads):
            slot = at + shift
            grad = grad_ref[...]
            drs.append(low_rank(grad, b_ref[0, slot, 0]))
            dbs.append(tn(hidden[:, slot * RANK : (slot + 1) * RANK], grad))
        dr = jnp.concatenate(drs, axis=1)
        low, da = 0, None
        for x_ref in xs:
            part = tn(dr[low : low + x_ref.shape[0]], x_ref[...])
            da = part if da is None else da + part
            low += x_ref.shape[0]
        olds = [None] * 4 if step.first else [sums_in[at * RANK : (at + 1) * RANK] for at in range(4)]
        if query:
            olds = [None, *olds[:2], None, *olds[2:]]
        total = [da[at * RANK : (at + 1) * RANK] for at in range(len(grads))] + dbs
        target = grads_ref if step.last else sums_ref
        for at, (new, old) in enumerate(zip(total, olds)):
            target[at * RANK : (at + 1) * RANK] = (new if old is None else new + old).astype(target.dtype)
        for part in weights():
            wait_all(part)
        rows = dk_all.shape[0]
        own = rows // count if step.last and not query else 0

        def body(cols):
            table = a_ref[0, shift:, 0, :, cols].reshape(len(grads) * RANK, COLS)
            value = nn(dr, table)
            for at, grad_ref in enumerate(grads):
                value = value + nt(grad_ref[...], w_ref[at, cols, :])
            if query:
                base_ref[:, cols] = value + d1_ref[:, cols]
            elif step.last:
                own_ref[:, cols] = value[:own]
                part_ref[:, cols] = value[own:].astype(BF16)
            else:
                part_ref[:, cols] = value.astype(BF16)

        each(width, COLS, body)


def back_step(step, scalars, qa, ga, q, do, k, v, kaug, r, xs, block_rows, proj_down, proj_up, state, d1):
    tokens, width = q.shape
    pairs = width // PAIR
    keys = k.shape[0]
    slots = 3 if step.causal else 2
    query = step.causal and step.last
    by_head = pl.BlockSpec((tokens, PAIR), lambda h, s: (0, h))
    keys_by_head = pl.BlockSpec((keys, PAIR), lambda h, s: (0, h))
    extended = pl.BlockSpec((1, PAIR + AUG, 2 * tokens), lambda h, s: (h, 0, 0))
    dqt_spec = pl.BlockSpec((1, PAIR, tokens), lambda h, s: (h, 0, 0))

    def whole(rows):
        return pl.BlockSpec((rows, width), lambda h, s: (0, 0))

    adapters = adapter_spec(0 if step.causal else 4, slots, width)
    in_specs = [
        extended,
        extended,
        by_head,
        by_head,
        keys_by_head,
        keys_by_head,
        pl.BlockSpec((keys, AUG), lambda h, s: (0, 0)),
        pl.BlockSpec((keys, slots * RANK), lambda h, s: (0, 0)),
        adapters,
        adapters,
        *[whole(block_rows)] * len(xs),
    ]
    args = [qa, ga, q, do, k, v, kaug, r, proj_down, proj_up, *xs]
    if not step.first:
        in_specs += [dqt_spec, whole(4 * RANK)]
        args += state
    scratch = [pltpu.VMEM((len(step.parts), width, width), BF16), pltpu.VMEM((keys, width), BF16), pltpu.VMEM((keys, width), BF16)]
    scratch.append(step.w.sems(len(step.parts)))
    if query:
        in_specs.append(whole(tokens))
        args.append(d1)
        scratch.append(pltpu.VMEM((tokens, width), BF16))
        out_specs = [whole(tokens), whole(6 * RANK)]
        out_shape = [jax.ShapeDtypeStruct((tokens, width), F32), jax.ShapeDtypeStruct((6 * RANK, width), BF16)]
    elif step.last:
        rest = keys - block_rows
        out_specs = [whole(block_rows), whole(rest), by_head, whole(4 * RANK)]
        out_shape = [
            jax.ShapeDtypeStruct((block_rows, width), F32),
            jax.ShapeDtypeStruct((rest, width), BF16),
            jax.ShapeDtypeStruct((tokens, width), BF16),
            jax.ShapeDtypeStruct((4 * RANK, width), BF16),
        ]
    else:
        out_specs = [whole(keys), dqt_spec, whole(4 * RANK)]
        out_shape = [
            jax.ShapeDtypeStruct((keys, width), BF16),
            jax.ShapeDtypeStruct((pairs, PAIR, tokens), F32),
            jax.ShapeDtypeStruct((4 * RANK, width), F32),
        ]
    return pl.pallas_call(
        functools.partial(back_step_kernel, step, len(xs)),
        grid_spec=pltpu.PrefetchScalarGridSpec(
            num_scalar_prefetch=1, grid=(pairs,), in_specs=in_specs + step.w.specs(), out_specs=out_specs, scratch_shapes=scratch
        ),
        out_shape=out_shape,
        name=step.name,
        compiler_params=params(60),
        cost_estimate=cost(17),
    )(scalars, *args, *step.w.arrays)


ROWS = 64


def normalize_rows(u_ref, norm_ref, low_ref, std_ref):
    def body(rows):
        values = u_ref[rows, :]
        centered = values - jnp.mean(values, -1, keepdims=True)
        inv_std = lax.rsqrt(jnp.mean(centered * centered, -1, keepdims=True) + NORM_EPS)
        normed = centered * inv_std
        norm_ref[rows, :] = normed
        low_ref[rows, :] = normed.astype(BF16)
        std_ref[rows, :] = inv_std

    each(u_ref.shape[0], ROWS, body)


def normalize_back(grads, normed, inv_std):
    return inv_std * (grads - jnp.mean(grads, -1, keepdims=True) - normed * jnp.mean(grads * normed, -1, keepdims=True))


def mid_kernel(w, part, query, sc_ref, o_ref, x_ref, a_ref, b_ref, aq_ref, bq_ref, *refs):
    pieces, refs = refs[: len(w.arrays)], refs[len(w.arrays) :]
    if query:
        norm_ref, low_ref, std_ref, r_ref, q_ref, w_ref, u_ref, sems = refs
    else:
        norm_ref, low_ref, std_ref, r_ref, w_ref, u_ref, sems = refs
    width = x_ref.shape[1]
    first = w.bring(pieces, sc_ref[1], part, w_ref.at[0], sems.at[0])
    start_all(first)
    if query:
        second = w.bring(pieces, sc_ref[1], 2, w_ref.at[1], sems.at[1])
        start_all(second)
    o = o_ref[...]
    hidden = low_rank(o, a_ref[0, 0, 0])
    r_ref[:, :RANK] = hidden
    wait_all(first)

    def body(cols):
        u_ref[:, cols] = x_ref[:, cols].astype(F32) + nn(o, w_ref[0, :, cols]) + nn(hidden, b_ref[0, 0, 0, :, cols])

    each(width, COLS, body)
    normalize_rows(u_ref, norm_ref, low_ref, std_ref)
    if query:
        low = low_ref[...]
        hidden_q = low_rank(low, aq_ref[0, 0, 0])
        r_ref[:, RANK:] = hidden_q
        wait_all(second)
        project_into(q_ref, low, w_ref.at[1], hidden_q, lambda cols: bq_ref[0, 0, 0, :, cols])


def mid(name, scalars, outs, residual, part, proj, query, proj_down, proj_up, w):
    rows, width = outs.shape
    shapes = [
        jax.ShapeDtypeStruct((rows, width), F32),
        jax.ShapeDtypeStruct((rows, width), BF16),
        jax.ShapeDtypeStruct((rows, 1), F32),
        jax.ShapeDtypeStruct((rows, 2 * RANK if query else RANK), BF16),
    ]
    if query:
        shapes.append(jax.ShapeDtypeStruct((rows, width), BF16))
    spec, spec_q = adapter_spec(proj, 1, width), adapter_spec(3, 1, width)
    return pl.pallas_call(
        functools.partial(mid_kernel, w, part, query),
        grid_spec=pltpu.PrefetchScalarGridSpec(
            num_scalar_prefetch=1,
            grid=(1,),
            in_specs=[WHOLE, WHOLE, spec, spec, spec_q, spec_q, *w.specs()],
            out_specs=[WHOLE] * len(shapes),
            scratch_shapes=[pltpu.VMEM((2, width, width), BF16), pltpu.VMEM((rows, width), F32), w.sems(2)],
        ),
        out_shape=shapes,
        name=name,
        compiler_params=params(60),
        cost_estimate=cost(8),
    )(scalars, outs, residual, proj_down, proj_up, proj_down, proj_up, *w.arrays)


def gelu_kernel(w, sc_ref, x_ref, a_ref, b_ref, *refs):
    pieces, (g_ref, slope_ref, r_ref, w_ref, sems) = refs[: len(w.arrays)], refs[len(w.arrays) :]
    copies = w.bring(pieces, sc_ref[1], 0, w_ref, sems.at[0])
    start_all(copies)
    x = x_ref[...]
    hidden = low_rank(x, a_ref[0, 0])
    r_ref[...] = hidden
    wait_all(copies)

    def body(cols):
        pre = nn(x, w_ref[:, cols]) + nn(hidden, b_ref[0, 0, :, cols])
        phi = 0.5 * (1.0 + lax.erf(pre * 0.7071067811865476))
        g_ref[:, cols] = (pre * phi).astype(BF16)
        slope_ref[:, cols] = (phi + pre * jnp.exp(-0.5 * pre * pre) * 0.3989422804014327).astype(BF16)

    each(g_ref.shape[1], COLS, body)


def gelu_up(scalars, x, down, up, w):
    rows, width = x.shape
    wide = up.shape[3]
    return pl.pallas_call(
        functools.partial(gelu_kernel, w),
        grid_spec=pltpu.PrefetchScalarGridSpec(
            num_scalar_prefetch=1,
            grid=(1,),
            in_specs=[WHOLE, mlp_adapter_spec(width), mlp_adapter_spec(wide), *w.specs()],
            out_specs=[WHOLE] * 3,
            scratch_shapes=[pltpu.VMEM((width, wide), BF16), w.sems(1)],
        ),
        out_shape=[
            jax.ShapeDtypeStruct((rows, wide), BF16),
            jax.ShapeDtypeStruct((rows, wide), BF16),
            jax.ShapeDtypeStruct((rows, RANK), BF16),
        ],
        name="gelu_up",
        compiler_params=params(60),
        cost_estimate=cost(15),
    )(scalars, x, down, up, *w.arrays)


FC_ROWS = {"da1": 0, "db1": 16, "da2": 80, "db2": 144, "da_co": 160, "db_co": 176, "pick": 192}
FC_TOTAL = 208


def mlp_kernel(w_up, w_down, w_mid, sc_ref, g_ref, slope_ref, h2_ref, h2_low_ref, std2_ref, cot_ref, r1_ref, rco_ref, oc_ref,
               a1_ref, b1_ref, a2_ref, b2_ref, a7_ref, b7_ref, *refs):
    ups, refs = refs[: len(w_up.arrays)], refs[len(w_up.arrays) :]
    downs, refs = refs[: len(w_down.arrays)], refs[len(w_down.arrays) :]
    mids, refs = refs[: len(w_mid.arrays)], refs[len(w_mid.arrays) :]
    y_ref, d2_ref, doc_ref, gac_ref, grads_ref, w1, w2, wco, u, low, dpre, sem1, sem2, sem3 = refs
    rows, width = h2_ref.shape
    wide = g_ref.shape[1]
    own = sc_ref[1]
    copies2 = w_down.bring(downs, own, 0, w2, sem2.at[0])
    copies1 = w_up.bring(ups, own, 0, w1, sem1.at[0])
    copies3 = w_mid.bring(mids, own, 1, wco, sem3.at[0])
    start_all(copies2)
    start_all(copies1)
    start_all(copies3)
    g = g_ref[...]
    r2 = low_rank(g, a2_ref[0, 0])
    wait_all(copies2)

    def second(cols):
        u[:, cols] = h2_ref[:, cols] + nn(g_ref[...], w2[:, cols]) + nn(r2, b2_ref[0, 0, :, cols])

    each(width, COLS, second)

    def third(at):
        values = u[at, :]
        centered = values - jnp.mean(values, -1, keepdims=True)
        inv_std = lax.rsqrt(jnp.mean(centered * centered, -1, keepdims=True) + NORM_EPS)
        normed = centered * inv_std
        y_ref[at, :] = normed.astype(BF16)
        d3 = normalize_back(cot_ref[at, :].astype(F32), normed, inv_std)
        u[at, :] = d3
        low[at, :] = d3.astype(BF16)

    each(rows, ROWS, third)
    d3_low = low[...]
    grads_ref[pl.ds(FC_ROWS["db2"], RANK), :] = tn(r2, d3_low).astype(BF16)
    dr2 = low_rank(d3_low, b2_ref[0, 0])
    r1 = r1_ref[...]
    run = 2 * COLS
    runs = width // run

    def slopes(at, carry):
        cols = pl.ds(pl.multiple_of(at * run, run), run)
        down_rows = nt(low[...], w2[cols, :]) + nn(dr2, a2_ref[0, 0, :, cols])
        part = (down_rows * slope_ref[:, cols].astype(F32)).astype(BF16)
        dpre[:, cols] = part
        row = pl.multiple_of((at // runs) * RANK, RANK)
        place = pl.ds(pl.multiple_of((at % runs) * run, run), run)
        grads_ref[pl.ds(FC_ROWS["da2"] + row, RANK), place] = tn(dr2, g_ref[:, cols]).astype(BF16)
        grads_ref[pl.ds(FC_ROWS["db1"] + row, RANK), place] = tn(r1, part).astype(BF16)
        return carry

    lax.fori_loop(0, wide // run, slopes, 0)
    dr1 = low_rank(dpre[...], b1_ref[0, 0])
    grads_ref[pl.ds(FC_ROWS["da1"], RANK), :] = tn(dr1, h2_low_ref[...]).astype(BF16)
    wait_all(copies1)

    def first(cols):
        u[:, cols] += nt(dpre[...], w1[cols, :]) + nn(dr1, a1_ref[0, 0, :, cols])

    each(width, COLS, first)

    def norm(at):
        d2 = normalize_back(u[at, :], h2_ref[at, :], std2_ref[at, :])
        d2_ref[at, :] = d2
        low[at, :] = d2.astype(BF16)

    each(rows, ROWS, norm)
    wait_all(copies3)
    d2_low = low[...]
    grads_ref[pl.ds(FC_ROWS["db_co"], RANK), :] = tn(rco_ref[...], d2_low).astype(BF16)
    drc = low_rank(d2_low, b7_ref[0, 0, 0])
    grads_ref[pl.ds(FC_ROWS["da_co"], RANK), :] = tn(drc, oc_ref[...]).astype(BF16)

    def cross(cols):
        doc_ref[:, cols] = (nt(low[...], wco[cols, :]) + nn(drc, a7_ref[0, 0, 0, :, cols])).astype(BF16)

    each(width, COLS, cross)
    slope_rows(gac_ref, doc_ref, oc_ref)
    mine = jnp.where(sc_ref[0] == 0, sc_ref[2], 0).astype(F32)
    grads_ref[pl.ds(FC_ROWS["pick"], 16), :] = jnp.full((16, width), mine, F32).astype(BF16)


def mlp(scalars, g, slope, h2, h2_low, std2, cot, r1, rco, oc, fc1_down, fc1_up, fc2_down, fc2_up, proj_down, proj_up, w_up, w_down, w_mid):
    rows, width = h2.shape
    wide = g.shape[1]
    return pl.pallas_call(
        functools.partial(mlp_kernel, w_up, w_down, w_mid),
        grid_spec=pltpu.PrefetchScalarGridSpec(
            num_scalar_prefetch=1,
            grid=(1,),
            in_specs=[
                *[WHOLE] * 9,
                mlp_adapter_spec(width),
                mlp_adapter_spec(wide),
                mlp_adapter_spec(wide),
                mlp_adapter_spec(width),
                adapter_spec(7, 1, width),
                adapter_spec(7, 1, width),
                *w_up.specs(),
                *w_down.specs(),
                *w_mid.specs(),
            ],
            out_specs=[WHOLE] * 5,
            scratch_shapes=[
                pltpu.VMEM((width, wide), BF16),
                pltpu.VMEM((wide, width), BF16),
                pltpu.VMEM((width, width), BF16),
                pltpu.VMEM((rows, width), F32),
                pltpu.VMEM((rows, width), BF16),
                pltpu.VMEM((rows, wide), BF16),
                w_up.sems(1),
                w_down.sems(1),
                w_mid.sems(1),
            ],
        ),
        out_shape=[
            jax.ShapeDtypeStruct((rows, width), BF16),
            jax.ShapeDtypeStruct((rows, width), F32),
            jax.ShapeDtypeStruct((rows, width), BF16),
            jax.ShapeDtypeStruct((width // PAIR, PAIR + AUG, 2 * rows), BF16),
            jax.ShapeDtypeStruct((FC_TOTAL, width), BF16),
        ],
        name="mlp",
        compiler_params=params(60),
        cost_estimate=cost(33),
    )(scalars, g, slope, h2, h2_low, std2, cot, r1, rco, oc, fc1_down, fc1_up, fc2_down, fc2_up, proj_down, proj_up,
      *w_up.arrays, *w_down.arrays, *w_mid.arrays)


def mid_back_kernel(w, sc_ref, dqc_ref, d2_ref, h1_ref, h1_low_ref, std1_ref, r_ref, o_ref, aq_ref, bq_ref, a_ref, b_ref, *refs):
    pieces, refs = refs[: len(w.arrays)], refs[len(w.arrays) :]
    d1_ref, do_ref, ga_ref, grads_ref, w_ref, low, sems = refs
    rows, width = d2_ref.shape
    first = w.bring(pieces, sc_ref[1], 2, w_ref.at[1], sems.at[1])
    second = w.bring(pieces, sc_ref[1], 0, w_ref.at[0], sems.at[0])
    start_all(first)
    start_all(second)
    dqc = dqc_ref[...]
    drq = low_rank(dqc, bq_ref[0, 0, 0])
    grads_ref[0:RANK, :] = tn(drq, h1_low_ref[...]).astype(BF16)
    grads_ref[2 * RANK : 3 * RANK, :] = tn(r_ref[:, RANK:], dqc).astype(BF16)
    wait_all(first)

    def query(cols):
        d1_ref[:, cols] = d2_ref[:, cols] + nt(dqc_ref[...], w_ref[1, cols, :]) + nn(drq, aq_ref[0, 0, 0, :, cols])

    each(width, COLS, query)

    def norm(at):
        d1 = normalize_back(d1_ref[at, :], h1_ref[at, :], std1_ref[at, :])
        d1_ref[at, :] = d1
        low[at, :] = d1.astype(BF16)

    each(rows, ROWS, norm)
    wait_all(second)
    d1_low = low[...]
    dr = low_rank(d1_low, b_ref[0, 0, 0])
    grads_ref[RANK : 2 * RANK, :] = tn(dr, o_ref[...]).astype(BF16)
    grads_ref[3 * RANK :, :] = tn(r_ref[:, :RANK], d1_low).astype(BF16)

    def out(cols):
        do_ref[:, cols] = (nt(low[...], w_ref[0, cols, :]) + nn(dr, a_ref[0, 0, 0, :, cols])).astype(BF16)

    each(width, COLS, out)

    slope_rows(ga_ref, do_ref, o_ref)


def mid_back(scalars, dqc, d2, h1, h1_low, std1, r, o, proj_down, proj_up, w):
    rows, width = d2.shape
    spec, spec_q = adapter_spec(6, 1, width), adapter_spec(3, 1, width)
    return pl.pallas_call(
        functools.partial(mid_back_kernel, w),
        grid_spec=pltpu.PrefetchScalarGridSpec(
            num_scalar_prefetch=1,
            grid=(1,),
            in_specs=[*[WHOLE] * 7, spec_q, spec_q, spec, spec, *w.specs()],
            out_specs=[WHOLE] * 4,
            scratch_shapes=[pltpu.VMEM((2, width, width), BF16), pltpu.VMEM((rows, width), BF16), w.sems(2)],
        ),
        out_shape=[
            jax.ShapeDtypeStruct((rows, width), F32),
            jax.ShapeDtypeStruct((rows, width), BF16),
            jax.ShapeDtypeStruct((width // PAIR, PAIR + AUG, 2 * rows), BF16),
            jax.ShapeDtypeStruct((4 * RANK, width), BF16),
        ],
        name="mid_back",
        compiler_params=params(60),
        cost_estimate=cost(11),
    )(scalars, dqc, d2, h1, h1_low, std1, r, o, proj_down, proj_up, proj_down, proj_up, *w.arrays)


def add_picked(picks_ref, sequences, out, source):
    adapters, view = out
    for adapter in range(adapters):
        view(adapter)[...] = jnp.zeros(view(adapter).shape, F32)
    for at in range(sequences):
        target = view(picks_ref[at])
        target[...] += source(at).astype(F32)


def fc_total_kernel(picks_ref, g_ref, a1_ref, b1_ref, a2_ref, b2_ref):
    sequences, _, width = g_ref.shape
    adapters = a1_ref.shape[1]

    def put(out_ref, col, row):
        def view(adapter):
            return out_ref.at[0, adapter, :, pl.ds(col, width)]

        add_picked(picks_ref, sequences, (adapters, view), lambda at: g_ref[at, pl.ds(row, RANK), :])

    for out_ref, name in ((a1_ref, "da1"), (b1_ref, "db1"), (a2_ref, "da2"), (b2_ref, "db2")):
        for at in range(out_ref.shape[3] // width):
            put(out_ref, at * width, FC_ROWS[name] + at * RANK)


def fc_total(picks, gathered, shapes):
    return pl.pallas_call(
        fc_total_kernel,
        grid_spec=pltpu.PrefetchScalarGridSpec(
            num_scalar_prefetch=1, grid=(1,), in_specs=[WHOLE], out_specs=[WHOLE] * 4
        ),
        out_shape=[jax.ShapeDtypeStruct(s, F32) for s in shapes],
        name="fc_total",
        compiler_params=params(60),
        cost_estimate=cost(6),
    )(picks, gathered)


PROJ_ROWS = {
    0: (2, 0, 48),
    1: (2, 16, 64),
    2: (2, 32, 80),
    3: (1, 0, 32),
    4: (1, 64, 96),
    5: (1, 80, 112),
    6: (1, 16, 48),
    7: (0, FC_ROWS["da_co"], FC_ROWS["db_co"]),
}


def proj_total_kernel(projs, first_source, count, sources, picks_ref, *refs):
    g_refs, (down_ref, up_ref) = refs[:sources], refs[-2:]
    adapters = down_ref.shape[2]
    for at, proj in enumerate(projs):
        source, down_row, up_row = PROJ_ROWS[proj]
        g_ref = g_refs[source - first_source]

        @pl.when(pl.program_id(0) == at)
        def _(g_ref=g_ref, down_row=down_row, up_row=up_row):
            for out_ref, row in ((down_ref, down_row), (up_ref, up_row)):
                add_picked(
                    picks_ref, g_ref.shape[0], (adapters, lambda adapter, out_ref=out_ref: out_ref.at[0, 0, adapter]),
                    lambda at, row=row: g_ref[at, pl.ds(row, RANK), :],
                )


def proj_total(picks, gathered, projs, so_far, shape):
    first = projs[0]
    block = pl.BlockSpec((1, 1, *shape[2:]), lambda p, s: (0, p + first, 0, 0, 0))
    rest = [] if so_far is None else list(so_far)
    first_source = min(PROJ_ROWS[proj][0] for proj in projs)
    return pl.pallas_call(
        functools.partial(proj_total_kernel, tuple(projs), first_source, len(rest), len(gathered)),
        grid_spec=pltpu.PrefetchScalarGridSpec(
            num_scalar_prefetch=1,
            grid=(len(projs),),
            in_specs=[WHOLE] * len(gathered) + [ANY] * len(rest),
            out_specs=[block] * 2,
        ),
        out_shape=[jax.ShapeDtypeStruct(shape, F32)] * 2,
        input_output_aliases={1 + len(gathered) + at: at for at in range(len(rest))},
        name=f"proj_total_{first}",
        compiler_params=params(60),
        cost_estimate=cost(1.4 * len(projs)),
    )(picks, *gathered, *rest)


class Gathering:
    def __init__(self, shard, parts, across, sibling):
        self.shard, self.parts, self.across, self.sibling = shard, parts, across, sibling
        self.half = shard.shape[0] // 2

    def begin(self):
        self.x, self.y = self.across(self.shard, 1), self.across(self.shard, 2)
        self.own = self.sibling(self.shard)

    def forward(self):
        self.xy, self.yx = self.across(self.x[: self.half], 2), self.across(self.y[self.half :], 1)
        self.sx, self.sy = self.sibling(self.x), self.sibling(self.y)

    def share(self):
        self.sxy, self.syx = self.sibling(self.xy), self.sibling(self.yx)

    def result(self):
        rows, half = self.shard.shape[0], self.half
        arrays = [self.shard, self.own, self.x, self.sx, self.y, self.sy, self.xy, self.sxy, self.yx, self.syx]
        layout = [[(0, True, who, 0, rows)] for who in range(6)]
        layout += [[(0, True, who, 0, half)] for who in (6, 7)]
        layout += [[(0, True, who, half, rows - half)] for who in (6, 7)]
        return Gathered(arrays, layout, rows // self.parts)


class Whole:
    def __init__(self, shard, parts, shards, gather):
        self.shard, self.parts, self.shards, self.gather = shard, parts, shards, gather
        self.x = self.y = self.xy = self.yx = shard

    def begin(self):
        self.whole = self.gather(self.shard)

    def forward(self):
        pass

    def share(self):
        pass

    def result(self):
        rows = self.shard.shape[0]
        return Gathered([self.whole], [[(at * rows, False, at, 0, rows) for at in range(self.shards)]], rows // self.parts)


def make_shards(mesh):
    chips, span = mesh.shape["chip"], mesh.shape["sp"]
    plane = ("chip", "core")

    def tie(*values):
        return lax.optimization_barrier(values)

    def turn(values, by):
        return lax.ppermute(values, "sp", [(i, (i + by) % span) for i in range(span)])

    def swap(values, bit):
        return lax.ppermute(values, "sp", [(i, i ^ bit) for i in range(span)])

    def across(values, bit):
        return lax.ppermute(values, "chip", [(i, i ^ bit) for i in range(chips)])

    def sibling(values):
        return lax.ppermute(values, "core", [(0, 1), (1, 0)])

    def gathering(shard, parts):
        if chips == 4:
            return Gathering(shard, parts, across, sibling)
        return Whole(shard, parts, 2 * chips, lambda v: lax.all_gather(v, plane, axis=0, tiled=True))

    def shards(
        inputs,
        segments,
        enc_states,
        adapter_pick,
        qkv_weights,
        out_weights,
        mlp_in,
        mlp_out,
        proj_down,
        proj_up,
        fc1_down,
        fc1_up,
        fc2_down,
        fc2_up,
        cotangent,
    ):
        x_low = inputs[0]
        memory = enc_states[0]
        tokens, width = x_low.shape
        mem_rows = memory.shape[0]
        own = lax.axis_index("chip") * 2 + lax.axis_index("core")
        scalars = jnp.stack([lax.axis_index("sp"), own, adapter_pick[0]]).astype(jnp.int32)
        tables = (proj_down, proj_up)

        a = gathering(qkv_weights[0, :3].reshape(-1, width), 3)
        b = gathering(jnp.concatenate([out_weights[0].reshape(-1, width), qkv_weights[0, 3:].reshape(-1, width)], axis=0), 5)
        c, d = gathering(mlp_in[0], 1), gathering(mlp_out[0], 1)

        seg_row = jnp.pad(segments.astype(BF16), ((0, 15), (0, width - tokens)))
        ext = [jnp.concatenate([x_low, seg_row], axis=0)]
        lane = jnp.arange(AUG, dtype=jnp.int32)
        kinds = (lane >= TERMS) & (lane < TERMS + SEG_KINDS)
        q_seg = (kinds[:, None] & (lane[:, None] - TERMS == segments)).astype(F32)
        free_seg = jnp.zeros((AUG, tokens), F32)

        def key_aug(block):
            seg = block[tokens, :tokens].astype(jnp.int32)
            return jnp.where(lane[None] < TERMS, 1.0, jnp.where(kinds[None] & (lane[None] - TERMS != seg[:, None]), FAR, 0.0)).astype(BF16)

        half = span // 2
        halves = [range(0, span, 2), range(1, span, 2)]
        free_aug = jnp.broadcast_to((lane[None] < TERMS).astype(BF16), (half * mem_rows, AUG))

        a.begin()
        ext.append(turn(ext[0], 1))
        a.x, a.y, ext[1] = tie(a.x, a.y, ext[1])
        a.forward()
        ext.append(turn(ext[1], 1))
        a.xy, a.yx, b.shard = tie(a.xy, a.yx, b.shard)
        a.share()
        b.begin()
        w_a = a.result()
        mems = [memory]

        state, ks, vs, rs, augs = None, [], [], [], []
        q = qa = o = None
        for at in range(span):
            step = Step(f"self_{at}", w_a, (0, 1, 2) if at == 0 else (1, 2), at, at == 0, at == span - 1, True)
            if at:
                ext[at], state[1] = tie(ext[at], state[1])
            augs.append(key_aug(ext[at]))
            out = attend_step(step, scalars, [ext[at]], tokens, tokens, *tables, augs[at], None, q_seg, state)
            if at == 0:
                q = out.pop(0)
            ks.append(out.pop(0))
            vs.append(out.pop(0))
            rs.append(out.pop(0))
            if at == 0:
                qa = out.pop(0)
            if at < span - 1:
                state = [qa, *out]
            else:
                o, qa = out
            if at == 0:
                state[1], ext[-1] = tie(state[1], ext[-1])
                while len(ext) < span:
                    ext.append(turn(ext[-1], 1))
            elif at == 1:
                state[1], b.x, b.y, ext[-1], on = tie(state[1], b.x, b.y, ext[-1], memory)
                b.forward()
                mems.append(turn(on, 1))
            elif at == 2 and at < span - 1:
                state[1], b.xy, b.yx, c.shard, mems[-1] = tie(state[1], b.xy, b.yx, c.shard, mems[-1])
                b.share()
                c.begin()
                mems.append(turn(mems[-1], 1))
        o, mems[-1] = tie(o, mems[-1])
        while len(mems) < span:
            mems.append(turn(mems[-1], 1))
        w_b = b.result()
        h1, h1_low, std1, r_mid, qc = mid("mid", scalars, o, x_low, 0, 6, True, *tables, w_b)
        qc, c.x, c.y = tie(qc, c.x, c.y)
        c.forward()
        state, kcs, vcs, rcs, oc = None, [], [], [], None
        for at, slots in enumerate(halves):
            step = Step(f"cross_{at}", w_b, (3, 4), at, at == 0, at == 1, False)
            out = attend_step(step, scalars, [mems[i] for i in slots], tokens, mem_rows, *tables, free_aug, qc, free_seg, state)
            kcs.append(out.pop(0))
            vcs.append(out.pop(0))
            rcs.append(out.pop(0))
            if at == 0:
                state = out
                state[1], c.xy, c.yx, d.shard, *mems[1:] = tie(state[1], c.xy, c.yx, d.shard, *mems[1:])
                c.share()
                d.begin()
            else:
                oc, qca = out
        h2, h2_low, std2, r_co = mid("mid_cross", scalars, oc, h1, 1, 7, False, *tables, w_b)
        h2_low, d.x, d.y = tie(h2_low, d.x, d.y)
        d.forward()
        w_c = c.result()
        g, slope, r_fc1 = gelu_up(scalars, h2_low, fc1_down, fc1_up, w_c)
        g, d.xy, d.yx = tie(g, d.xy, d.yx)
        d.share()
        w_d = d.result()
        y, d2, doc, gac, fc_grads = mlp(
            scalars, g, slope, h2, h2_low, std2, cotangent[0], r_fc1, r_co, oc,
            fc1_down, fc1_up, fc2_down, fc2_up, *tables, w_c, w_d, w_b,
        )
        g0 = lax.psum(fc_grads, "sp")

        state, dmem_parts, dqc, cross_grads, dmem = None, {}, None, None, None
        for at in (1, 0):
            step = Step(f"cross_back_{at}", w_b, (3, 4), at, at == 1, at == 0, False)
            out = back_step(step, scalars, qca, gac, qc, doc, kcs[at], vcs[at], free_aug, rcs[at], [mems[i] for i in halves[at]], mem_rows, *tables, state, None)
            if at:
                part, *state = out
            else:
                dmem, late, dqc, cross_grads = out
                continue
            for i, slot in enumerate(halves[at]):
                dmem_parts[slot] = turn(part[i * mem_rows : (i + 1) * mem_rows], -slot)
        d1, do, ga, mid_grads = mid_back(scalars, dqc, d2, h1, h1_low, std1, r_mid, o, *tables, w_b)
        ga, *values = tie(ga, *dmem_parts.values())
        dmem_parts = dict(zip(dmem_parts, values))
        g0, g1 = tie(g0, jnp.concatenate([mid_grads, cross_grads], axis=0))
        g1 = lax.psum(g1, "sp")
        g0 = g0[None]

        def doubled(values, bit):
            return jnp.concatenate([values, across(values, bit)], axis=0)

        bits = [1 << at for at in range(chips.bit_length() - 1)]
        state, moving, at_bit = None, None, 0
        for at in reversed(range(span)):
            step = Step(f"self_back_{at}", w_a, (0, 1, 2) if at == 0 else (1, 2), at, at == span - 1, at == 0, True)
            out = back_step(step, scalars, qa, ga, q, do, ks[at], vs[at], augs[at], rs[at], [ext[at]], tokens, *tables, state, d1)
            if at == 0:
                dx, g2 = out
                dx, g2, moving, g0, g1 = tie(dx, g2, moving, g0, g1)
                dx = dx + moving.astype(F32)
            else:
                part, *state = out
                if at == span - 1:
                    part, state[0] = tie(part, state[0])
                else:
                    part, state[0], moving, g0, *on = tie(part, state[0], moving, g0, *([g1] if at == 1 else []))
                    part = (part.astype(F32) + moving.astype(F32)).astype(BF16)
                    part, state[0] = tie(part, state[0])
                moving = turn(part, -1)
                if at_bit < len(bits):
                    g0 = doubled(g0, bits[at_bit])
                    at_bit += 1
                if at == 1:
                    while at_bit < len(bits):
                        g0 = doubled(g0, bits[at_bit])
                        at_bit += 1
                    g1 = doubled(on[0][None], bits[0])
        g0 = jnp.concatenate([g0, sibling(g0)], axis=0)
        g2 = (g2.astype(F32) + swap(g2, 1).astype(F32)).astype(BF16)
        g2, g1, g0 = tie(g2, g1, g0)
        for bit in bits[1:]:
            g1 = doubled(g1, bit)
        picks = g0[:, FC_ROWS["pick"], 0].astype(jnp.int32)
        fcs = fc_total(picks, g0, (fc1_down.shape, fc1_up.shape, fc2_down.shape, fc2_up.shape))
        bit = 2
        while bit < span:
            g2 = (g2.astype(F32) + swap(g2, bit).astype(F32)).astype(BF16)
            bit *= 2
        g2, g1, late, picks, *fcs = tie(g2, g1, late, picks, *fcs)
        for i, slot in enumerate(list(halves[0])[1:]):
            dmem_parts[slot] = turn(late[i * mem_rows : (i + 1) * mem_rows], -slot)
        g1 = jnp.concatenate([g1, sibling(g1)], axis=0)
        g2 = doubled(g2[None], bits[0])
        g2, g1, picks = tie(g2, g1, picks)
        projs = proj_total(picks, (g0, g1), range(3, 8), None, proj_down.shape)
        for bit in bits[1:]:
            g2 = doubled(g2, bit)
        g2, *projs = tie(g2, *projs)
        g2 = jnp.concatenate([g2, sibling(g2)], axis=0)
        projs = proj_total(picks, (g2,), range(3), projs, proj_down.shape)
        for part in dmem_parts.values():
            dmem = dmem + part.astype(F32)
        return (y[None], dx[None], dmem[None], *projs, *fcs)

    return shards


def solution(mesh):
    count = mesh.shape["fsdp"]
    fine = Mesh(mesh.devices.reshape(count // 2, 2, mesh.shape["sp"]), ("chip", "core", "sp"))
    fsdp = ("chip", "core")
    row = P(fsdp, "sp", None)
    return jax.shard_map(
        make_shards(fine),
        mesh=fine,
        in_specs=(
            row,
            P(fsdp, "sp"),
            row,
            P(fsdp),
            P(None, None, fsdp, None),
            P(None, None, fsdp, None),
            P(None, fsdp, None),
            P(None, fsdp, None),
            P(),
            P(),
            P(),
            P(),
            P(),
            P(),
            row,
        ),
        out_specs=(row, row, row, P(), P(), P(), P(), P(), P()),
        check_vma=False,
    )
```

```python
import functools

import jax
import jax.numpy as jnp
from jax import lax
from jax.experimental import pallas as pl
from jax.experimental.pallas import tpu as pltpu
from jax.sharding import Mesh
from jax.sharding import PartitionSpec as P

HEAD = 64
PAIR = 2 * HEAD
RANK = 16
AUG = 16
TERMS = 3
SEG_KINDS = 5
COLS = 256
NORM_EPS = 1e-05
FAR = -1e30
SCALE = HEAD**-0.5
F32 = jnp.float32
BF16 = jnp.bfloat16
ANY = pl.BlockSpec(memory_space=pltpu.HBM)
WHOLE = pl.BlockSpec(memory_space=pltpu.VMEM)


def dot(left, right, left_dim, right_dim):
    return lax.dot_general(left, right, (((left_dim,), (right_dim,)), ((), ())), preferred_element_type=F32)


def nn(left, right):
    return dot(left, right, 1, 0)


def nt(left, right):
    return dot(left, right, 1, 1)


def tn(left, right):
    return dot(left, right, 0, 0)


def params(mib):
    return pltpu.CompilerParams(vmem_limit_bytes=mib * 1024 * 1024)


def cost(us):
    return pl.CostEstimate(flops=int(us * 1.15e9), bytes_accessed=0, transcendentals=0)


def each(total, size, body, unroll=4):
    def step(at, carry):
        body(pl.ds(pl.multiple_of(at * size, size), size))
        return carry

    lax.fori_loop(0, total // size, step, 0, unroll=min(unroll, total // size))


def fetch(refs, layout, own, rows, part, target, sems):
    copies = []
    for ref, entries in zip(refs, layout):
        for source, flip, who, first, count in entries:
            low, high = max(first, part * rows), min(first + count, (part + 1) * rows)
            if low < high:
                shard = own ^ who if flip else who
                copies.append(
                    pltpu.make_async_copy(
                        ref.at[pl.ds(source + low - first, high - low)],
                        target.at[pl.ds(pl.multiple_of(shard * rows + (low - part * rows), 16), high - low)],
                        sems.at[len(copies)],
                    )
                )
    return copies


def start_all(copies):
    for copy in copies:
        copy.start()


def wait_all(copies):
    for copy in copies:
        copy.wait()


def low_half(shape, axis):
    return lax.broadcasted_iota(jnp.int32, shape, axis) < HEAD


def split_pair(rows):
    low = low_half(rows.shape, 1)
    zero = jnp.zeros_like(rows)
    return jnp.concatenate([jnp.where(low, rows, zero), jnp.where(low, zero, rows)], axis=0)


def split_pair_t(cols):
    low = low_half(cols.shape, 0)
    zero = jnp.zeros_like(cols)
    return jnp.concatenate([jnp.where(low, cols, zero), jnp.where(low, zero, cols)], axis=1)


def join_pair_t(cols):
    half = cols.shape[1] // 2
    return jnp.where(low_half((PAIR, half), 0), cols[:, :half], cols[:, half:])


def turned(rows):
    return rows.astype(F32).T


def term_rows(row, rest):
    high = row.astype(BF16).astype(F32)
    mid = (row - high).astype(BF16).astype(F32)
    low = row - high - mid
    at = lax.broadcasted_iota(jnp.int32, rest.shape, 0)
    return jnp.where(at == 0, high, jnp.where(at == 1, mid, jnp.where(at == 2, low, rest))).astype(BF16)


def causal_scores(scores):
    keys, columns = scores.shape
    row = lax.broadcasted_iota(jnp.int32, (keys, columns // 2), 0)
    col = lax.broadcasted_iota(jnp.int32, (keys, columns // 2), 1)
    keep = row <= col
    return jnp.where(jnp.concatenate([keep, keep], axis=1), scores, FAR)


def out_slopes(grads, outs):
    gt = turned(grads)
    products = gt * turned(outs)
    delta = jnp.concatenate([jnp.sum(products[:HEAD], axis=0, keepdims=True), jnp.sum(products[HEAD:], axis=0, keepdims=True)], axis=1)
    rest = jnp.zeros((AUG, delta.shape[1]), F32)
    return jnp.concatenate([split_pair_t(gt.astype(BF16)), term_rows(-delta, rest)], axis=0)


def block_back(keys, values, kaug, qa, ga, q, grads, diagonal):
    scores = nn(jnp.concatenate([keys, kaug], axis=1), qa)
    if diagonal:
        scores = causal_scores(scores)
    chances = jnp.exp(scores)
    slopes = nn(jnp.concatenate([values, kaug], axis=1), ga)
    low_slopes = (chances * slopes).astype(BF16)
    grad_values = nn(chances.astype(BF16), grads).astype(BF16)
    grad_keys = nn(low_slopes, q).astype(BF16)
    grad_q = join_pair_t(nn(turned(keys).astype(BF16), low_slopes))
    return grad_q, grad_keys, grad_values


def slope_rows(ga_ref, do_ref, o_ref):
    for at in range(ga_ref.shape[0]):
        cols = slice(at * PAIR, (at + 1) * PAIR)
        ga_ref[at] = out_slopes(do_ref[:, cols], o_ref[:, cols])


def adapter_spec(first, count, width):
    return pl.BlockSpec((1, count, 1, RANK, width), lambda *at: (0, first // count, at[-1][2], 0, 0))


def mlp_adapter_spec(width):
    return pl.BlockSpec((1, 1, RANK, width), lambda *at: (0, at[-1][2], 0, 0))


def low_rank(rows, table):
    return nt(rows, table).astype(BF16)


class Gathered:
    def __init__(self, arrays, layout, rows):
        self.arrays, self.layout, self.rows = arrays, layout, rows
        self.count = sum(len(entries) for entries in layout)

    def bring(self, refs, own, part, target, sems):
        return fetch(refs, self.layout, own, self.rows, part, target, sems)

    def specs(self):
        return [ANY] * len(self.arrays)

    def sems(self, parts):
        return pltpu.SemaphoreType.DMA((parts, self.count))


def project_into(out_ref, rows, weight, hidden, up):
    def body(cols):
        out_ref[:, cols] = (nn(rows, weight[:, cols]) + nn(hidden, up(cols))).astype(out_ref.dtype)

    each(out_ref.shape[1], COLS, body)


class Gathered:
    def __init__(self, arrays, layout, rows):
        self.arrays, self.layout, self.rows = arrays, layout, rows
        self.count = sum(len(entries) for entries in layout)

    def bring(self, refs, own, part, target, sems):
        return fetch(refs, self.layout, own, self.rows, part, target, sems)

    def specs(self):
        return [ANY] * len(self.arrays)

    def sems(self, parts):
        return pltpu.SemaphoreType.DMA((parts, self.count))


def project_into(out_ref, rows, weight, hidden, up):
    def body(cols):
        out_ref[:, cols] = (nn(rows, weight[:, cols]) + nn(hidden, up(cols))).astype(out_ref.dtype)

    each(out_ref.shape[1], COLS, body)


PER = 2


class Step:
    def __init__(self, name, w, parts, blocks, first, last, causal):
        self.name, self.w, self.parts, self.blocks, self.first, self.last, self.causal = name, w, parts, blocks, first, last, causal

    def on(self, sc_ref, at, condition=None):
        conditions = [] if condition is None else [condition]
        if self.causal and at:
            conditions.append(sc_ref[0] >= at)
        if not conditions:
            return lambda body: body()
        return pl.when(conditions[0] if len(conditions) == 1 else conditions[0] & conditions[1])


def head_cols(pair):
    return pl.ds(pl.multiple_of((pl.program_id(0) * PER + pair) * PAIR, PAIR), PAIR)


def pair_cols(pair):
    return slice(pair * PAIR, (pair + 1) * PAIR)


def attend_step_kernel(step, counts, sc_ref, *refs):
    refs = list(refs)
    make_q = step.causal and step.first

    def take(number):
        return [refs.pop(0) for _ in range(number)]

    groups = len(counts)
    xs = [take(count) for count in counts]
    kaugs = take(groups)
    a_ref, b_ref = take(2)
    q_ref = take(1)[0] if step.first and not make_q else None
    seg_ref = take(1)[0] if step.first else None
    qa_in, acc_in, m_in = (None, None, None) if step.first else take(3)
    pieces = take(len(step.w.arrays))
    q_out = take(1)[0] if make_q else None
    k_outs, v_outs, r_outs = take(groups), take(groups), take(groups)
    qa_out, o_out = None, None
    if step.first and not step.last:
        qa_out = take(1)[0]
    if step.last:
        o_out, qa_out, w_ref, sems = take(4)
    else:
        acc_ref, m_ref, w_ref, sems = take(4)
    k_alls, v_alls = take(groups), take(groups)
    if step.last:
        acc_ref, m_ref = take(2)
    q_all = take(1)[0] if make_q else None
    parts = step.parts

    def copies(at):
        return step.w.bring(pieces, sc_ref[1], parts[at], w_ref.at[at], sems.at[at])

    for group, at in enumerate(step.blocks):

        @step.on(sc_ref, at, pl.program_id(0) == 0)
        def _(group=group):
            if group == 0:
                for slot in range(len(parts)):
                    start_all(copies(slot))
            low = 0
            tables = a_ref[...].reshape(-1, a_ref.shape[-1])
            for x_ref in xs[group]:
                x = x_ref[...]
                span = pl.ds(low, x.shape[0])
                low += x.shape[0]
                hidden = low_rank(x, tables)
                r_outs[group][span, :] = hidden
                outs = [k_alls[group], v_alls[group]]
                if make_q and group == 0:
                    outs.insert(0, q_all)
                for number, out in enumerate(outs):
                    place = number + len(parts) - len(outs)
                    slot = number + a_ref.shape[1] - len(outs)
                    own = hidden[:, slot * RANK : (slot + 1) * RANK]
                    if group == 0 and x_ref is xs[0][0]:
                        wait_all(copies(place))

                    def body(cols, place=place, slot=slot, own=own, out=out):
                        out[span, cols] = (nn(x, w_ref[place, :, cols]) + nn(own, b_ref[0, slot, 0, :, cols])).astype(BF16)

                    each(out.shape[1], COLS, body)

    qas = []
    for pair in range(PER):
        if step.first:
            q = q_all[:, head_cols(pair)] if make_q else q_ref[:, pair_cols(pair)]
            if make_q:
                q_out[:, pair_cols(pair)] = q
            seg = seg_ref[...]
            qt = split_pair_t((turned(q) * SCALE).astype(BF16))
            qas.append(jnp.concatenate([qt, jnp.concatenate([seg, seg], axis=1).astype(BF16)], axis=0))
            if not step.last:
                qa_out[pair] = qas[pair]
        else:
            qas.append(qa_in[pair])

    def block(group, at, opens):
        for pair in range(PER):
            keys, values = k_alls[group][:, head_cols(pair)], v_alls[group][:, head_cols(pair)]
            k_outs[group][:, pair_cols(pair)] = keys
            v_outs[group][:, pair_cols(pair)] = values
            scores = nn(jnp.concatenate([keys, kaugs[group][...]], axis=1), qas[pair])
            if step.causal and at == 0:
                scores = causal_scores(scores)
            top = jnp.max(scores, axis=0, keepdims=True)
            vt = jnp.concatenate([turned(values).astype(BF16), jnp.ones((16, keys.shape[0]), BF16)], axis=0)
            if opens and step.first:
                acc_ref[pair] = nn(vt, jnp.exp(scores - top).astype(BF16))
            else:
                old = m_in[pair, 0:1] if opens else m_ref[pair, 0:1]
                so_far = acc_in[pair] if opens else acc_ref[pair]
                top = jnp.maximum(old, top)
                acc_ref[pair] = so_far * jnp.exp(old - top) + nn(vt, jnp.exp(scores - top).astype(BF16))
            m_ref[pair] = jnp.broadcast_to(top, m_ref.shape[1:])

    for group, at in enumerate(step.blocks):
        step.on(sc_ref, at)(functools.partial(block, group, at, group == 0))
    if step.causal and step.blocks[0]:

        @pl.when(sc_ref[0] < step.blocks[0])
        def _():
            acc_ref[...] = acc_in[...]
            m_ref[...] = m_in[...]

    if step.last:
        for pair in range(PER):
            total = acc_ref[pair, PAIR : PAIR + 1]
            o_out[:, pair_cols(pair)] = join_pair_t(acc_ref[pair, :PAIR] / total).T.astype(BF16)
            lse = m_ref[pair, 0:1] + jnp.log(total)
            qa_out[pair] = jnp.concatenate([qas[pair][:PAIR], term_rows(-lse, qas[pair][PAIR:].astype(F32))], axis=0)


def attend_step(step, scalars, xs, tokens, block_rows, tables, kaugs, q, seg, state):
    width = xs[0][0].shape[1]
    pairs = width // PAIR
    keys = [block_rows * len(group) for group in xs]
    make_q = step.causal and step.first
    kinds = len(step.parts)
    slots = 3 if step.causal else 2
    by_head = pl.BlockSpec((tokens, PER * PAIR), lambda h, s: (0, h))
    extended = pl.BlockSpec((PER, PAIR + AUG, 2 * tokens), lambda h, s: (h, 0, 0))
    m_spec = pl.BlockSpec((PER, 8, 2 * tokens), lambda h, s: (h, 0, 0))
    adapters = adapter_spec(0 if step.causal else 4, slots, width)
    q_shape = jax.ShapeDtypeStruct((tokens, width), BF16)
    qa_shape = jax.ShapeDtypeStruct((pairs, PAIR + AUG, 2 * tokens), BF16)
    in_specs = [pl.BlockSpec((block_rows, width), lambda h, s: (0, 0))] * sum(len(group) for group in xs)
    in_specs += [pl.BlockSpec((rows, AUG), lambda h, s: (0, 0)) for rows in keys] + [adapters, adapters]
    args = [x for group in xs for x in group] + [*kaugs, *tables]
    if step.first and not make_q:
        in_specs.append(by_head)
        args.append(q)
    if step.first:
        in_specs.append(pl.BlockSpec((AUG, tokens), lambda h, s: (0, 0)))
        args.append(seg)
    else:
        in_specs += [extended, extended, m_spec]
        args += state
    keys_by_head = [pl.BlockSpec((rows, PER * PAIR), lambda h, s: (0, h)) for rows in keys]
    out_specs = [*keys_by_head, *keys_by_head, *[pl.BlockSpec((rows, slots * RANK), lambda h, s: (0, 0)) for rows in keys]]
    kv_shapes = [jax.ShapeDtypeStruct((rows, width), BF16) for rows in keys]
    out_shape = [*kv_shapes, *kv_shapes, *[jax.ShapeDtypeStruct((rows, slots * RANK), BF16) for rows in keys]]
    if make_q:
        out_specs.insert(0, by_head)
        out_shape.insert(0, q_shape)
    scratch = [pltpu.VMEM((kinds, width, width), BF16), step.w.sems(kinds)]
    scratch += [pltpu.VMEM((rows, width), BF16) for rows in keys] * 2
    state_shapes = [(PAIR + 16, 2 * tokens), (8, 2 * tokens)]
    if step.first and not step.last:
        out_specs.append(extended)
        out_shape.append(qa_shape)
    if step.last:
        out_specs += [by_head, extended]
        out_shape += [q_shape, qa_shape]
        scratch += [pltpu.VMEM((PER, *shape), F32) for shape in state_shapes]
    else:
        out_specs += [extended, m_spec]
        out_shape += [jax.ShapeDtypeStruct((pairs, *shape), F32) for shape in state_shapes]
    if make_q:
        scratch.append(pltpu.VMEM((tokens, width), BF16))
    call = pl.pallas_call(
        functools.partial(attend_step_kernel, step, [len(group) for group in xs]),
        grid_spec=pltpu.PrefetchScalarGridSpec(
            num_scalar_prefetch=1, grid=(pairs // PER,), in_specs=in_specs + step.w.specs(), out_specs=out_specs, scratch_shapes=scratch
        ),
        out_shape=out_shape,
        name=step.name,
        compiler_params=params(60),
        cost_estimate=cost(sum(keys) / 32),
    )
    out = list(call(scalars, *args, *step.w.arrays))
    q = out.pop(0) if make_q else q
    count = len(xs)
    return q, out[:count], out[count : 2 * count], out[2 * count : 3 * count], out[3 * count :]


def back_step_kernel(step, count, sc_ref, *refs):
    refs = list(refs)

    def take(number):
        return [refs.pop(0) for _ in range(number)]

    qa_ref, ga_ref, q_ref, do_ref, k_ref, v_ref, kaug_ref, r_ref, a_ref, b_ref = take(10)
    xs = take(count)
    dqt_in, sums_in = (None, None) if step.first else take(2)
    query = step.causal and step.last
    d1_ref = take(1)[0] if query else None
    pieces = take(len(step.w.arrays))
    dq_all = None
    if query:
        base_ref, grads_ref, w_ref, dk_all, dv_all, sems, dq_all = refs
    elif step.last:
        own_ref, part_ref, dq_ref, grads_ref, w_ref, dk_all, dv_all, sems = refs
    else:
        part_ref, dqt_ref, sums_ref, w_ref, dk_all, dv_all, sems = refs
    h = pl.program_id(0)
    final = h == pl.num_programs(0) - 1
    width = a_ref.shape[-1]
    parts = step.parts
    slots = a_ref.shape[1]
    keys = k_ref.shape[0]
    block = min(keys, 512)
    (at,) = step.blocks

    def weights():
        return [step.w.bring(pieces, sc_ref[1], part, w_ref.at[place], sems.at[place]) for place, part in enumerate(parts)]

    @step.on(sc_ref, at, h == 0)
    def _():
        for part in weights():
            start_all(part)

    @step.on(sc_ref, at)
    def _():
        for pair in range(PER):
            cols, all_cols = pair_cols(pair), head_cols(pair)
            q = split_pair(q_ref[:, cols] * jnp.asarray(SCALE, BF16))
            grads = split_pair(do_ref[:, cols])
            total = None
            for low in range(0, keys, block):
                span = slice(low, low + block)
                grad_q, grad_keys, grad_values = block_back(
                    k_ref[span, cols], v_ref[span, cols], kaug_ref[span], qa_ref[pair], ga_ref[pair], q, grads, step.causal and at == 0
                )
                dk_all[span, all_cols] = grad_keys
                dv_all[span, all_cols] = grad_values
                total = grad_q if total is None else total + grad_q
            if not step.first:
                total = total + dqt_in[pair]
            if query:
                dq_all[:, all_cols] = (total * SCALE).T.astype(BF16)
            elif step.last:
                dq_ref[:, cols] = (total * SCALE).T.astype(BF16)
            else:
                dqt_ref[pair] = total

    if step.causal and at:

        @pl.when(sc_ref[0] < at)
        def _():
            dqt_ref[...] = jnp.zeros_like(dqt_ref[...]) if step.first else dqt_in[...]

            @pl.when(final)
            def _():
                part_ref[...] = jnp.zeros_like(part_ref)
                sums_ref[...] = jnp.zeros_like(sums_ref) if step.first else sums_in[...]

    @step.on(sc_ref, at, final)
    def _():
        grads = [dq_all, dk_all, dv_all] if query else [dk_all, dv_all]
        shift = slots - len(grads)
        drs, dbs = [], []
        hidden = r_ref[...]
        for place, grad_ref in enumerate(grads):
            slot = place + shift
            grad = grad_ref[...]
            drs.append(low_rank(grad, b_ref[0, slot, 0]))
            dbs.append(tn(hidden[:, slot * RANK : (slot + 1) * RANK], grad))
        dr = jnp.concatenate(drs, axis=1)
        low, da = 0, None
        for x_ref in xs:
            part = tn(dr[low : low + x_ref.shape[0]], x_ref[...])
            da = part if da is None else da + part
            low += x_ref.shape[0]
        olds = [None] * 4 if step.first else [sums_in[place * RANK : (place + 1) * RANK] for place in range(4)]
        if query:
            olds = [None, *olds[:2], None, *olds[2:]]
        total = [da[place * RANK : (place + 1) * RANK] for place in range(len(grads))] + dbs
        target = grads_ref if step.last else sums_ref
        for place, (new, old) in enumerate(zip(total, olds)):
            target[place * RANK : (place + 1) * RANK] = (new if old is None else new + old).astype(target.dtype)
        for part in weights():
            wait_all(part)
        own = keys // count if step.last and not query else 0

        def body(cols):
            table = a_ref[0, shift:, 0, :, cols].reshape(len(grads) * RANK, COLS)
            value = nn(dr, table)
            for place, grad_ref in enumerate(grads):
                value = value + nt(grad_ref[...], w_ref[place, cols, :])
            if query:
                base_ref[:, cols] = value + d1_ref[:, cols]
            elif step.last:
                own_ref[:, cols] = value[:own]
                part_ref[:, cols] = value[own:].astype(BF16)
            else:
                part_ref[:, cols] = value.astype(BF16)

        each(width, COLS, body)


def back_step(step, scalars, qa, ga, q, do, k, v, kaug, r, xs, block_rows, tables, state, d1):
    tokens, width = q.shape
    pairs = width // PAIR
    keys = k.shape[0]
    slots = 3 if step.causal else 2
    query = step.causal and step.last
    by_head = pl.BlockSpec((tokens, PER * PAIR), lambda h, s: (0, h))
    keys_by_head = pl.BlockSpec((keys, PER * PAIR), lambda h, s: (0, h))
    extended = pl.BlockSpec((PER, PAIR + AUG, 2 * tokens), lambda h, s: (h, 0, 0))
    dqt_spec = pl.BlockSpec((PER, PAIR, tokens), lambda h, s: (h, 0, 0))

    def whole(rows):
        return pl.BlockSpec((rows, width), lambda h, s: (0, 0))

    adapters = adapter_spec(0 if step.causal else 4, slots, width)
    in_specs = [
        extended,
        extended,
        by_head,
        by_head,
        keys_by_head,
        keys_by_head,
        pl.BlockSpec((keys, AUG), lambda h, s: (0, 0)),
        pl.BlockSpec((keys, slots * RANK), lambda h, s: (0, 0)),
        adapters,
        adapters,
        *[whole(block_rows)] * len(xs),
    ]
    args = [qa, ga, q, do, k, v, kaug, r, *tables, *xs]
    if not step.first:
        in_specs += [dqt_spec, whole(4 * RANK)]
        args += state
    scratch = [pltpu.VMEM((len(step.parts), width, width), BF16), pltpu.VMEM((keys, width), BF16), pltpu.VMEM((keys, width), BF16)]
    scratch.append(step.w.sems(len(step.parts)))
    if query:
        in_specs.append(whole(tokens))
        args.append(d1)
        scratch.append(pltpu.VMEM((tokens, width), BF16))
        out_specs = [whole(tokens), whole(6 * RANK)]
        out_shape = [jax.ShapeDtypeStruct((tokens, width), F32), jax.ShapeDtypeStruct((6 * RANK, width), BF16)]
    elif step.last:
        rest = keys - block_rows
        out_specs = [whole(block_rows), whole(rest), by_head, whole(4 * RANK)]
        out_shape = [
            jax.ShapeDtypeStruct((block_rows, width), F32),
            jax.ShapeDtypeStruct((rest, width), BF16),
            jax.ShapeDtypeStruct((tokens, width), BF16),
            jax.ShapeDtypeStruct((4 * RANK, width), BF16),
        ]
    else:
        out_specs = [whole(keys), dqt_spec, whole(4 * RANK)]
        out_shape = [
            jax.ShapeDtypeStruct((keys, width), BF16),
            jax.ShapeDtypeStruct((pairs, PAIR, tokens), F32),
            jax.ShapeDtypeStruct((4 * RANK, width), F32),
        ]
    return pl.pallas_call(
        functools.partial(back_step_kernel, step, len(xs)),
        grid_spec=pltpu.PrefetchScalarGridSpec(
            num_scalar_prefetch=1, grid=(pairs // PER,), in_specs=in_specs + step.w.specs(), out_specs=out_specs, scratch_shapes=scratch
        ),
        out_shape=out_shape,
        name=step.name,
        compiler_params=params(60),
        cost_estimate=cost(keys / 24),
    )(scalars, *args, *step.w.arrays)


ROWS = 64


def normalize_rows(u_ref, norm_ref, low_ref, std_ref):
    def body(rows):
        values = u_ref[rows, :]
        centered = values - jnp.mean(values, -1, keepdims=True)
        inv_std = lax.rsqrt(jnp.mean(centered * centered, -1, keepdims=True) + NORM_EPS)
        normed = centered * inv_std
        norm_ref[rows, :] = normed
        low_ref[rows, :] = normed.astype(BF16)
        std_ref[rows, :] = inv_std

    each(u_ref.shape[0], ROWS, body)


def normalize_back(grads, normed, inv_std):
    return inv_std * (grads - jnp.mean(grads, -1, keepdims=True) - normed * jnp.mean(grads * normed, -1, keepdims=True))


def mid_kernel(w, part, query, sc_ref, o_ref, x_ref, a_ref, b_ref, aq_ref, bq_ref, *refs):
    pieces, refs = refs[: len(w.arrays)], refs[len(w.arrays) :]
    if query:
        norm_ref, low_ref, std_ref, r_ref, q_ref, w_ref, u_ref, sems = refs
    else:
        norm_ref, low_ref, std_ref, r_ref, w_ref, u_ref, sems = refs
    width = x_ref.shape[1]
    first = w.bring(pieces, sc_ref[1], part, w_ref.at[0], sems.at[0])
    start_all(first)
    if query:
        second = w.bring(pieces, sc_ref[1], 2, w_ref.at[1], sems.at[1])
        start_all(second)
    o = o_ref[...]
    hidden = low_rank(o, a_ref[0, 0, 0])
    r_ref[:, :RANK] = hidden
    wait_all(first)

    def body(cols):
        u_ref[:, cols] = x_ref[:, cols].astype(F32) + nn(o, w_ref[0, :, cols]) + nn(hidden, b_ref[0, 0, 0, :, cols])

    each(width, COLS, body)
    normalize_rows(u_ref, norm_ref, low_ref, std_ref)
    if query:
        low = low_ref[...]
        hidden_q = low_rank(low, aq_ref[0, 0, 0])
        r_ref[:, RANK:] = hidden_q
        wait_all(second)
        project_into(q_ref, low, w_ref.at[1], hidden_q, lambda cols: bq_ref[0, 0, 0, :, cols])


def mid(name, scalars, outs, residual, part, proj, query, proj_down, proj_up, w):
    rows, width = outs.shape
    shapes = [
        jax.ShapeDtypeStruct((rows, width), F32),
        jax.ShapeDtypeStruct((rows, width), BF16),
        jax.ShapeDtypeStruct((rows, 1), F32),
        jax.ShapeDtypeStruct((rows, 2 * RANK if query else RANK), BF16),
    ]
    if query:
        shapes.append(jax.ShapeDtypeStruct((rows, width), BF16))
    spec, spec_q = adapter_spec(proj, 1, width), adapter_spec(3, 1, width)
    return pl.pallas_call(
        functools.partial(mid_kernel, w, part, query),
        grid_spec=pltpu.PrefetchScalarGridSpec(
            num_scalar_prefetch=1,
            grid=(1,),
            in_specs=[WHOLE, WHOLE, spec, spec, spec_q, spec_q, *w.specs()],
            out_specs=[WHOLE] * len(shapes),
            scratch_shapes=[pltpu.VMEM((2, width, width), BF16), pltpu.VMEM((rows, width), F32), w.sems(2)],
        ),
        out_shape=shapes,
        name=name,
        compiler_params=params(60),
        cost_estimate=cost(1),
    )(scalars, outs, residual, proj_down, proj_up, proj_down, proj_up, *w.arrays)


def gelu_kernel(w, sc_ref, x_ref, a_ref, b_ref, *refs):
    pieces, (g_ref, slope_ref, r_ref, w_ref, sems) = refs[: len(w.arrays)], refs[len(w.arrays) :]
    copies = w.bring(pieces, sc_ref[1], 0, w_ref, sems.at[0])
    start_all(copies)
    x = x_ref[...]
    hidden = low_rank(x, a_ref[0, 0])
    r_ref[...] = hidden
    wait_all(copies)

    def body(cols):
        pre = nn(x, w_ref[:, cols]) + nn(hidden, b_ref[0, 0, :, cols])
        phi = 0.5 * (1.0 + lax.erf(pre * 0.7071067811865476))
        g_ref[:, cols] = (pre * phi).astype(BF16)
        slope_ref[:, cols] = (phi + pre * jnp.exp(-0.5 * pre * pre) * 0.3989422804014327).astype(BF16)

    each(g_ref.shape[1], COLS, body)


def gelu_up(scalars, x, down, up, w):
    rows, width = x.shape
    wide = up.shape[3]
    return pl.pallas_call(
        functools.partial(gelu_kernel, w),
        grid_spec=pltpu.PrefetchScalarGridSpec(
            num_scalar_prefetch=1,
            grid=(1,),
            in_specs=[WHOLE, mlp_adapter_spec(width), mlp_adapter_spec(wide), *w.specs()],
            out_specs=[WHOLE] * 3,
            scratch_shapes=[pltpu.VMEM((width, wide), BF16), w.sems(1)],
        ),
        out_shape=[
            jax.ShapeDtypeStruct((rows, wide), BF16),
            jax.ShapeDtypeStruct((rows, wide), BF16),
            jax.ShapeDtypeStruct((rows, RANK), BF16),
        ],
        name="gelu_up",
        compiler_params=params(60),
        cost_estimate=cost(15),
    )(scalars, x, down, up, *w.arrays)


FC_ROWS = {"da1": 0, "db1": 16, "da2": 80, "db2": 144, "da_co": 160, "db_co": 176, "pick": 192}
FC_TOTAL = 208


def mlp_kernel(w_up, w_down, w_mid, sc_ref, g_ref, slope_ref, h2_ref, h2_low_ref, std2_ref, cot_ref, r1_ref, rco_ref, oc_ref,
               a1_ref, b1_ref, a2_ref, b2_ref, a7_ref, b7_ref, *refs):
    ups, refs = refs[: len(w_up.arrays)], refs[len(w_up.arrays) :]
    downs, refs = refs[: len(w_down.arrays)], refs[len(w_down.arrays) :]
    mids, refs = refs[: len(w_mid.arrays)], refs[len(w_mid.arrays) :]
    y_ref, d2_ref, doc_ref, gac_ref, grads_ref, w1, w2, wco, u, low, dpre, sem1, sem2, sem3 = refs
    rows, width = h2_ref.shape
    wide = g_ref.shape[1]
    own = sc_ref[1]
    copies2 = w_down.bring(downs, own, 0, w2, sem2.at[0])
    copies1 = w_up.bring(ups, own, 0, w1, sem1.at[0])
    copies3 = w_mid.bring(mids, own, 1, wco, sem3.at[0])
    start_all(copies2)
    start_all(copies1)
    start_all(copies3)
    g = g_ref[...]
    r2 = low_rank(g, a2_ref[0, 0])
    wait_all(copies2)

    def second(cols):
        u[:, cols] = h2_ref[:, cols] + nn(g_ref[...], w2[:, cols]) + nn(r2, b2_ref[0, 0, :, cols])

    each(width, COLS, second)

    def third(at):
        values = u[at, :]
        centered = values - jnp.mean(values, -1, keepdims=True)
        inv_std = lax.rsqrt(jnp.mean(centered * centered, -1, keepdims=True) + NORM_EPS)
        normed = centered * inv_std
        y_ref[at, :] = normed.astype(BF16)
        d3 = normalize_back(cot_ref[at, :].astype(F32), normed, inv_std)
        u[at, :] = d3
        low[at, :] = d3.astype(BF16)

    each(rows, ROWS, third)
    d3_low = low[...]
    grads_ref[pl.ds(FC_ROWS["db2"], RANK), :] = tn(r2, d3_low).astype(BF16)
    dr2 = low_rank(d3_low, b2_ref[0, 0])
    r1 = r1_ref[...]
    run = 2 * COLS
    runs = width // run

    def slopes(at, carry):
        cols = pl.ds(pl.multiple_of(at * run, run), run)
        down_rows = nt(low[...], w2[cols, :]) + nn(dr2, a2_ref[0, 0, :, cols])
        part = (down_rows * slope_ref[:, cols].astype(F32)).astype(BF16)
        dpre[:, cols] = part
        row = pl.multiple_of((at // runs) * RANK, RANK)
        place = pl.ds(pl.multiple_of((at % runs) * run, run), run)
        grads_ref[pl.ds(FC_ROWS["da2"] + row, RANK), place] = tn(dr2, g_ref[:, cols]).astype(BF16)
        grads_ref[pl.ds(FC_ROWS["db1"] + row, RANK), place] = tn(r1, part).astype(BF16)
        return carry

    lax.fori_loop(0, wide // run, slopes, 0)
    dr1 = low_rank(dpre[...], b1_ref[0, 0])
    grads_ref[pl.ds(FC_ROWS["da1"], RANK), :] = tn(dr1, h2_low_ref[...]).astype(BF16)
    wait_all(copies1)

    def first(cols):
        u[:, cols] += nt(dpre[...], w1[cols, :]) + nn(dr1, a1_ref[0, 0, :, cols])

    each(width, COLS, first)

    def norm(at):
        d2 = normalize_back(u[at, :], h2_ref[at, :], std2_ref[at, :])
        d2_ref[at, :] = d2
        low[at, :] = d2.astype(BF16)

    each(rows, ROWS, norm)
    wait_all(copies3)
    d2_low = low[...]
    grads_ref[pl.ds(FC_ROWS["db_co"], RANK), :] = tn(rco_ref[...], d2_low).astype(BF16)
    drc = low_rank(d2_low, b7_ref[0, 0, 0])
    grads_ref[pl.ds(FC_ROWS["da_co"], RANK), :] = tn(drc, oc_ref[...]).astype(BF16)

    def cross(cols):
        doc_ref[:, cols] = (nt(low[...], wco[cols, :]) + nn(drc, a7_ref[0, 0, 0, :, cols])).astype(BF16)

    each(width, COLS, cross)
    slope_rows(gac_ref, doc_ref, oc_ref)
    mine = jnp.where(sc_ref[0] == 0, sc_ref[2], 0).astype(F32)
    grads_ref[pl.ds(FC_ROWS["pick"], 16), :] = jnp.full((16, width), mine, F32).astype(BF16)


def mlp(scalars, g, slope, h2, h2_low, std2, cot, r1, rco, oc, fc1_down, fc1_up, fc2_down, fc2_up, proj_down, proj_up, w_up, w_down, w_mid):
    rows, width = h2.shape
    wide = g.shape[1]
    return pl.pallas_call(
        functools.partial(mlp_kernel, w_up, w_down, w_mid),
        grid_spec=pltpu.PrefetchScalarGridSpec(
            num_scalar_prefetch=1,
            grid=(1,),
            in_specs=[
                *[WHOLE] * 9,
                mlp_adapter_spec(width),
                mlp_adapter_spec(wide),
                mlp_adapter_spec(wide),
                mlp_adapter_spec(width),
                adapter_spec(7, 1, width),
                adapter_spec(7, 1, width),
                *w_up.specs(),
                *w_down.specs(),
                *w_mid.specs(),
            ],
            out_specs=[WHOLE] * 5,
            scratch_shapes=[
                pltpu.VMEM((width, wide), BF16),
                pltpu.VMEM((wide, width), BF16),
                pltpu.VMEM((width, width), BF16),
                pltpu.VMEM((rows, width), F32),
                pltpu.VMEM((rows, width), BF16),
                pltpu.VMEM((rows, wide), BF16),
                w_up.sems(1),
                w_down.sems(1),
                w_mid.sems(1),
            ],
        ),
        out_shape=[
            jax.ShapeDtypeStruct((rows, width), BF16),
            jax.ShapeDtypeStruct((rows, width), F32),
            jax.ShapeDtypeStruct((rows, width), BF16),
            jax.ShapeDtypeStruct((width // PAIR, PAIR + AUG, 2 * rows), BF16),
            jax.ShapeDtypeStruct((FC_TOTAL, width), BF16),
        ],
        name="mlp",
        compiler_params=params(60),
        cost_estimate=cost(33),
    )(scalars, g, slope, h2, h2_low, std2, cot, r1, rco, oc, fc1_down, fc1_up, fc2_down, fc2_up, proj_down, proj_up,
      *w_up.arrays, *w_down.arrays, *w_mid.arrays)


def mid_back_kernel(w, sc_ref, dqc_ref, d2_ref, h1_ref, h1_low_ref, std1_ref, r_ref, o_ref, aq_ref, bq_ref, a_ref, b_ref, *refs):
    pieces, refs = refs[: len(w.arrays)], refs[len(w.arrays) :]
    d1_ref, do_ref, ga_ref, grads_ref, w_ref, low, sems = refs
    rows, width = d2_ref.shape
    first = w.bring(pieces, sc_ref[1], 2, w_ref.at[1], sems.at[1])
    second = w.bring(pieces, sc_ref[1], 0, w_ref.at[0], sems.at[0])
    start_all(first)
    start_all(second)
    dqc = dqc_ref[...]
    drq = low_rank(dqc, bq_ref[0, 0, 0])
    grads_ref[0:RANK, :] = tn(drq, h1_low_ref[...]).astype(BF16)
    grads_ref[2 * RANK : 3 * RANK, :] = tn(r_ref[:, RANK:], dqc).astype(BF16)
    wait_all(first)

    def query(cols):
        d1_ref[:, cols] = d2_ref[:, cols] + nt(dqc_ref[...], w_ref[1, cols, :]) + nn(drq, aq_ref[0, 0, 0, :, cols])

    each(width, COLS, query)

    def norm(at):
        d1 = normalize_back(d1_ref[at, :], h1_ref[at, :], std1_ref[at, :])
        d1_ref[at, :] = d1
        low[at, :] = d1.astype(BF16)

    each(rows, ROWS, norm)
    wait_all(second)
    d1_low = low[...]
    dr = low_rank(d1_low, b_ref[0, 0, 0])
    grads_ref[RANK : 2 * RANK, :] = tn(dr, o_ref[...]).astype(BF16)
    grads_ref[3 * RANK :, :] = tn(r_ref[:, :RANK], d1_low).astype(BF16)

    def out(cols):
        do_ref[:, cols] = (nt(low[...], w_ref[0, cols, :]) + nn(dr, a_ref[0, 0, 0, :, cols])).astype(BF16)

    each(width, COLS, out)

    slope_rows(ga_ref, do_ref, o_ref)


def mid_back(scalars, dqc, d2, h1, h1_low, std1, r, o, proj_down, proj_up, w):
    rows, width = d2.shape
    spec, spec_q = adapter_spec(6, 1, width), adapter_spec(3, 1, width)
    return pl.pallas_call(
        functools.partial(mid_back_kernel, w),
        grid_spec=pltpu.PrefetchScalarGridSpec(
            num_scalar_prefetch=1,
            grid=(1,),
            in_specs=[*[WHOLE] * 7, spec_q, spec_q, spec, spec, *w.specs()],
            out_specs=[WHOLE] * 4,
            scratch_shapes=[pltpu.VMEM((2, width, width), BF16), pltpu.VMEM((rows, width), BF16), w.sems(2)],
        ),
        out_shape=[
            jax.ShapeDtypeStruct((rows, width), F32),
            jax.ShapeDtypeStruct((rows, width), BF16),
            jax.ShapeDtypeStruct((width // PAIR, PAIR + AUG, 2 * rows), BF16),
            jax.ShapeDtypeStruct((4 * RANK, width), BF16),
        ],
        name="mid_back",
        compiler_params=params(60),
        cost_estimate=cost(1),
    )(scalars, dqc, d2, h1, h1_low, std1, r, o, proj_down, proj_up, proj_down, proj_up, *w.arrays)


def add_picked(picks_ref, sequences, out, source):
    adapters, view = out
    for adapter in range(adapters):
        view(adapter)[...] = jnp.zeros(view(adapter).shape, F32)
    for at in range(sequences):
        target = view(picks_ref[at])
        target[...] += source(at).astype(F32)


def fc_total_kernel(picks_ref, g_ref, a1_ref, b1_ref, a2_ref, b2_ref):
    sequences, _, width = g_ref.shape
    adapters = a1_ref.shape[1]

    def put(out_ref, col, row):
        def view(adapter):
            return out_ref.at[0, adapter, :, pl.ds(col, width)]

        add_picked(picks_ref, sequences, (adapters, view), lambda at: g_ref[at, pl.ds(row, RANK), :])

    for out_ref, name in ((a1_ref, "da1"), (b1_ref, "db1"), (a2_ref, "da2"), (b2_ref, "db2")):
        for at in range(out_ref.shape[3] // width):
            put(out_ref, at * width, FC_ROWS[name] + at * RANK)


def fc_total(picks, gathered, shapes):
    return pl.pallas_call(
        fc_total_kernel,
        grid_spec=pltpu.PrefetchScalarGridSpec(
            num_scalar_prefetch=1, grid=(1,), in_specs=[WHOLE], out_specs=[WHOLE] * 4
        ),
        out_shape=[jax.ShapeDtypeStruct(s, F32) for s in shapes],
        name="fc_total",
        compiler_params=params(60),
        cost_estimate=cost(6),
    )(picks, gathered)


PROJ_ROWS = {
    0: (2, 0, 48),
    1: (2, 16, 64),
    2: (2, 32, 80),
    3: (1, 0, 32),
    4: (1, 64, 96),
    5: (1, 80, 112),
    6: (1, 16, 48),
    7: (0, FC_ROWS["da_co"], FC_ROWS["db_co"]),
}


def proj_total_kernel(projs, first_source, count, sources, picks_ref, *refs):
    g_refs, (down_ref, up_ref) = refs[:sources], refs[-2:]
    adapters = down_ref.shape[2]
    for at, proj in enumerate(projs):
        source, down_row, up_row = PROJ_ROWS[proj]
        g_ref = g_refs[source - first_source]

        @pl.when(pl.program_id(0) == at)
        def _(g_ref=g_ref, down_row=down_row, up_row=up_row):
            for out_ref, row in ((down_ref, down_row), (up_ref, up_row)):
                add_picked(
                    picks_ref, g_ref.shape[0], (adapters, lambda adapter, out_ref=out_ref: out_ref.at[0, 0, adapter]),
                    lambda at, row=row: g_ref[at, pl.ds(row, RANK), :],
                )


def proj_total(picks, gathered, projs, so_far, shape):
    first = projs[0]
    block = pl.BlockSpec((1, 1, *shape[2:]), lambda p, s: (0, p + first, 0, 0, 0))
    rest = [] if so_far is None else list(so_far)
    first_source = min(PROJ_ROWS[proj][0] for proj in projs)
    return pl.pallas_call(
        functools.partial(proj_total_kernel, tuple(projs), first_source, len(rest), len(gathered)),
        grid_spec=pltpu.PrefetchScalarGridSpec(
            num_scalar_prefetch=1,
            grid=(len(projs),),
            in_specs=[WHOLE] * len(gathered) + [ANY] * len(rest),
            out_specs=[block] * 2,
        ),
        out_shape=[jax.ShapeDtypeStruct(shape, F32)] * 2,
        input_output_aliases={1 + len(gathered) + at: at for at in range(len(rest))},
        name=f"proj_total_{first}",
        compiler_params=params(60),
        cost_estimate=cost(1.4 * len(projs)),
    )(picks, *gathered, *rest)


class Gathering:
    def __init__(self, shard, parts, across, sibling, together):
        self.shard, self.parts, self.across, self.sibling, self.together = shard, parts, across, sibling, together
        self.half = shard.shape[0] // 2

    def begin(self):
        self.x, self.y = self.across(self.shard, 1), self.across(self.shard, 2)
        self.own = self.sibling(self.shard)

    def forward(self):
        self.xy, self.yx = self.across(self.x[: self.half], 2), self.across(self.y[self.half :], 1)
        if self.together:
            self.near = [self.sibling(jnp.concatenate([self.x, self.y], axis=0))]
        else:
            self.near = [self.sibling(self.x), self.sibling(self.y)]

    def share(self):
        self.far = self.sibling(jnp.concatenate([self.xy, self.yx], axis=0))

    def result(self):
        rows, half = self.shard.shape[0], self.half
        arrays = [self.shard, self.own, self.x, self.y, *self.near, self.xy, self.yx, self.far]
        layout = [[(0, True, who, 0, rows)] for who in (0, 1, 2, 4)]
        if self.together:
            layout += [[(0, True, 3, 0, rows), (rows, True, 5, 0, rows)]]
        else:
            layout += [[(0, True, 3, 0, rows)], [(0, True, 5, 0, rows)]]
        layout += [[(0, True, 6, 0, half)], [(0, True, 6, half, rows - half)]]
        layout += [[(0, True, 7, 0, half), (half, True, 7, half, rows - half)]]
        return Gathered(arrays, layout, rows // self.parts)


class Whole:
    def __init__(self, shard, parts, shards, gather):
        self.shard, self.parts, self.shards, self.gather = shard, parts, shards, gather
        self.x = self.y = self.own = self.xy = self.yx = shard
        self.near = []

    def begin(self):
        self.whole = self.gather(self.shard)

    def forward(self):
        pass

    def share(self):
        pass

    def result(self):
        rows = self.shard.shape[0]
        return Gathered([self.whole], [[(at * rows, False, at, 0, rows) for at in range(self.shards)]], rows // self.parts)


def make_shards(mesh):
    chips, span = mesh.shape["chip"], mesh.shape["sp"]
    plane = ("chip", "core")

    def tie(*values):
        return lax.optimization_barrier(values)

    def turn(values, by):
        return lax.ppermute(values, "sp", [(i, (i + by) % span) for i in range(span)])

    def swap(values, bit):
        return lax.ppermute(values, "sp", [(i, i ^ bit) for i in range(span)])

    def across(values, bit):
        return lax.ppermute(values, "chip", [(i, i ^ bit) for i in range(chips)])

    def sibling(values):
        return lax.ppermute(values, "core", [(0, 1), (1, 0)])

    def gathering(shard, parts, steps, together=False):
        if chips == 4 and steps:
            return Gathering(shard, parts, across, sibling, together)
        return Whole(shard, parts, 2 * chips, lambda v: lax.all_gather(v, plane, axis=0, tiled=True))

    def shards(
        inputs,
        segments,
        enc_states,
        adapter_pick,
        qkv_weights,
        out_weights,
        mlp_in,
        mlp_out,
        proj_down,
        proj_up,
        fc1_down,
        fc1_up,
        fc2_down,
        fc2_up,
        cotangent,
    ):
        x_low = inputs[0]
        memory = enc_states[0]
        tokens, width = x_low.shape
        mem_rows = memory.shape[0]
        own = lax.axis_index("chip") * 2 + lax.axis_index("core")
        scalars = jnp.stack([lax.axis_index("sp"), own, adapter_pick[0]]).astype(jnp.int32)
        tables = (proj_down, proj_up)

        a = gathering(qkv_weights[0, :3].reshape(-1, width), 3, True)
        b_shard = jnp.concatenate([out_weights[0].reshape(-1, width), qkv_weights[0, 3:].reshape(-1, width)], axis=0)
        b = gathering(b_shard, 5, True, True)
        c, d = gathering(mlp_in[0], 1, False), gathering(mlp_out[0], 1, True, True)

        seg_row = jnp.pad(segments.astype(BF16), ((0, 15), (0, width - tokens)))
        ext = [jnp.concatenate([x_low, seg_row], axis=0)]
        lane = jnp.arange(AUG, dtype=jnp.int32)
        kinds = (lane >= TERMS) & (lane < TERMS + SEG_KINDS)
        q_seg = (kinds[:, None] & (lane[:, None] - TERMS == segments)).astype(F32)
        free_seg = jnp.zeros((AUG, tokens), F32)

        def key_aug(block):
            seg = block[tokens, :tokens].astype(jnp.int32)
            return jnp.where(lane[None] < TERMS, 1.0, jnp.where(kinds[None] & (lane[None] - TERMS != seg[:, None]), FAR, 0.0)).astype(BF16)

        free_aug = jnp.broadcast_to((lane[None] < TERMS).astype(BF16), (span * mem_rows, AUG))

        a.begin()
        ext.append(turn(ext[0], 1))
        a.x, a.y, a.own, ext[1] = tie(a.x, a.y, a.own, ext[1])
        a.forward()
        ext.append(turn(ext[1], 1))
        a.xy, a.yx, b.shard, ext[2], *a.near = tie(a.xy, a.yx, b.shard, ext[2], *a.near)
        a.share()
        b.begin()
        while len(ext) < span:
            ext.append(turn(ext[-1], 1))
        w_a = a.result()

        state, ks, vs, rs, augs = None, [], [], [], []
        q = o = None
        for at in range(0, span, 2):
            step = Step(f"self_{at}", w_a, (0, 1, 2) if at == 0 else (1, 2), (at, at + 1), at == 0, at == span - 2, True)
            if at:
                ext[at], ext[at + 1], state[1] = tie(ext[at], ext[at + 1], state[1])
            augs += [key_aug(ext[at]), key_aug(ext[at + 1])]
            q, k, v, r, out = attend_step(step, scalars, [[ext[at]], [ext[at + 1]]], tokens, tokens, tables, augs[at:], q, q_seg, state)
            ks, vs, rs = ks + k, vs + v, rs + r
            if at < span - 2:
                state = out if at == 0 else [state[0], *out]
            else:
                o, qa = out
            if at == 0:
                state[1], b.x, b.y, b.own, ext[-1], on, c.shard = tie(state[1], b.x, b.y, b.own, ext[-1], memory, c.shard)
                b.forward()
                c.begin()
                mems = [memory, turn(on, 1), *[None] * (span - 3), turn(on, -1)]
        o, mems[1], mems[-1], b.xy, b.yx, *b.near = tie(o, mems[1], mems[-1], b.xy, b.yx, *b.near)
        b.share()
        for by in range(2, span - 1):
            mems[by] = turn(mems[by - 1], 1)
        w_b = b.result()
        h1, h1_low, std1, r_mid, qc = mid("mid", scalars, o, x_low, 0, 6, True, *tables, w_b)
        qc, d.shard, *mems[1:] = tie(qc, d.shard, *mems[1:])
        d.begin()
        step = Step("cross", w_b, (3, 4), (0,), True, True, False)
        _, (kc,), (vc,), (r_mem,), (oc, qca) = attend_step(step, scalars, [mems], tokens, mem_rows, tables, [free_aug], qc, free_seg, None)
        oc, d.x, d.y, d.own = tie(oc, d.x, d.y, d.own)
        d.forward()
        h2, h2_low, std2, r_co = mid("mid_cross", scalars, oc, h1, 1, 7, False, *tables, w_b)
        w_c = c.result()
        g, slope, r_fc1 = gelu_up(scalars, h2_low, fc1_down, fc1_up, w_c)
        g, d.xy, d.yx, *d.near = tie(g, d.xy, d.yx, *d.near)
        d.share()
        w_d = d.result()
        y, d2, doc, gac, fc_grads = mlp(
            scalars, g, slope, h2, h2_low, std2, cotangent[0], r_fc1, r_co, oc,
            fc1_down, fc1_up, fc2_down, fc2_up, *tables, w_c, w_d, w_b,
        )
        g0 = lax.psum(fc_grads, "sp")

        step = Step("cross_back", w_b, (3, 4), (0,), True, True, False)
        dmem, parts, dqc, cross_grads = back_step(step, scalars, qca, gac, qc, doc, kc, vc, free_aug, r_mem, mems, mem_rows, tables, None, None)

        def mem_part(slot):
            return parts[(slot - 1) * mem_rows : slot * mem_rows]

        def added(slot, arrived):
            return (mem_part(slot).astype(F32) + arrived.astype(F32)).astype(BF16)

        middle = span // 2
        lower, upper = turn(mem_part(middle), -1), turn(mem_part(middle + 1), 1)
        d1, do, ga, mid_grads = mid_back(scalars, dqc, d2, h1, h1_low, std1, r_mid, o, *tables, w_b)
        g0, g1 = tie(g0, jnp.concatenate([mid_grads, cross_grads], axis=0))
        g1 = lax.psum(g1, "sp")
        g0 = g0[None]

        def doubled(values, bit):
            return jnp.concatenate([values, across(values, bit)], axis=0)

        bits = [1 << at for at in range(chips.bit_length() - 1)]
        state, moving, at_bit = None, None, 0
        for at in reversed(range(span)):
            step = Step(f"self_back_{at}", w_a, (0, 1, 2) if at == 0 else (1, 2), (at,), at == span - 1, at == 0, True)
            out = back_step(step, scalars, qa, ga, q, do, ks[at], vs[at], augs[at], rs[at], [ext[at]], tokens, tables, state, d1)
            if at == 0:
                dx, g2 = out
                dx, g2, moving, g0, g1 = tie(dx, g2, moving, g0, g1)
                dx = dx + moving.astype(F32)
            else:
                part, *state = out
                if at == span - 1:
                    part, state[0], lower, upper = tie(part, state[0], lower, upper)
                    for slot in range(middle - 1, 1, -1):
                        lower = turn(added(slot, lower), -1)
                    for slot in range(middle + 2, span):
                        upper = turn(added(slot, upper), 1)
                    lower = added(1, lower)
                else:
                    part, state[0], moving, g0, *on = tie(part, state[0], moving, g0, *([g1] if at == 1 else []))
                    part = (part.astype(F32) + moving.astype(F32)).astype(BF16)
                    part, state[0] = tie(part, state[0])
                moving = turn(part, -1)
                if at_bit < len(bits):
                    g0 = doubled(g0, bits[at_bit])
                    at_bit += 1
                if at == 1:
                    while at_bit < len(bits):
                        g0 = doubled(g0, bits[at_bit])
                        at_bit += 1
                    g1 = doubled(on[0][None], bits[0])
        g0 = jnp.concatenate([g0, sibling(g0)], axis=0)
        g2 = (g2.astype(F32) + swap(g2, 1).astype(F32)).astype(BF16)
        g2, g1, g0 = tie(g2, g1, g0)
        for bit in bits[1:]:
            g1 = doubled(g1, bit)
        picks = g0[:, FC_ROWS["pick"], 0].astype(jnp.int32)
        fcs = fc_total(picks, g0, (fc1_down.shape, fc1_up.shape, fc2_down.shape, fc2_up.shape))
        bit = 2
        while bit < span:
            g2 = (g2.astype(F32) + swap(g2, bit).astype(F32)).astype(BF16)
            bit *= 2
        g2, g1, lower, picks, *fcs = tie(g2, g1, lower, picks, *fcs)
        lower = turn(lower, -1)
        g1 = jnp.concatenate([g1, sibling(g1)], axis=0)
        g2 = doubled(g2[None], bits[0])
        g2, g1, picks = tie(g2, g1, picks)
        projs = proj_total(picks, (g0, g1), range(3, 8), None, proj_down.shape)
        for bit in bits[1:]:
            g2 = doubled(g2, bit)
        g2, *projs = tie(g2, *projs)
        g2 = jnp.concatenate([g2, sibling(g2)], axis=0)
        projs = proj_total(picks, (g2,), range(3), projs, proj_down.shape)
        dmem = dmem + lower.astype(F32) + upper.astype(F32)
        return (y[None], dx[None], dmem[None], *projs, *fcs)

    return shards


def solution(mesh):
    count = mesh.shape["fsdp"]
    fine = Mesh(mesh.devices.reshape(count // 2, 2, mesh.shape["sp"]), ("chip", "core", "sp"))
    fsdp = ("chip", "core")
    row = P(fsdp, "sp", None)
    return jax.shard_map(
        make_shards(fine),
        mesh=fine,
        in_specs=(
            row,
            P(fsdp, "sp"),
            row,
            P(fsdp),
            P(None, None, fsdp, None),
            P(None, None, fsdp, None),
            P(None, fsdp, None),
            P(None, fsdp, None),
            P(),
            P(),
            P(),
            P(),
            P(),
            P(),
            row,
        ),
        out_specs=(row, row, row, P(), P(), P(), P(), P(), P()),
        check_vma=False,
    )
```

```python
import functools

import jax
import jax.numpy as jnp
from jax import lax
from jax.experimental import pallas as pl
from jax.experimental.pallas import tpu as pltpu
from jax.sharding import Mesh
from jax.sharding import PartitionSpec as P

HEAD = 64
PAIR = 2 * HEAD
RANK = 16
AUG = 16
TERMS = 3
SEG_KINDS = 5
COLS = 256
NORM_EPS = 1e-05
FAR = -1e30
SCALE = HEAD**-0.5
F32 = jnp.float32
BF16 = jnp.bfloat16
ANY = pl.BlockSpec(memory_space=pltpu.HBM)
WHOLE = pl.BlockSpec(memory_space=pltpu.VMEM)


def dot(left, right, left_dim, right_dim):
    return lax.dot_general(left, right, (((left_dim,), (right_dim,)), ((), ())), preferred_element_type=F32)


def nn(left, right):
    return dot(left, right, 1, 0)


def nt(left, right):
    return dot(left, right, 1, 1)


def tn(left, right):
    return dot(left, right, 0, 0)


def params(mib):
    return pltpu.CompilerParams(vmem_limit_bytes=mib * 1024 * 1024)


def cost(us):
    return pl.CostEstimate(flops=int(us * 1.15e9), bytes_accessed=0, transcendentals=0)


def each(total, size, body, unroll=4):
    def step(at, carry):
        body(pl.ds(pl.multiple_of(at * size, size), size))
        return carry

    lax.fori_loop(0, total // size, step, 0, unroll=min(unroll, total // size))


def fetch(refs, layout, own, rows, part, target, sems):
    copies = []
    for ref, entries in zip(refs, layout):
        for source, flip, who, first, count in entries:
            low, high = max(first, part * rows), min(first + count, (part + 1) * rows)
            if low < high:
                shard = own ^ who if flip else who
                copies.append(
                    pltpu.make_async_copy(
                        ref.at[pl.ds(source + low - first, high - low)],
                        target.at[pl.ds(pl.multiple_of(shard * rows + (low - part * rows), 16), high - low)],
                        sems.at[len(copies)],
                    )
                )
    return copies


def start_all(copies):
    for copy in copies:
        copy.start()


def wait_all(copies):
    for copy in copies:
        copy.wait()


def low_half(shape, axis):
    return lax.broadcasted_iota(jnp.int32, shape, axis) < HEAD


def split_pair(rows):
    low = low_half(rows.shape, 1)
    zero = jnp.zeros_like(rows)
    return jnp.concatenate([jnp.where(low, rows, zero), jnp.where(low, zero, rows)], axis=0)


def split_pair_t(cols):
    low = low_half(cols.shape, 0)
    zero = jnp.zeros_like(cols)
    return jnp.concatenate([jnp.where(low, cols, zero), jnp.where(low, zero, cols)], axis=1)


def join_pair_t(cols):
    half = cols.shape[1] // 2
    return jnp.where(low_half((PAIR, half), 0), cols[:, :half], cols[:, half:])


def turned(rows):
    return rows.astype(F32).T


def term_rows(row, rest):
    high = row.astype(BF16).astype(F32)
    mid = (row - high).astype(BF16).astype(F32)
    low = row - high - mid
    at = lax.broadcasted_iota(jnp.int32, rest.shape, 0)
    return jnp.where(at == 0, high, jnp.where(at == 1, mid, jnp.where(at == 2, low, rest))).astype(BF16)


def causal_scores(scores):
    keys, columns = scores.shape
    row = lax.broadcasted_iota(jnp.int32, (keys, columns // 2), 0)
    col = lax.broadcasted_iota(jnp.int32, (keys, columns // 2), 1)
    keep = row <= col
    return jnp.where(jnp.concatenate([keep, keep], axis=1), scores, FAR)


def out_slopes(grads, outs):
    gt = turned(grads)
    products = gt * turned(outs)
    delta = jnp.concatenate([jnp.sum(products[:HEAD], axis=0, keepdims=True), jnp.sum(products[HEAD:], axis=0, keepdims=True)], axis=1)
    rest = jnp.zeros((AUG, delta.shape[1]), F32)
    return jnp.concatenate([split_pair_t(gt.astype(BF16)), term_rows(-delta, rest)], axis=0)


def block_back(keys, values, kaug, qa, ga, q, grads, diagonal):
    scores = nn(jnp.concatenate([keys, kaug], axis=1), qa)
    if diagonal:
        scores = causal_scores(scores)
    chances = jnp.exp(scores)
    slopes = nn(jnp.concatenate([values, kaug], axis=1), ga)
    low_slopes = (chances * slopes).astype(BF16)
    grad_values = nn(chances.astype(BF16), grads).astype(BF16)
    grad_keys = nn(low_slopes, q).astype(BF16)
    grad_q = join_pair_t(nn(turned(keys).astype(BF16), low_slopes))
    return grad_q, grad_keys, grad_values


def slope_rows(ga_ref, do_ref, o_ref):
    for at in range(ga_ref.shape[0]):
        cols = slice(at * PAIR, (at + 1) * PAIR)
        ga_ref[at] = out_slopes(do_ref[:, cols], o_ref[:, cols])


def adapter_spec(first, count, width):
    return pl.BlockSpec((1, count, 1, RANK, width), lambda *at: (0, first // count, at[-1][2], 0, 0))


def mlp_adapter_spec(width):
    return pl.BlockSpec((1, 1, RANK, width), lambda *at: (0, at[-1][2], 0, 0))


def low_rank(rows, table):
    return nt(rows, table).astype(BF16)


class Gathered:
    def __init__(self, arrays, layout, rows):
        self.arrays, self.layout, self.rows = arrays, layout, rows
        self.count = sum(len(entries) for entries in layout)

    def bring(self, refs, own, part, target, sems):
        return fetch(refs, self.layout, own, self.rows, part, target, sems)

    def specs(self):
        return [ANY] * len(self.arrays)

    def sems(self, parts):
        return pltpu.SemaphoreType.DMA((parts, self.count))


def project_into(out_ref, rows, weight, hidden, up):
    def body(cols):
        out_ref[:, cols] = (nn(rows, weight[:, cols]) + nn(hidden, up(cols))).astype(out_ref.dtype)

    each(out_ref.shape[1], COLS, body)


class Gathered:
    def __init__(self, arrays, layout, rows):
        self.arrays, self.layout, self.rows = arrays, layout, rows
        self.count = sum(len(entries) for entries in layout)

    def bring(self, refs, own, part, target, sems):
        return fetch(refs, self.layout, own, self.rows, part, target, sems)

    def specs(self):
        return [ANY] * len(self.arrays)

    def groups(self):
        groups, at = {}, 0
        for entries in self.layout:
            for _, flip, who, _, _ in entries:
                groups.setdefault((flip, who), []).append(at)
                at += 1
        return groups.items()

    def sems(self, parts):
        return pltpu.SemaphoreType.DMA((parts, self.count))


def project_into(out_ref, rows, weight, hidden, up):
    def body(cols):
        out_ref[:, cols] = (nn(rows, weight[:, cols]) + nn(hidden, up(cols))).astype(out_ref.dtype)

    each(out_ref.shape[1], COLS, body)


PER = 2


class Step:
    def __init__(self, name, w, parts, blocks, first, last, causal):
        self.name, self.w, self.parts, self.blocks, self.first, self.last, self.causal = name, w, parts, blocks, first, last, causal

    def on(self, sc_ref, at, condition=None):
        conditions = [] if condition is None else [condition]
        if self.causal and at:
            conditions.append(sc_ref[0] >= at)
        if not conditions:
            return lambda body: body()
        return pl.when(conditions[0] if len(conditions) == 1 else conditions[0] & conditions[1])


def head_cols(pair):
    return pl.ds(pl.multiple_of((pl.program_id(0) * PER + pair) * PAIR, PAIR), PAIR)


def pair_cols(pair):
    return slice(pair * PAIR, (pair + 1) * PAIR)


def key_rows(seg_ref, keys):
    at = lax.broadcasted_iota(jnp.int32, (AUG, keys), 0)
    if seg_ref is None:
        return jnp.where(at < TERMS, 1.0, 0.0)
    other = (at.astype(F32) - TERMS != seg_ref[0:1, :keys].astype(F32)) & (at < TERMS + SEG_KINDS)
    return jnp.where(at < TERMS, 1.0, jnp.where(other, FAR, 0.0))


def query_rows(seg_ref, queries):
    at = lax.broadcasted_iota(jnp.int32, (AUG, queries), 0)
    if seg_ref is None:
        return jnp.zeros((AUG, queries), F32)
    same = (at.astype(F32) - TERMS == seg_ref[0:1, :queries].astype(F32)) & (at >= TERMS) & (at < TERMS + SEG_KINDS)
    return jnp.where(same, 1.0, 0.0)


def attend_step_kernel(step, counts, sc_ref, *refs):
    refs = list(refs)
    make_q = step.causal and step.first

    def take(number):
        return [refs.pop(0) for _ in range(number)]

    groups = len(counts)
    xs = [take(count) for count in counts]
    segs = take(groups) if step.causal else [None] * groups
    a_ref, b_ref = take(2)
    q_ref = take(1)[0] if step.first and not make_q else None
    qa_in, acc_in, m_in = (None, None, None) if step.first else take(3)
    pieces = take(len(step.w.arrays))
    q_out = take(1)[0] if make_q else None
    k_outs, v_outs, r_outs, kaugs = take(groups), take(groups), take(groups), take(groups)
    qa_out, o_out = None, None
    if step.first and not step.last:
        qa_out = take(1)[0]
    if step.last:
        o_out, qa_out, w_ref, sems = take(4)
    else:
        acc_ref, m_ref, w_ref, sems = take(4)
    k_alls, v_alls = take(groups), take(groups)
    if step.last:
        acc_ref, m_ref = take(2)
    q_all = take(1)[0] if make_q else None
    parts = step.parts

    def copies(at):
        return step.w.bring(pieces, sc_ref[1], parts[at], w_ref.at[at], sems.at[at])

    for group, at in enumerate(step.blocks):

        @step.on(sc_ref, at, pl.program_id(0) == 0)
        def _(group=group):
            if group == 0:
                for slot in range(len(parts)):
                    start_all(copies(slot))
            kaugs[group][...] = key_rows(segs[group], kaugs[group].shape[0]).T.astype(BF16)
            low = 0
            tables = a_ref[...].reshape(-1, a_ref.shape[-1])
            for x_ref in xs[group]:
                x = x_ref[...]
                span = pl.ds(low, x.shape[0])
                low += x.shape[0]
                hidden = low_rank(x, tables)
                r_outs[group][span, :] = hidden
                outs = [k_alls[group], v_alls[group]]
                if make_q and group == 0:
                    outs.insert(0, q_all)
                for number, out in enumerate(outs):
                    place = number + len(parts) - len(outs)
                    slot = number + a_ref.shape[1] - len(outs)
                    own = hidden[:, slot * RANK : (slot + 1) * RANK]
                    if group == 0 and x_ref is xs[0][0]:
                        wait_all(copies(place))

                    def body(cols, place=place, slot=slot, own=own, out=out):
                        out[span, cols] = (nn(x, w_ref[place, :, cols]) + nn(own, b_ref[0, slot, 0, :, cols])).astype(BF16)

                    each(out.shape[1], COLS, body)

    qas = []
    for pair in range(PER):
        if step.first:
            q = q_all[:, head_cols(pair)] if make_q else q_ref[:, pair_cols(pair)]
            if make_q:
                q_out[:, pair_cols(pair)] = q
            seg = query_rows(segs[0], q.shape[0])
            qt = split_pair_t((turned(q) * SCALE).astype(BF16))
            qas.append(jnp.concatenate([qt, jnp.concatenate([seg, seg], axis=1).astype(BF16)], axis=0))
            if not step.last:
                qa_out[pair] = qas[pair]
        else:
            qas.append(qa_in[pair])

    def block(group, at, opens):
        for pair in range(PER):
            keys, values = k_alls[group][:, head_cols(pair)], v_alls[group][:, head_cols(pair)]
            k_outs[group][:, pair_cols(pair)] = keys
            v_outs[group][:, pair_cols(pair)] = values
            scores = nn(jnp.concatenate([keys, kaugs[group][...]], axis=1), qas[pair])
            if step.causal and at == 0:
                scores = causal_scores(scores)
            top = jnp.max(scores, axis=0, keepdims=True)
            vt = jnp.concatenate([turned(values).astype(BF16), jnp.ones((16, keys.shape[0]), BF16)], axis=0)
            if opens and step.first:
                acc_ref[pair] = nn(vt, jnp.exp(scores - top).astype(BF16))
            else:
                old = m_in[pair, 0:1] if opens else m_ref[pair, 0:1]
                so_far = acc_in[pair] if opens else acc_ref[pair]
                top = jnp.maximum(old, top)
                acc_ref[pair] = so_far * jnp.exp(old - top) + nn(vt, jnp.exp(scores - top).astype(BF16))
            m_ref[pair] = jnp.broadcast_to(top, m_ref.shape[1:])

    for group, at in enumerate(step.blocks):
        step.on(sc_ref, at)(functools.partial(block, group, at, group == 0))
    if step.causal and step.blocks[0]:

        @pl.when(sc_ref[0] < step.blocks[0])
        def _():
            acc_ref[...] = acc_in[...]
            m_ref[...] = m_in[...]

    if step.last:
        for pair in range(PER):
            total = acc_ref[pair, PAIR : PAIR + 1]
            o_out[:, pair_cols(pair)] = join_pair_t(acc_ref[pair, :PAIR] / total).T.astype(BF16)
            lse = m_ref[pair, 0:1] + jnp.log(total)
            qa_out[pair] = jnp.concatenate([qas[pair][:PAIR], term_rows(-lse, qas[pair][PAIR:].astype(F32))], axis=0)


def attend_step(step, scalars, xs, tokens, block_rows, tables, q, state):
    width = xs[0][0].shape[1]
    pairs = width // PAIR
    keys = [block_rows * len(group) for group in xs]
    make_q = step.causal and step.first
    kinds = len(step.parts)
    slots = 3 if step.causal else 2
    by_head = pl.BlockSpec((tokens, PER * PAIR), lambda h, s: (0, h))
    extended = pl.BlockSpec((PER, PAIR + AUG, 2 * tokens), lambda h, s: (h, 0, 0))
    m_spec = pl.BlockSpec((PER, 8, 2 * tokens), lambda h, s: (h, 0, 0))
    adapters = adapter_spec(0 if step.causal else 4, slots, width)
    q_shape = jax.ShapeDtypeStruct((tokens, width), BF16)
    qa_shape = jax.ShapeDtypeStruct((pairs, PAIR + AUG, 2 * tokens), BF16)
    in_specs = [pl.BlockSpec((block_rows, width), lambda h, s: (0, 0))] * sum(len(group) for group in xs)
    args = [x for group in xs for x in group]
    if step.causal:
        in_specs += [pl.BlockSpec((16, width), lambda h, s: (tokens // 16, 0))] * len(xs)
        args += [group[0] for group in xs]
    in_specs += [adapters, adapters]
    args += tables
    if step.first and not make_q:
        in_specs.append(by_head)
        args.append(q)
    if not step.first:
        in_specs += [extended, extended, m_spec]
        args += state
    keys_by_head = [pl.BlockSpec((rows, PER * PAIR), lambda h, s: (0, h)) for rows in keys]
    out_specs = [*keys_by_head, *keys_by_head]
    out_specs += [pl.BlockSpec((rows, cols), lambda h, s: (0, 0)) for cols in (slots * RANK, AUG) for rows in keys]
    kv_shapes = [jax.ShapeDtypeStruct((rows, width), BF16) for rows in keys]
    out_shape = [*kv_shapes, *kv_shapes, *[jax.ShapeDtypeStruct((rows, cols), BF16) for cols in (slots * RANK, AUG) for rows in keys]]
    if make_q:
        out_specs.insert(0, by_head)
        out_shape.insert(0, q_shape)
    scratch = [pltpu.VMEM((kinds, width, width), BF16), step.w.sems(kinds)]
    scratch += [pltpu.VMEM((rows, width), BF16) for rows in keys] * 2
    state_shapes = [(PAIR + 16, 2 * tokens), (8, 2 * tokens)]
    if step.first and not step.last:
        out_specs.append(extended)
        out_shape.append(qa_shape)
    if step.last:
        out_specs += [by_head, extended]
        out_shape += [q_shape, qa_shape]
        scratch += [pltpu.VMEM((PER, *shape), F32) for shape in state_shapes]
    else:
        out_specs += [extended, m_spec]
        out_shape += [jax.ShapeDtypeStruct((pairs, *shape), F32) for shape in state_shapes]
    if make_q:
        scratch.append(pltpu.VMEM((tokens, width), BF16))
    call = pl.pallas_call(
        functools.partial(attend_step_kernel, step, [len(group) for group in xs]),
        grid_spec=pltpu.PrefetchScalarGridSpec(
            num_scalar_prefetch=1, grid=(pairs // PER,), in_specs=in_specs + step.w.specs(), out_specs=out_specs, scratch_shapes=scratch
        ),
        out_shape=out_shape,
        name=step.name,
        compiler_params=params(60),
        cost_estimate=cost(sum(keys) / 32),
    )
    out = list(call(scalars, *args, *step.w.arrays))
    q = out.pop(0) if make_q else q
    count = len(xs)
    return q, *[out[at * count : (at + 1) * count] for at in range(4)], out[4 * count :]


def back_step_kernel(step, count, sc_ref, *refs):
    refs = list(refs)

    def take(number):
        return [refs.pop(0) for _ in range(number)]

    qa_ref, ga_ref, q_ref, do_ref, k_ref, v_ref, kaug_ref, r_ref, a_ref, b_ref = take(10)
    xs = take(count)
    dqt_in, sums_in = (None, None) if step.first else take(2)
    query = step.causal and step.last
    d1_ref = take(1)[0] if query else None
    pieces = take(len(step.w.arrays))
    dq_all = None
    if query:
        base_ref, grads_ref, w_ref, dk_all, dv_all, sems, dq_all = refs
    elif step.last:
        own_ref, part_ref, dq_ref, grads_ref, w_ref, dk_all, dv_all, sems = refs
    else:
        part_ref, dqt_ref, sums_ref, w_ref, dk_all, dv_all, sems = refs
    h = pl.program_id(0)
    final = h == pl.num_programs(0) - 1
    width = a_ref.shape[-1]
    parts = step.parts
    slots = a_ref.shape[1]
    keys = k_ref.shape[0]
    block = min(keys, 512)
    (at,) = step.blocks

    def weights():
        return [step.w.bring(pieces, sc_ref[1], part, w_ref.at[place], sems.at[place]) for place, part in enumerate(parts)]

    @step.on(sc_ref, at, h == 0)
    def _():
        for part in weights():
            start_all(part)

    @step.on(sc_ref, at)
    def _():
        for pair in range(PER):
            cols, all_cols = pair_cols(pair), head_cols(pair)
            q = split_pair(q_ref[:, cols] * jnp.asarray(SCALE, BF16))
            grads = split_pair(do_ref[:, cols])
            total = None
            for low in range(0, keys, block):
                span = slice(low, low + block)
                grad_q, grad_keys, grad_values = block_back(
                    k_ref[span, cols], v_ref[span, cols], kaug_ref[span], qa_ref[pair], ga_ref[pair], q, grads, step.causal and at == 0
                )
                dk_all[span, all_cols] = grad_keys
                dv_all[span, all_cols] = grad_values
                total = grad_q if total is None else total + grad_q
            if not step.first:
                total = total + dqt_in[pair]
            if query:
                dq_all[:, all_cols] = (total * SCALE).T.astype(BF16)
            elif step.last:
                dq_ref[:, cols] = (total * SCALE).T.astype(BF16)
            else:
                dqt_ref[pair] = total

    if step.causal and at:

        @pl.when(sc_ref[0] < at)
        def _():
            dqt_ref[...] = jnp.zeros_like(dqt_ref[...]) if step.first else dqt_in[...]

            @pl.when(final)
            def _():
                part_ref[...] = jnp.zeros_like(part_ref)
                sums_ref[...] = jnp.zeros_like(sums_ref) if step.first else sums_in[...]

    @step.on(sc_ref, at, final)
    def _():
        grads = [dq_all, dk_all, dv_all] if query else [dk_all, dv_all]
        shift = slots - len(grads)
        drs, dbs = [], []
        hidden = r_ref[...]
        for place, grad_ref in enumerate(grads):
            slot = place + shift
            grad = grad_ref[...]
            drs.append(low_rank(grad, b_ref[0, slot, 0]))
            dbs.append(tn(hidden[:, slot * RANK : (slot + 1) * RANK], grad))
        dr = jnp.concatenate(drs, axis=1)
        low, da = 0, None
        for x_ref in xs:
            part = tn(dr[low : low + x_ref.shape[0]], x_ref[...])
            da = part if da is None else da + part
            low += x_ref.shape[0]
        olds = [None] * 4 if step.first else [sums_in[place * RANK : (place + 1) * RANK] for place in range(4)]
        if query:
            olds = [None, *olds[:2], None, *olds[2:]]
        total = [da[place * RANK : (place + 1) * RANK] for place in range(len(grads))] + dbs
        target = grads_ref if step.last else sums_ref
        for place, (new, old) in enumerate(zip(total, olds)):
            target[place * RANK : (place + 1) * RANK] = (new if old is None else new + old).astype(target.dtype)
        for part in weights():
            wait_all(part)
        own = keys // count if step.last and not query else 0

        def body(cols):
            table = a_ref[0, shift:, 0, :, cols].reshape(len(grads) * RANK, COLS)
            value = nn(dr, table)
            for place, grad_ref in enumerate(grads):
                value = value + nt(grad_ref[...], w_ref[place, cols, :])
            if query:
                base_ref[:, cols] = value + d1_ref[:, cols]
            elif step.last:
                own_ref[:, cols] = value[:own]
                part_ref[:, cols] = value[own:].astype(BF16)
            else:
                part_ref[:, cols] = value.astype(BF16)

        each(width, COLS, body)


def back_step(step, scalars, qa, ga, q, do, k, v, kaug, r, xs, block_rows, tables, state, d1):
    tokens, width = q.shape
    pairs = width // PAIR
    keys = k.shape[0]
    slots = 3 if step.causal else 2
    query = step.causal and step.last
    by_head = pl.BlockSpec((tokens, PER * PAIR), lambda h, s: (0, h))
    keys_by_head = pl.BlockSpec((keys, PER * PAIR), lambda h, s: (0, h))
    extended = pl.BlockSpec((PER, PAIR + AUG, 2 * tokens), lambda h, s: (h, 0, 0))
    dqt_spec = pl.BlockSpec((PER, PAIR, tokens), lambda h, s: (h, 0, 0))

    def whole(rows):
        return pl.BlockSpec((rows, width), lambda h, s: (0, 0))

    adapters = adapter_spec(0 if step.causal else 4, slots, width)
    in_specs = [
        extended,
        extended,
        by_head,
        by_head,
        keys_by_head,
        keys_by_head,
        pl.BlockSpec((keys, AUG), lambda h, s: (0, 0)),
        pl.BlockSpec((keys, slots * RANK), lambda h, s: (0, 0)),
        adapters,
        adapters,
        *[whole(block_rows)] * len(xs),
    ]
    args = [qa, ga, q, do, k, v, kaug, r, *tables, *xs]
    if not step.first:
        in_specs += [dqt_spec, whole(4 * RANK)]
        args += state
    scratch = [pltpu.VMEM((len(step.parts), width, width), BF16), pltpu.VMEM((keys, width), BF16), pltpu.VMEM((keys, width), BF16)]
    scratch.append(step.w.sems(len(step.parts)))
    if query:
        in_specs.append(whole(tokens))
        args.append(d1)
        scratch.append(pltpu.VMEM((tokens, width), BF16))
        out_specs = [whole(tokens), whole(6 * RANK)]
        out_shape = [jax.ShapeDtypeStruct((tokens, width), F32), jax.ShapeDtypeStruct((6 * RANK, width), BF16)]
    elif step.last:
        rest = keys - block_rows
        out_specs = [whole(block_rows), whole(rest), by_head, whole(4 * RANK)]
        out_shape = [
            jax.ShapeDtypeStruct((block_rows, width), F32),
            jax.ShapeDtypeStruct((rest, width), BF16),
            jax.ShapeDtypeStruct((tokens, width), BF16),
            jax.ShapeDtypeStruct((4 * RANK, width), BF16),
        ]
    else:
        out_specs = [whole(keys), dqt_spec, whole(4 * RANK)]
        out_shape = [
            jax.ShapeDtypeStruct((keys, width), BF16),
            jax.ShapeDtypeStruct((pairs, PAIR, tokens), F32),
            jax.ShapeDtypeStruct((4 * RANK, width), F32),
        ]
    return pl.pallas_call(
        functools.partial(back_step_kernel, step, len(xs)),
        grid_spec=pltpu.PrefetchScalarGridSpec(
            num_scalar_prefetch=1, grid=(pairs // PER,), in_specs=in_specs + step.w.specs(), out_specs=out_specs, scratch_shapes=scratch
        ),
        out_shape=out_shape,
        name=step.name,
        compiler_params=params(60),
        cost_estimate=cost(keys / 24),
    )(scalars, *args, *step.w.arrays)


ROWS = 64


def normalize_rows(u_ref, norm_ref, low_ref, std_ref):
    def body(rows):
        values = u_ref[rows, :]
        centered = values - jnp.mean(values, -1, keepdims=True)
        inv_std = lax.rsqrt(jnp.mean(centered * centered, -1, keepdims=True) + NORM_EPS)
        normed = centered * inv_std
        norm_ref[rows, :] = normed
        low_ref[rows, :] = normed.astype(BF16)
        std_ref[rows, :] = inv_std

    each(u_ref.shape[0], ROWS, body)


def normalize_back(grads, normed, inv_std):
    return inv_std * (grads - jnp.mean(grads, -1, keepdims=True) - normed * jnp.mean(grads * normed, -1, keepdims=True))


def mid_kernel(w, part, query, sc_ref, o_ref, x_ref, a_ref, b_ref, aq_ref, bq_ref, *refs):
    pieces, refs = refs[: len(w.arrays)], refs[len(w.arrays) :]
    if query:
        norm_ref, low_ref, std_ref, r_ref, q_ref, w_ref, u_ref, sems = refs
    else:
        norm_ref, low_ref, std_ref, r_ref, w_ref, u_ref, sems = refs
    width = x_ref.shape[1]
    first = w.bring(pieces, sc_ref[1], part, w_ref.at[0], sems.at[0])
    start_all(first)
    if query:
        second = w.bring(pieces, sc_ref[1], 2, w_ref.at[1], sems.at[1])
        start_all(second)
    o = o_ref[...]
    hidden = low_rank(o, a_ref[0, 0, 0])
    r_ref[:, :RANK] = hidden
    wait_all(first)

    def body(cols):
        u_ref[:, cols] = x_ref[:, cols].astype(F32) + nn(o, w_ref[0, :, cols]) + nn(hidden, b_ref[0, 0, 0, :, cols])

    each(width, COLS, body)
    normalize_rows(u_ref, norm_ref, low_ref, std_ref)
    if query:
        low = low_ref[...]
        hidden_q = low_rank(low, aq_ref[0, 0, 0])
        r_ref[:, RANK:] = hidden_q
        wait_all(second)
        project_into(q_ref, low, w_ref.at[1], hidden_q, lambda cols: bq_ref[0, 0, 0, :, cols])


def mid(name, scalars, outs, residual, part, proj, query, proj_down, proj_up, w):
    rows, width = outs.shape
    shapes = [
        jax.ShapeDtypeStruct((rows, width), F32),
        jax.ShapeDtypeStruct((rows, width), BF16),
        jax.ShapeDtypeStruct((rows, 1), F32),
        jax.ShapeDtypeStruct((rows, 2 * RANK if query else RANK), BF16),
    ]
    if query:
        shapes.append(jax.ShapeDtypeStruct((rows, width), BF16))
    spec, spec_q = adapter_spec(proj, 1, width), adapter_spec(3, 1, width)
    return pl.pallas_call(
        functools.partial(mid_kernel, w, part, query),
        grid_spec=pltpu.PrefetchScalarGridSpec(
            num_scalar_prefetch=1,
            grid=(1,),
            in_specs=[WHOLE, WHOLE, spec, spec, spec_q, spec_q, *w.specs()],
            out_specs=[WHOLE] * len(shapes),
            scratch_shapes=[pltpu.VMEM((2, width, width), BF16), pltpu.VMEM((rows, width), F32), w.sems(2)],
        ),
        out_shape=shapes,
        name=name,
        compiler_params=params(60),
        cost_estimate=cost(1),
    )(scalars, outs, residual, proj_down, proj_up, proj_down, proj_up, *w.arrays)


def gelu_kernel(sc_ref, x_ref, a_ref, b_ref, w_in, g_ref, slope_ref, r_ref, w_ref, low, sems):
    at = pl.program_id(0)
    run = g_ref.shape[1]

    def column(step):
        cols = pl.ds(pl.multiple_of(step * run, run), run)
        return pltpu.make_async_copy(w_in.at[:, cols], w_ref.at[:, cols], sems.at[step])

    @pl.when(at == 0)
    def _():
        for step in range(w_in.shape[1] // run):
            column(step).start()
        low[...] = low_rank(x_ref[...], a_ref[0, 0])
        r_ref[...] = low[...]

    column(at).wait()

    def body(cols):
        across = pl.ds(pl.multiple_of(at * run, run) + cols.start, COLS)
        pre = nn(x_ref[...], w_ref[:, across]) + nn(low[...], b_ref[0, 0, :, cols])
        phi = 0.5 * (1.0 + lax.erf(pre * 0.7071067811865476))
        g_ref[:, cols] = (pre * phi).astype(BF16)
        slope_ref[:, cols] = (phi + pre * jnp.exp(-0.5 * pre * pre) * 0.3989422804014327).astype(BF16)

    each(run, COLS, body)


def gelu_up(scalars, x, down, up, w):
    rows, width = x.shape
    wide = up.shape[3]
    by_column = pl.BlockSpec((rows, width), lambda c, s: (0, c))
    return pl.pallas_call(
        gelu_kernel,
        grid_spec=pltpu.PrefetchScalarGridSpec(
            num_scalar_prefetch=1,
            grid=(wide // width,),
            in_specs=[
                pl.BlockSpec((rows, width), lambda c, s: (0, 0)),
                mlp_adapter_spec(width),
                pl.BlockSpec((1, 1, RANK, width), lambda c, s: (0, s[2], 0, c)),
                ANY,
            ],
            out_specs=[by_column, by_column, pl.BlockSpec((rows, RANK), lambda c, s: (0, 0))],
            scratch_shapes=[pltpu.VMEM((width, wide), BF16), pltpu.VMEM((rows, RANK), BF16), pltpu.SemaphoreType.DMA((wide // width,))],
        ),
        out_shape=[
            jax.ShapeDtypeStruct((rows, wide), BF16),
            jax.ShapeDtypeStruct((rows, wide), BF16),
            jax.ShapeDtypeStruct((rows, RANK), BF16),
        ],
        name="gelu_up",
        compiler_params=params(60),
        cost_estimate=cost(15),
    )(scalars, x, down, up, *w.arrays)


FC_ROWS = {"da1": 0, "db1": 16, "da2": 80, "db2": 144, "da_co": 160, "db_co": 176, "pick": 192}
FC_TOTAL = 208


def mlp_kernel(w_up, w_down, w_mid, sc_ref, g_in, slope_in, h2_in, h2_low_in, std2_ref, cot_in, r1_ref, rco_ref, oc_in,
               a1_ref, b1_ref, a2_ref, b2_ref, a7_ref, b7_ref, *refs):
    ups, refs = refs[: len(w_up.arrays)], refs[len(w_up.arrays) :]
    downs, refs = refs[: len(w_down.arrays)], refs[len(w_down.arrays) :]
    mids, refs = refs[: len(w_mid.arrays)], refs[len(w_mid.arrays) :]
    y_ref, d2_ref, doc_ref, gac_ref, grads_ref, w1, w2, wco, u, low, dpre, sem1, sem2, sem3, *local = refs
    g_ref, slope_ref, h2_ref, h2_low_ref, cot_ref, oc_ref, sem4 = local
    rows, width = h2_ref.shape
    wide = g_ref.shape[1]
    own = sc_ref[1]
    pairs = ((g_in, g_ref), (h2_in, h2_ref), (cot_in, cot_ref), (slope_in, slope_ref), (h2_low_in, h2_low_ref), (oc_in, oc_ref))
    inputs = [pltpu.make_async_copy(source, target, sem4.at[at]) for at, (source, target) in enumerate(pairs)]
    inputs[0].start()
    copies2 = w_down.bring(downs, own, 0, w2, sem2.at[0])
    copies1 = w_up.bring(ups, own, 0, w1, sem1.at[0])
    copies3 = w_mid.bring(mids, own, 1, wco, sem3.at[0])
    start_all(copies2)
    start_all(inputs[1:])
    start_all(copies1)
    start_all(copies3)
    inputs[0].wait()
    g = g_ref[...]
    r2 = low_rank(g, a2_ref[0, 0])
    wait_all(copies2)
    inputs[1].wait()

    def second(cols):
        u[:, cols] = h2_ref[:, cols] + nn(g_ref[...], w2[:, cols]) + nn(r2, b2_ref[0, 0, :, cols])

    each(width, COLS, second)

    def third(at):
        values = u[at, :]
        centered = values - jnp.mean(values, -1, keepdims=True)
        inv_std = lax.rsqrt(jnp.mean(centered * centered, -1, keepdims=True) + NORM_EPS)
        normed = centered * inv_std
        y_ref[at, :] = normed.astype(BF16)
        d3 = normalize_back(cot_ref[at, :].astype(F32), normed, inv_std)
        u[at, :] = d3
        low[at, :] = d3.astype(BF16)

    inputs[2].wait()
    each(rows, ROWS, third)
    wait_all(inputs[3:])
    d3_low = low[...]
    grads_ref[pl.ds(FC_ROWS["db2"], RANK), :] = tn(r2, d3_low).astype(BF16)
    dr2 = low_rank(d3_low, b2_ref[0, 0])
    r1 = r1_ref[...]
    run = 2 * COLS
    runs = width // run

    def slopes(at, carry):
        cols = pl.ds(pl.multiple_of(at * run, run), run)
        down_rows = nt(low[...], w2[cols, :]) + nn(dr2, a2_ref[0, 0, :, cols])
        part = (down_rows * slope_ref[:, cols].astype(F32)).astype(BF16)
        dpre[:, cols] = part
        row = pl.multiple_of((at // runs) * RANK, RANK)
        place = pl.ds(pl.multiple_of((at % runs) * run, run), run)
        grads_ref[pl.ds(FC_ROWS["da2"] + row, RANK), place] = tn(dr2, g_ref[:, cols]).astype(BF16)
        grads_ref[pl.ds(FC_ROWS["db1"] + row, RANK), place] = tn(r1, part).astype(BF16)
        return carry

    lax.fori_loop(0, wide // run, slopes, 0, unroll=2)
    dr1 = low_rank(dpre[...], b1_ref[0, 0])
    grads_ref[pl.ds(FC_ROWS["da1"], RANK), :] = tn(dr1, h2_low_ref[...]).astype(BF16)
    wait_all(copies1)

    def first(cols):
        u[:, cols] += nt(dpre[...], w1[cols, :]) + nn(dr1, a1_ref[0, 0, :, cols])

    each(width, COLS, first)

    def norm(at):
        d2 = normalize_back(u[at, :], h2_ref[at, :], std2_ref[at, :])
        d2_ref[at, :] = d2
        low[at, :] = d2.astype(BF16)

    each(rows, ROWS, norm)
    wait_all(copies3)
    d2_low = low[...]
    grads_ref[pl.ds(FC_ROWS["db_co"], RANK), :] = tn(rco_ref[...], d2_low).astype(BF16)
    drc = low_rank(d2_low, b7_ref[0, 0, 0])
    grads_ref[pl.ds(FC_ROWS["da_co"], RANK), :] = tn(drc, oc_ref[...]).astype(BF16)

    def cross(cols):
        doc_ref[:, cols] = (nt(low[...], wco[cols, :]) + nn(drc, a7_ref[0, 0, 0, :, cols])).astype(BF16)

    each(width, COLS, cross)
    slope_rows(gac_ref, doc_ref, oc_ref)
    mine = jnp.where(sc_ref[0] == 0, sc_ref[2], 0).astype(F32)
    grads_ref[pl.ds(FC_ROWS["pick"], 16), :] = jnp.full((16, width), mine, F32).astype(BF16)


def mlp(scalars, g, slope, h2, h2_low, std2, cot, r1, rco, oc, fc1_down, fc1_up, fc2_down, fc2_up, proj_down, proj_up, w_up, w_down, w_mid):
    rows, width = h2.shape
    wide = g.shape[1]
    return pl.pallas_call(
        functools.partial(mlp_kernel, w_up, w_down, w_mid),
        grid_spec=pltpu.PrefetchScalarGridSpec(
            num_scalar_prefetch=1,
            grid=(1,),
            in_specs=[
                *[ANY] * 4, WHOLE, ANY, WHOLE, WHOLE, ANY,
                mlp_adapter_spec(width),
                mlp_adapter_spec(wide),
                mlp_adapter_spec(wide),
                mlp_adapter_spec(width),
                adapter_spec(7, 1, width),
                adapter_spec(7, 1, width),
                *w_up.specs(),
                *w_down.specs(),
                *w_mid.specs(),
            ],
            out_specs=[WHOLE] * 5,
            scratch_shapes=[
                pltpu.VMEM((width, wide), BF16),
                pltpu.VMEM((wide, width), BF16),
                pltpu.VMEM((width, width), BF16),
                pltpu.VMEM((rows, width), F32),
                pltpu.VMEM((rows, width), BF16),
                pltpu.VMEM((rows, wide), BF16),
                w_up.sems(1),
                w_down.sems(1),
                w_mid.sems(1),
                pltpu.VMEM((rows, wide), BF16),
                pltpu.VMEM((rows, wide), BF16),
                pltpu.VMEM((rows, width), F32),
                pltpu.VMEM((rows, width), BF16),
                pltpu.VMEM((rows, width), BF16),
                pltpu.VMEM((rows, width), BF16),
                pltpu.SemaphoreType.DMA((6,)),
            ],
        ),
        out_shape=[
            jax.ShapeDtypeStruct((rows, width), BF16),
            jax.ShapeDtypeStruct((rows, width), F32),
            jax.ShapeDtypeStruct((rows, width), BF16),
            jax.ShapeDtypeStruct((width // PAIR, PAIR + AUG, 2 * rows), BF16),
            jax.ShapeDtypeStruct((FC_TOTAL, width), BF16),
        ],
        name="mlp",
        compiler_params=params(60),
        cost_estimate=cost(33),
    )(scalars, g, slope, h2, h2_low, std2, cot, r1, rco, oc, fc1_down, fc1_up, fc2_down, fc2_up, proj_down, proj_up,
      *w_up.arrays, *w_down.arrays, *w_mid.arrays)


def mid_back_kernel(w, sc_ref, dqc_ref, d2_ref, h1_ref, h1_low_ref, std1_ref, r_ref, o_ref, aq_ref, bq_ref, a_ref, b_ref, *refs):
    pieces, refs = refs[: len(w.arrays)], refs[len(w.arrays) :]
    d1_ref, do_ref, ga_ref, grads_ref, w_ref, low, sems = refs
    rows, width = d2_ref.shape
    first = w.bring(pieces, sc_ref[1], 2, w_ref.at[1], sems.at[1])
    second = w.bring(pieces, sc_ref[1], 0, w_ref.at[0], sems.at[0])
    start_all(first)
    start_all(second)
    dqc = dqc_ref[...]
    drq = low_rank(dqc, bq_ref[0, 0, 0])
    grads_ref[0:RANK, :] = tn(drq, h1_low_ref[...]).astype(BF16)
    grads_ref[2 * RANK : 3 * RANK, :] = tn(r_ref[:, RANK:], dqc).astype(BF16)
    wait_all(first)

    def query(cols):
        d1_ref[:, cols] = d2_ref[:, cols] + nt(dqc_ref[...], w_ref[1, cols, :]) + nn(drq, aq_ref[0, 0, 0, :, cols])

    each(width, COLS, query)

    def norm(at):
        d1 = normalize_back(d1_ref[at, :], h1_ref[at, :], std1_ref[at, :])
        d1_ref[at, :] = d1
        low[at, :] = d1.astype(BF16)

    each(rows, ROWS, norm)
    wait_all(second)
    d1_low = low[...]
    dr = low_rank(d1_low, b_ref[0, 0, 0])
    grads_ref[RANK : 2 * RANK, :] = tn(dr, o_ref[...]).astype(BF16)
    grads_ref[3 * RANK :, :] = tn(r_ref[:, :RANK], d1_low).astype(BF16)

    def out(cols):
        do_ref[:, cols] = (nt(low[...], w_ref[0, cols, :]) + nn(dr, a_ref[0, 0, 0, :, cols])).astype(BF16)

    each(width, COLS, out)

    slope_rows(ga_ref, do_ref, o_ref)


def mid_back(scalars, dqc, d2, h1, h1_low, std1, r, o, proj_down, proj_up, w):
    rows, width = d2.shape
    spec, spec_q = adapter_spec(6, 1, width), adapter_spec(3, 1, width)
    return pl.pallas_call(
        functools.partial(mid_back_kernel, w),
        grid_spec=pltpu.PrefetchScalarGridSpec(
            num_scalar_prefetch=1,
            grid=(1,),
            in_specs=[*[WHOLE] * 7, spec_q, spec_q, spec, spec, *w.specs()],
            out_specs=[WHOLE] * 4,
            scratch_shapes=[pltpu.VMEM((2, width, width), BF16), pltpu.VMEM((rows, width), BF16), w.sems(2)],
        ),
        out_shape=[
            jax.ShapeDtypeStruct((rows, width), F32),
            jax.ShapeDtypeStruct((rows, width), BF16),
            jax.ShapeDtypeStruct((width // PAIR, PAIR + AUG, 2 * rows), BF16),
            jax.ShapeDtypeStruct((4 * RANK, width), BF16),
        ],
        name="mid_back",
        compiler_params=params(60),
        cost_estimate=cost(1),
    )(scalars, dqc, d2, h1, h1_low, std1, r, o, proj_down, proj_up, proj_down, proj_up, *w.arrays)


def add_picked(picks_ref, sequences, out, source):
    adapters, view = out
    for adapter in range(adapters):
        view(adapter)[...] = jnp.zeros(view(adapter).shape, F32)
    for at in range(sequences):
        target = view(picks_ref[at])
        target[...] += source(at).astype(F32)


def fc_total_kernel(picks_ref, g_ref, a1_ref, b1_ref, a2_ref, b2_ref):
    sequences, _, width = g_ref.shape
    adapters = a1_ref.shape[1]

    def put(out_ref, col, row):
        def view(adapter):
            return out_ref.at[0, adapter, :, pl.ds(col, width)]

        add_picked(picks_ref, sequences, (adapters, view), lambda at: g_ref[at, pl.ds(row, RANK), :])

    for out_ref, name in ((a1_ref, "da1"), (b1_ref, "db1"), (a2_ref, "da2"), (b2_ref, "db2")):
        for at in range(out_ref.shape[3] // width):
            put(out_ref, at * width, FC_ROWS[name] + at * RANK)


def fc_total(picks, gathered, shapes):
    return pl.pallas_call(
        fc_total_kernel,
        grid_spec=pltpu.PrefetchScalarGridSpec(
            num_scalar_prefetch=1, grid=(1,), in_specs=[WHOLE], out_specs=[WHOLE] * 4
        ),
        out_shape=[jax.ShapeDtypeStruct(s, F32) for s in shapes],
        name="fc_total",
        compiler_params=params(60),
        cost_estimate=cost(6),
    )(picks, gathered)


PROJ_ROWS = {
    0: (2, 0, 48),
    1: (2, 16, 64),
    2: (2, 32, 80),
    3: (1, 0, 32),
    4: (1, 64, 96),
    5: (1, 80, 112),
    6: (1, 16, 48),
    7: (0, FC_ROWS["da_co"], FC_ROWS["db_co"]),
}


def proj_total_kernel(projs, first_source, count, sources, picks_ref, *refs):
    g_refs, (down_ref, up_ref) = refs[:sources], refs[-2:]
    adapters = down_ref.shape[2]
    for at, proj in enumerate(projs):
        source, down_row, up_row = PROJ_ROWS[proj]
        g_ref = g_refs[source - first_source]

        @pl.when(pl.program_id(0) == at)
        def _(g_ref=g_ref, down_row=down_row, up_row=up_row):
            for out_ref, row in ((down_ref, down_row), (up_ref, up_row)):
                add_picked(
                    picks_ref, g_ref.shape[0], (adapters, lambda adapter, out_ref=out_ref: out_ref.at[0, 0, adapter]),
                    lambda at, row=row: g_ref[at, pl.ds(row, RANK), :],
                )


def proj_total(picks, gathered, projs, so_far, shape):
    first = projs[0]
    block = pl.BlockSpec((1, 1, *shape[2:]), lambda p, s: (0, p + first, 0, 0, 0))
    rest = [] if so_far is None else list(so_far)
    first_source = min(PROJ_ROWS[proj][0] for proj in projs)
    return pl.pallas_call(
        functools.partial(proj_total_kernel, tuple(projs), first_source, len(rest), len(gathered)),
        grid_spec=pltpu.PrefetchScalarGridSpec(
            num_scalar_prefetch=1,
            grid=(len(projs),),
            in_specs=[WHOLE] * len(gathered) + [ANY] * len(rest),
            out_specs=[block] * 2,
        ),
        out_shape=[jax.ShapeDtypeStruct(shape, F32)] * 2,
        input_output_aliases={1 + len(gathered) + at: at for at in range(len(rest))},
        name=f"proj_total_{first}",
        compiler_params=params(60),
        cost_estimate=cost(1.4 * len(projs)),
    )(picks, *gathered, *rest)


class Gathering:
    def __init__(self, shard, parts, across, sibling, together):
        self.shard, self.parts, self.across, self.sibling, self.together = shard, parts, across, sibling, together
        self.half = shard.shape[0] // 2

    def begin(self):
        self.x, self.y = self.across(self.shard, 1), self.across(self.shard, 2)
        self.own = self.sibling(self.shard)

    def forward(self):
        self.xy, self.yx = self.across(self.x[: self.half], 2), self.across(self.y[self.half :], 1)
        if self.together:
            self.near = [self.sibling(jnp.concatenate([self.x, self.y], axis=0))]
        else:
            self.near = [self.sibling(self.x), self.sibling(self.y)]

    def share(self):
        self.far = self.sibling(jnp.concatenate([self.xy, self.yx], axis=0))

    def result(self):
        rows, half = self.shard.shape[0], self.half
        arrays = [self.shard, self.own, self.x, self.y, *self.near, self.xy, self.yx, self.far]
        layout = [[(0, True, who, 0, rows)] for who in (0, 1, 2, 4)]
        if self.together:
            layout += [[(0, True, 3, 0, rows), (rows, True, 5, 0, rows)]]
        else:
            layout += [[(0, True, 3, 0, rows)], [(0, True, 5, 0, rows)]]
        layout += [[(0, True, 6, 0, half)], [(0, True, 6, half, rows - half)]]
        layout += [[(0, True, 7, 0, half), (half, True, 7, half, rows - half)]]
        return Gathered(arrays, layout, rows // self.parts)


class Whole:
    def __init__(self, shard, parts, shards, gather):
        self.shard, self.parts, self.shards, self.gather = shard, parts, shards, gather
        self.x = self.y = self.own = self.xy = self.yx = shard
        self.near = []

    def begin(self):
        self.whole = self.gather(self.shard)

    def forward(self):
        pass

    def share(self):
        pass

    def result(self):
        rows = self.shard.shape[0]
        return Gathered([self.whole], [[(at * rows, False, at, 0, rows) for at in range(self.shards)]], rows // self.parts)


def make_shards(mesh):
    chips, span = mesh.shape["chip"], mesh.shape["sp"]
    plane = ("chip", "core")

    def tie(*values):
        return lax.optimization_barrier(values)

    def turn(values, by):
        return lax.ppermute(values, "sp", [(i, (i + by) % span) for i in range(span)])

    def swap(values, bit):
        return lax.ppermute(values, "sp", [(i, i ^ bit) for i in range(span)])

    def across(values, bit):
        return lax.ppermute(values, "chip", [(i, i ^ bit) for i in range(chips)])

    def sibling(values):
        return lax.ppermute(values, "core", [(0, 1), (1, 0)])

    def gathering(shard, parts, steps, together=False):
        if chips == 4 and steps:
            return Gathering(shard, parts, across, sibling, together)
        return Whole(shard, parts, 2 * chips, lambda v: lax.all_gather(v, plane, axis=0, tiled=True))

    def shards(
        inputs,
        segments,
        enc_states,
        adapter_pick,
        qkv_weights,
        out_weights,
        mlp_in,
        mlp_out,
        proj_down,
        proj_up,
        fc1_down,
        fc1_up,
        fc2_down,
        fc2_up,
        cotangent,
    ):
        x_low = inputs[0]
        memory = enc_states[0]
        tokens, width = x_low.shape
        mem_rows = memory.shape[0]
        own = lax.axis_index("chip") * 2 + lax.axis_index("core")
        scalars = jnp.stack([lax.axis_index("sp"), own, adapter_pick[0]]).astype(jnp.int32)
        tables = (proj_down, proj_up)

        a = gathering(qkv_weights[0, :3].reshape(-1, width), 3, True)
        b_shard = jnp.concatenate([out_weights[0].reshape(-1, width), qkv_weights[0, 3:].reshape(-1, width)], axis=0)
        b = gathering(b_shard, 5, True, True)
        c, d = gathering(mlp_in[0], 1, False), gathering(mlp_out[0], 1, True, True)

        seg_row = jnp.pad(segments.astype(BF16), ((0, 15), (0, width - tokens)))
        ext = [jnp.concatenate([x_low, seg_row], axis=0)]
        a.begin()
        ext.append(turn(ext[0], 1))
        a.x, a.y, a.own, ext[1] = tie(a.x, a.y, a.own, ext[1])
        a.forward()
        ext.append(turn(ext[1], 1))
        a.xy, a.yx, b.shard, ext[2], *a.near = tie(a.xy, a.yx, b.shard, ext[2], *a.near)
        a.share()
        b.begin()
        while len(ext) < span:
            ext.append(turn(ext[-1], 1))
        w_a = a.result()

        state, ks, vs, rs, augs = None, [], [], [], []
        q = o = None
        for at in range(0, span, 2):
            step = Step(f"self_{at}", w_a, (0, 1, 2) if at == 0 else (1, 2), (at, at + 1), at == 0, at == span - 2, True)
            if at:
                ext[at], ext[at + 1], state[1] = tie(ext[at], ext[at + 1], state[1])
            q, k, v, r, aug, out = attend_step(step, scalars, [[ext[at]], [ext[at + 1]]], tokens, tokens, tables, q, state)
            ks, vs, rs, augs = ks + k, vs + v, rs + r, augs + aug
            if at < span - 2:
                state = out if at == 0 else [state[0], *out]
            else:
                o, qa = out
            if at == 0:
                state[1], b.x, b.y, b.own, ext[-1], on, c.shard = tie(state[1], b.x, b.y, b.own, ext[-1], memory, c.shard)
                b.forward()
                c.begin()
                mems = [memory, turn(on, 1), *[None] * (span - 3), turn(on, -1)]
        o, mems[1], mems[-1], b.xy, b.yx, *b.near = tie(o, mems[1], mems[-1], b.xy, b.yx, *b.near)
        b.share()
        for by in range(2, span - 1):
            mems[by] = turn(mems[by - 1], 1)
        w_b = b.result()
        h1, h1_low, std1, r_mid, qc = mid("mid", scalars, o, x_low, 0, 6, True, *tables, w_b)
        qc, d.shard, *mems[1:] = tie(qc, d.shard, *mems[1:])
        d.begin()
        step = Step("cross", w_b, (3, 4), (0,), True, True, False)
        _, (kc,), (vc,), (r_mem,), (free_aug,), (oc, qca) = attend_step(step, scalars, [mems], tokens, mem_rows, tables, qc, None)
        h2, h2_low, std2, r_co = mid("mid_cross", scalars, oc, h1, 1, 7, False, *tables, w_b)
        h2_low, d.x, d.y, d.own = tie(h2_low, d.x, d.y, d.own)
        d.forward()
        w_c = c.result()
        g, slope, r_fc1 = gelu_up(scalars, h2_low, fc1_down, fc1_up, w_c)
        g, d.xy, d.yx, *d.near = tie(g, d.xy, d.yx, *d.near)
        d.share()
        w_d = d.result()
        y, d2, doc, gac, fc_grads = mlp(
            scalars, g, slope, h2, h2_low, std2, cotangent[0], r_fc1, r_co, oc,
            fc1_down, fc1_up, fc2_down, fc2_up, *tables, w_c, w_d, w_b,
        )
        g0 = lax.psum(fc_grads, "sp")

        step = Step("cross_back", w_b, (3, 4), (0,), True, True, False)
        dmem, parts, dqc, cross_grads = back_step(step, scalars, qca, gac, qc, doc, kc, vc, free_aug, r_mem, mems, mem_rows, tables, None, None)

        def mem_part(slot):
            return parts[(slot - 1) * mem_rows : slot * mem_rows]

        def added(slot, arrived):
            return (mem_part(slot).astype(F32) + arrived.astype(F32)).astype(BF16)

        middle = span // 2
        lower, upper = turn(mem_part(middle), -1), turn(mem_part(middle + 1), 1)
        d1, do, ga, mid_grads = mid_back(scalars, dqc, d2, h1, h1_low, std1, r_mid, o, *tables, w_b)
        g0, g1 = tie(g0, jnp.concatenate([mid_grads, cross_grads], axis=0))
        g1 = lax.psum(g1, "sp")
        g0 = g0[None]

        def doubled(values, bit):
            return jnp.concatenate([values, across(values, bit)], axis=0)

        bits = [1 << at for at in range(chips.bit_length() - 1)]
        state, moving, waiting, at_bit = None, None, [], 0
        for at in reversed(range(span)):
            step = Step(f"self_back_{at}", w_a, (0, 1, 2) if at == 0 else (1, 2), (at,), at == span - 1, at == 0, True)
            out = back_step(step, scalars, qa, ga, q, do, ks[at], vs[at], augs[at], rs[at], [ext[at]], tokens, tables, state, d1)
            if at == 0:
                dx, g2 = out
                g2, g0, g1, moving = tie(g2, g0, g1, moving)
            else:
                part, *state = out
                if at == span - 1:
                    part, state[0], lower, upper = tie(part, state[0], lower, upper)
                    for slot in range(middle - 1, 1, -1):
                        lower = turn(added(slot, lower), -1)
                    for slot in range(middle + 2, span):
                        upper = turn(added(slot, upper), 1)
                    lower = added(1, lower)
                    moving = turn(part, -1)
                elif at == 1:
                    waiting.append(part)
                    state[0], moving, *waiting = tie(state[0], moving, *waiting)
                    while len(waiting) > 1:
                        part = (waiting.pop(0).astype(F32) + moving.astype(F32)).astype(BF16)
                        part, state[0] = tie(part, state[0])
                        moving = turn(part, -1)
                else:
                    waiting.append(part)
                if at == span - 2:
                    g0, state[0] = tie(g0, state[0])
                if at >= span - 2 and at_bit < len(bits):
                    g0 = doubled(g0, bits[at_bit])
                    at_bit += 1
        while at_bit < len(bits):
            g0 = doubled(g0, bits[at_bit])
            at_bit += 1

        g0 = jnp.concatenate([g0, sibling(g0)], axis=0)
        g1 = doubled(g1[None], bits[0])
        g2 = (g2.astype(F32) + swap(g2, 1).astype(F32)).astype(BF16)
        g2, g1, g0 = tie(g2, g1, g0)
        for bit in bits[1:]:
            g1 = doubled(g1, bit)
        picks = g0[:, FC_ROWS["pick"], 0].astype(jnp.int32)
        fcs = fc_total(picks, g0, (fc1_down.shape, fc1_up.shape, fc2_down.shape, fc2_up.shape))
        bit = 2
        while bit < span:
            g2 = (g2.astype(F32) + swap(g2, bit).astype(F32)).astype(BF16)
            bit *= 2
        g2, g1, lower, picks, moving, *fcs = tie(g2, g1, lower, picks, moving, *fcs)
        moving = turn((waiting[0].astype(F32) + moving.astype(F32)).astype(BF16), -1)
        g1 = jnp.concatenate([g1, sibling(g1)], axis=0)
        g2 = doubled(g2[None], bits[0])
        g2, g1, picks = tie(g2, g1, picks)
        lower = turn(lower, -1)
        projs = proj_total(picks, (g0, g1), range(3, 8), None, proj_down.shape)
        for bit in bits[1:]:
            g2 = doubled(g2, bit)
        g2, lower, moving, *projs = tie(g2, lower, moving, *projs)
        g2 = jnp.concatenate([g2, sibling(g2)], axis=0)
        projs = list(proj_total(picks, (g2,), range(3), projs, proj_down.shape))
        dx = dx + moving.astype(F32)
        dmem = dmem + lower.astype(F32) + upper.astype(F32)
        return (y[None], dx[None], dmem[None], *projs, *fcs)

    return shards


def solution(mesh):
    count = mesh.shape["fsdp"]
    fine = Mesh(mesh.devices.reshape(count // 2, 2, mesh.shape["sp"]), ("chip", "core", "sp"))
    fsdp = ("chip", "core")
    row = P(fsdp, "sp", None)
    return jax.shard_map(
        make_shards(fine),
        mesh=fine,
        in_specs=(
            row,
            P(fsdp, "sp"),
            row,
            P(fsdp),
            P(None, None, fsdp, None),
            P(None, None, fsdp, None),
            P(None, fsdp, None),
            P(None, fsdp, None),
            P(),
            P(),
            P(),
            P(),
            P(),
            P(),
            row,
        ),
        out_specs=(row, row, row, P(), P(), P(), P(), P(), P()),
        check_vma=False,
    )
```

```python
import functools

import jax
import jax.numpy as jnp
from jax import lax
from jax.experimental import pallas as pl
from jax.experimental.pallas import tpu as pltpu
from jax.sharding import Mesh
from jax.sharding import PartitionSpec as P

HEAD = 64
PAIR = 2 * HEAD
RANK = 16
AUG = 16
TERMS = 3
SEG_KINDS = 5
COLS = 256
NORM_EPS = 1e-05
FAR = -1e30
SCALE = HEAD**-0.5
F32 = jnp.float32
BF16 = jnp.bfloat16
ANY = pl.BlockSpec(memory_space=pltpu.HBM)
WHOLE = pl.BlockSpec(memory_space=pltpu.VMEM)


def dot(left, right, left_dim, right_dim):
    return lax.dot_general(left, right, (((left_dim,), (right_dim,)), ((), ())), preferred_element_type=F32)


def nn(left, right):
    return dot(left, right, 1, 0)


def nt(left, right):
    return dot(left, right, 1, 1)


def tn(left, right):
    return dot(left, right, 0, 0)


def params(mib):
    return pltpu.CompilerParams(vmem_limit_bytes=mib * 1024 * 1024)


def cost(us):
    return pl.CostEstimate(flops=int(us * 1.15e9), bytes_accessed=0, transcendentals=0)


def each(total, size, body, unroll=4):
    def step(at, carry):
        body(pl.ds(pl.multiple_of(at * size, size), size))
        return carry

    lax.fori_loop(0, total // size, step, 0, unroll=min(unroll, total // size))


def fetch(refs, layout, own, rows, part, target, sems):
    copies = []
    for ref, entries in zip(refs, layout):
        for source, flip, who, first, count in entries:
            low, high = max(first, part * rows), min(first + count, (part + 1) * rows)
            if low < high:
                shard = own ^ who if flip else who
                copies.append(
                    pltpu.make_async_copy(
                        ref.at[pl.ds(source + low - first, high - low)],
                        target.at[pl.ds(pl.multiple_of(shard * rows + (low - part * rows), 16), high - low)],
                        sems.at[len(copies)],
                    )
                )
    return copies


def start_all(copies):
    for copy in copies:
        copy.start()


def wait_all(copies):
    for copy in copies:
        copy.wait()


def low_half(shape, axis):
    return lax.broadcasted_iota(jnp.int32, shape, axis) < HEAD


def split_pair(rows):
    low = low_half(rows.shape, 1)
    zero = jnp.zeros_like(rows)
    return jnp.concatenate([jnp.where(low, rows, zero), jnp.where(low, zero, rows)], axis=0)


def split_pair_t(cols):
    low = low_half(cols.shape, 0)
    zero = jnp.zeros_like(cols)
    return jnp.concatenate([jnp.where(low, cols, zero), jnp.where(low, zero, cols)], axis=1)


def join_pair_t(cols):
    half = cols.shape[1] // 2
    return jnp.where(low_half((PAIR, half), 0), cols[:, :half], cols[:, half:])


def turned(rows):
    return rows.astype(F32).T


def term_rows(row, rest):
    high = row.astype(BF16).astype(F32)
    mid = (row - high).astype(BF16).astype(F32)
    low = row - high - mid
    at = lax.broadcasted_iota(jnp.int32, rest.shape, 0)
    return jnp.where(at == 0, high, jnp.where(at == 1, mid, jnp.where(at == 2, low, rest))).astype(BF16)


def causal_scores(scores):
    keys, columns = scores.shape
    row = lax.broadcasted_iota(jnp.int32, (keys, columns // 2), 0)
    col = lax.broadcasted_iota(jnp.int32, (keys, columns // 2), 1)
    keep = row <= col
    return jnp.where(jnp.concatenate([keep, keep], axis=1), scores, FAR)


def out_slopes(grads, outs):
    gt = turned(grads)
    products = gt * turned(outs)
    delta = jnp.concatenate([jnp.sum(products[:HEAD], axis=0, keepdims=True), jnp.sum(products[HEAD:], axis=0, keepdims=True)], axis=1)
    rest = jnp.zeros((AUG, delta.shape[1]), F32)
    return jnp.concatenate([split_pair_t(gt.astype(BF16)), term_rows(-delta, rest)], axis=0)


def block_back(keys, values, kaug, qa, ga, q, grads, diagonal):
    scores = nn(jnp.concatenate([keys, kaug], axis=1), qa)
    if diagonal:
        scores = causal_scores(scores)
    chances = jnp.exp(scores)
    slopes = nn(jnp.concatenate([values, kaug], axis=1), ga)
    low_slopes = (chances * slopes).astype(BF16)
    grad_values = nn(chances.astype(BF16), grads).astype(BF16)
    grad_keys = nn(low_slopes, q).astype(BF16)
    grad_q = join_pair_t(nn(turned(keys).astype(BF16), low_slopes))
    return grad_q, grad_keys, grad_values


def slope_rows(ga_ref, do_ref, o_ref):
    for at in range(ga_ref.shape[0]):
        cols = slice(at * PAIR, (at + 1) * PAIR)
        ga_ref[at] = out_slopes(do_ref[:, cols], o_ref[:, cols])


def adapter_spec(first, count, width):
    return pl.BlockSpec((1, count, 1, RANK, width), lambda *at: (0, first // count, at[-1][2], 0, 0))


def mlp_adapter_spec(width):
    return pl.BlockSpec((1, 1, RANK, width), lambda *at: (0, at[-1][2], 0, 0))


def low_rank(rows, table):
    return nt(rows, table).astype(BF16)


class Gathered:
    def __init__(self, arrays, layout, rows):
        self.arrays, self.layout, self.rows = arrays, layout, rows
        self.count = sum(len(entries) for entries in layout)

    def bring(self, refs, own, part, target, sems):
        return fetch(refs, self.layout, own, self.rows, part, target, sems)

    def specs(self):
        return [ANY] * len(self.arrays)

    def sems(self, parts):
        return pltpu.SemaphoreType.DMA((parts, self.count))


def project_into(out_ref, rows, weight, hidden, up):
    def body(cols):
        out_ref[:, cols] = (nn(rows, weight[:, cols]) + nn(hidden, up(cols))).astype(out_ref.dtype)

    each(out_ref.shape[1], COLS, body)


class Gathered:
    def __init__(self, arrays, layout, rows):
        self.arrays, self.layout, self.rows = arrays, layout, rows
        self.count = sum(len(entries) for entries in layout)

    def bring(self, refs, own, part, target, sems):
        return fetch(refs, self.layout, own, self.rows, part, target, sems)

    def specs(self):
        return [ANY] * len(self.arrays)

    def groups(self):
        groups, at = {}, 0
        for entries in self.layout:
            for _, flip, who, _, _ in entries:
                groups.setdefault((flip, who), []).append(at)
                at += 1
        return groups.items()

    def sems(self, parts):
        return pltpu.SemaphoreType.DMA((parts, self.count))


def project_into(out_ref, rows, weight, hidden, up):
    def body(cols):
        out_ref[:, cols] = (nn(rows, weight[:, cols]) + nn(hidden, up(cols))).astype(out_ref.dtype)

    each(out_ref.shape[1], COLS, body)


PER = 2


class Step:
    def __init__(self, name, w, parts, blocks, first, last, causal):
        self.name, self.w, self.parts, self.blocks, self.first, self.last, self.causal = name, w, parts, blocks, first, last, causal

    def on(self, sc_ref, at, condition=None):
        conditions = [] if condition is None else [condition]
        if self.causal and at:
            conditions.append(sc_ref[0] >= at)
        if not conditions:
            return lambda body: body()
        return pl.when(conditions[0] if len(conditions) == 1 else conditions[0] & conditions[1])


def head_cols(pair):
    return pl.ds(pl.multiple_of((pl.program_id(0) * PER + pair) * PAIR, PAIR), PAIR)


def pair_cols(pair):
    return slice(pair * PAIR, (pair + 1) * PAIR)


def key_rows(seg_ref, keys):
    at = lax.broadcasted_iota(jnp.int32, (AUG, keys), 0)
    if seg_ref is None:
        return jnp.where(at < TERMS, 1.0, 0.0)
    other = (at.astype(F32) - TERMS != seg_ref[0:1, :keys].astype(F32)) & (at < TERMS + SEG_KINDS)
    return jnp.where(at < TERMS, 1.0, jnp.where(other, FAR, 0.0))


def query_rows(seg_ref, queries):
    at = lax.broadcasted_iota(jnp.int32, (AUG, queries), 0)
    if seg_ref is None:
        return jnp.zeros((AUG, queries), F32)
    same = (at.astype(F32) - TERMS == seg_ref[0:1, :queries].astype(F32)) & (at >= TERMS) & (at < TERMS + SEG_KINDS)
    return jnp.where(same, 1.0, 0.0)


def attend_step_kernel(step, counts, sc_ref, *refs):
    refs = list(refs)
    make_q = step.causal and step.first

    def take(number):
        return [refs.pop(0) for _ in range(number)]

    groups = len(counts)
    xs = [take(count) for count in counts]
    segs = take(groups) if step.causal else [None] * groups
    a_ref, b_ref = take(2)
    q_ref = take(1)[0] if step.first and not make_q else None
    qa_in, acc_in, m_in = (None, None, None) if step.first else take(3)
    pieces = take(len(step.w.arrays))
    q_out = take(1)[0] if make_q else None
    k_outs, v_outs, r_outs, kaugs = take(groups), take(groups), take(groups), take(groups)
    qa_out, o_out = None, None
    if step.first and not step.last:
        qa_out = take(1)[0]
    if step.last:
        o_out, qa_out, w_ref, sems = take(4)
    else:
        acc_ref, m_ref, w_ref, sems = take(4)
    k_alls, v_alls = take(groups), take(groups)
    if step.last:
        acc_ref, m_ref = take(2)
    q_all = take(1)[0] if make_q else None
    parts = step.parts

    def copies(at):
        return step.w.bring(pieces, sc_ref[1], parts[at], w_ref.at[at], sems.at[at])

    for group, at in enumerate(step.blocks):

        @step.on(sc_ref, at, pl.program_id(0) == 0)
        def _(group=group):
            if group == 0:
                for slot in range(len(parts)):
                    start_all(copies(slot))
            kaugs[group][...] = key_rows(segs[group], kaugs[group].shape[0]).T.astype(BF16)
            low = 0
            tables = a_ref[...].reshape(-1, a_ref.shape[-1])
            for x_ref in xs[group]:
                x = x_ref[...]
                span = pl.ds(low, x.shape[0])
                low += x.shape[0]
                hidden = low_rank(x, tables)
                r_outs[group][span, :] = hidden
                outs = [k_alls[group], v_alls[group]]
                if make_q and group == 0:
                    outs.insert(0, q_all)
                for number, out in enumerate(outs):
                    place = number + len(parts) - len(outs)
                    slot = number + a_ref.shape[1] - len(outs)
                    own = hidden[:, slot * RANK : (slot + 1) * RANK]
                    if group == 0 and x_ref is xs[0][0]:
                        wait_all(copies(place))

                    def body(cols, place=place, slot=slot, own=own, out=out):
                        out[span, cols] = (nn(x, w_ref[place, :, cols]) + nn(own, b_ref[0, slot, 0, :, cols])).astype(BF16)

                    each(out.shape[1], COLS, body)

    qas = []
    for pair in range(PER):
        if step.first:
            q = q_all[:, head_cols(pair)] if make_q else q_ref[:, pair_cols(pair)]
            if make_q:
                q_out[:, pair_cols(pair)] = q
            seg = query_rows(segs[0], q.shape[0])
            qt = split_pair_t((turned(q) * SCALE).astype(BF16))
            qas.append(jnp.concatenate([qt, jnp.concatenate([seg, seg], axis=1).astype(BF16)], axis=0))
            if not step.last:
                qa_out[pair] = qas[pair]
        else:
            qas.append(qa_in[pair])

    def block(group, at, opens):
        for pair in range(PER):
            keys, values = k_alls[group][:, head_cols(pair)], v_alls[group][:, head_cols(pair)]
            k_outs[group][:, pair_cols(pair)] = keys
            v_outs[group][:, pair_cols(pair)] = values
            scores = nn(jnp.concatenate([keys, kaugs[group][...]], axis=1), qas[pair])
            if step.causal and at == 0:
                scores = causal_scores(scores)
            top = jnp.max(scores, axis=0, keepdims=True)
            vt = jnp.concatenate([turned(values).astype(BF16), jnp.ones((16, keys.shape[0]), BF16)], axis=0)
            if opens and step.first:
                acc_ref[pair] = nn(vt, jnp.exp(scores - top).astype(BF16))
            else:
                old = m_in[pair, 0:1] if opens else m_ref[pair, 0:1]
                so_far = acc_in[pair] if opens else acc_ref[pair]
                top = jnp.maximum(old, top)
                acc_ref[pair] = so_far * jnp.exp(old - top) + nn(vt, jnp.exp(scores - top).astype(BF16))
            m_ref[pair] = jnp.broadcast_to(top, m_ref.shape[1:])

    for group, at in enumerate(step.blocks):
        step.on(sc_ref, at)(functools.partial(block, group, at, group == 0))
    if step.causal and step.blocks[0]:

        @pl.when(sc_ref[0] < step.blocks[0])
        def _():
            acc_ref[...] = acc_in[...]
            m_ref[...] = m_in[...]

    if step.last:
        for pair in range(PER):
            total = acc_ref[pair, PAIR : PAIR + 1]
            o_out[:, pair_cols(pair)] = join_pair_t(acc_ref[pair, :PAIR] / total).T.astype(BF16)
            lse = m_ref[pair, 0:1] + jnp.log(total)
            qa_out[pair] = jnp.concatenate([qas[pair][:PAIR], term_rows(-lse, qas[pair][PAIR:].astype(F32))], axis=0)


def attend_step(step, scalars, xs, tokens, block_rows, tables, q, state):
    width = xs[0][0].shape[1]
    pairs = width // PAIR
    keys = [block_rows * len(group) for group in xs]
    make_q = step.causal and step.first
    kinds = len(step.parts)
    slots = 3 if step.causal else 2
    by_head = pl.BlockSpec((tokens, PER * PAIR), lambda h, s: (0, h))
    extended = pl.BlockSpec((PER, PAIR + AUG, 2 * tokens), lambda h, s: (h, 0, 0))
    m_spec = pl.BlockSpec((PER, 8, 2 * tokens), lambda h, s: (h, 0, 0))
    adapters = adapter_spec(0 if step.causal else 4, slots, width)
    q_shape = jax.ShapeDtypeStruct((tokens, width), BF16)
    qa_shape = jax.ShapeDtypeStruct((pairs, PAIR + AUG, 2 * tokens), BF16)
    in_specs = [pl.BlockSpec((block_rows, width), lambda h, s: (0, 0))] * sum(len(group) for group in xs)
    args = [x for group in xs for x in group]
    if step.causal:
        in_specs += [pl.BlockSpec((16, width), lambda h, s: (tokens // 16, 0))] * len(xs)
        args += [group[0] for group in xs]
    in_specs += [adapters, adapters]
    args += tables
    if step.first and not make_q:
        in_specs.append(by_head)
        args.append(q)
    if not step.first:
        in_specs += [extended, extended, m_spec]
        args += state
    keys_by_head = [pl.BlockSpec((rows, PER * PAIR), lambda h, s: (0, h)) for rows in keys]
    out_specs = [*keys_by_head, *keys_by_head]
    out_specs += [pl.BlockSpec((rows, cols), lambda h, s: (0, 0)) for cols in (slots * RANK, AUG) for rows in keys]
    kv_shapes = [jax.ShapeDtypeStruct((rows, width), BF16) for rows in keys]
    out_shape = [*kv_shapes, *kv_shapes, *[jax.ShapeDtypeStruct((rows, cols), BF16) for cols in (slots * RANK, AUG) for rows in keys]]
    if make_q:
        out_specs.insert(0, by_head)
        out_shape.insert(0, q_shape)
    scratch = [pltpu.VMEM((kinds, width, width), BF16), step.w.sems(kinds)]
    scratch += [pltpu.VMEM((rows, width), BF16) for rows in keys] * 2
    state_shapes = [(PAIR + 16, 2 * tokens), (8, 2 * tokens)]
    if step.first and not step.last:
        out_specs.append(extended)
        out_shape.append(qa_shape)
    if step.last:
        out_specs += [by_head, extended]
        out_shape += [q_shape, qa_shape]
        scratch += [pltpu.VMEM((PER, *shape), F32) for shape in state_shapes]
    else:
        out_specs += [extended, m_spec]
        out_shape += [jax.ShapeDtypeStruct((pairs, *shape), F32) for shape in state_shapes]
    if make_q:
        scratch.append(pltpu.VMEM((tokens, width), BF16))
    call = pl.pallas_call(
        functools.partial(attend_step_kernel, step, [len(group) for group in xs]),
        grid_spec=pltpu.PrefetchScalarGridSpec(
            num_scalar_prefetch=1, grid=(pairs // PER,), in_specs=in_specs + step.w.specs(), out_specs=out_specs, scratch_shapes=scratch
        ),
        out_shape=out_shape,
        name=step.name,
        compiler_params=params(60),
        cost_estimate=cost(sum(keys) / 32),
    )
    out = list(call(scalars, *args, *step.w.arrays))
    q = out.pop(0) if make_q else q
    count = len(xs)
    return q, *[out[at * count : (at + 1) * count] for at in range(4)], out[4 * count :]


def back_step_kernel(step, count, sc_ref, *refs):
    refs = list(refs)

    def take(number):
        return [refs.pop(0) for _ in range(number)]

    qa_ref, ga_ref, q_ref, do_ref, k_ref, v_ref, kaug_ref, r_ref, a_ref, b_ref = take(10)
    xs = take(count)
    dqt_in, sums_in = (None, None) if step.first else take(2)
    query = step.causal and step.last
    d1_ref = take(1)[0] if query else None
    pieces = take(len(step.w.arrays))
    dq_all = None
    if query:
        base_ref, grads_ref, w_ref, dk_all, dv_all, sems, dq_all = refs
    elif step.last:
        own_ref, part_ref, dq_ref, grads_ref, w_ref, dk_all, dv_all, sems = refs
    else:
        part_ref, dqt_ref, sums_ref, w_ref, dk_all, dv_all, sems = refs
    h = pl.program_id(0)
    final = h == pl.num_programs(0) - 1
    width = a_ref.shape[-1]
    parts = step.parts
    slots = a_ref.shape[1]
    keys = k_ref.shape[0]
    block = min(keys, 512)
    (at,) = step.blocks

    def weights():
        return [step.w.bring(pieces, sc_ref[1], part, w_ref.at[place], sems.at[place]) for place, part in enumerate(parts)]

    @step.on(sc_ref, at, h == 0)
    def _():
        for part in weights():
            start_all(part)

    @step.on(sc_ref, at)
    def _():
        for pair in range(PER):
            cols, all_cols = pair_cols(pair), head_cols(pair)
            q = split_pair(q_ref[:, cols] * jnp.asarray(SCALE, BF16))
            grads = split_pair(do_ref[:, cols])
            total = None
            for low in range(0, keys, block):
                span = slice(low, low + block)
                grad_q, grad_keys, grad_values = block_back(
                    k_ref[span, cols], v_ref[span, cols], kaug_ref[span], qa_ref[pair], ga_ref[pair], q, grads, step.causal and at == 0
                )
                dk_all[span, all_cols] = grad_keys
                dv_all[span, all_cols] = grad_values
                total = grad_q if total is None else total + grad_q
            if not step.first:
                total = total + dqt_in[pair]
            if query:
                dq_all[:, all_cols] = (total * SCALE).T.astype(BF16)
            elif step.last:
                dq_ref[:, cols] = (total * SCALE).T.astype(BF16)
            else:
                dqt_ref[pair] = total

    if step.causal and at:

        @pl.when(sc_ref[0] < at)
        def _():
            dqt_ref[...] = jnp.zeros_like(dqt_ref[...]) if step.first else dqt_in[...]

            @pl.when(final)
            def _():
                part_ref[...] = jnp.zeros_like(part_ref)
                sums_ref[...] = jnp.zeros_like(sums_ref) if step.first else sums_in[...]

    @step.on(sc_ref, at, final)
    def _():
        grads = [dq_all, dk_all, dv_all] if query else [dk_all, dv_all]
        shift = slots - len(grads)
        drs, dbs = [], []
        hidden = r_ref[...]
        for place, grad_ref in enumerate(grads):
            slot = place + shift
            grad = grad_ref[...]
            drs.append(low_rank(grad, b_ref[0, slot, 0]))
            dbs.append(tn(hidden[:, slot * RANK : (slot + 1) * RANK], grad))
        dr = jnp.concatenate(drs, axis=1)
        low, da = 0, None
        for x_ref in xs:
            part = tn(dr[low : low + x_ref.shape[0]], x_ref[...])
            da = part if da is None else da + part
            low += x_ref.shape[0]
        olds = [None] * 4 if step.first else [sums_in[place * RANK : (place + 1) * RANK] for place in range(4)]
        if query:
            olds = [None, *olds[:2], None, *olds[2:]]
        total = [da[place * RANK : (place + 1) * RANK] for place in range(len(grads))] + dbs
        target = grads_ref if step.last else sums_ref
        for place, (new, old) in enumerate(zip(total, olds)):
            target[place * RANK : (place + 1) * RANK] = (new if old is None else new + old).astype(target.dtype)
        for part in weights():
            wait_all(part)
        own = keys // count if step.last and not query else 0

        def body(cols):
            table = a_ref[0, shift:, 0, :, cols].reshape(len(grads) * RANK, COLS)
            value = nn(dr, table)
            for place, grad_ref in enumerate(grads):
                value = value + nt(grad_ref[...], w_ref[place, cols, :])
            if query:
                base_ref[:, cols] = value + d1_ref[:, cols]
            elif step.last:
                own_ref[:, cols] = value[:own]
                part_ref[:, cols] = value[own:].astype(BF16)
            else:
                part_ref[:, cols] = value.astype(BF16)

        each(width, COLS, body)


def back_step(step, scalars, qa, ga, q, do, k, v, kaug, r, xs, block_rows, tables, state, d1):
    tokens, width = q.shape
    pairs = width // PAIR
    keys = k.shape[0]
    slots = 3 if step.causal else 2
    query = step.causal and step.last
    by_head = pl.BlockSpec((tokens, PER * PAIR), lambda h, s: (0, h))
    keys_by_head = pl.BlockSpec((keys, PER * PAIR), lambda h, s: (0, h))
    extended = pl.BlockSpec((PER, PAIR + AUG, 2 * tokens), lambda h, s: (h, 0, 0))
    dqt_spec = pl.BlockSpec((PER, PAIR, tokens), lambda h, s: (h, 0, 0))

    def whole(rows):
        return pl.BlockSpec((rows, width), lambda h, s: (0, 0))

    adapters = adapter_spec(0 if step.causal else 4, slots, width)
    in_specs = [
        extended,
        extended,
        by_head,
        by_head,
        keys_by_head,
        keys_by_head,
        pl.BlockSpec((keys, AUG), lambda h, s: (0, 0)),
        pl.BlockSpec((keys, slots * RANK), lambda h, s: (0, 0)),
        adapters,
        adapters,
        *[whole(block_rows)] * len(xs),
    ]
    args = [qa, ga, q, do, k, v, kaug, r, *tables, *xs]
    if not step.first:
        in_specs += [dqt_spec, whole(4 * RANK)]
        args += state
    scratch = [pltpu.VMEM((len(step.parts), width, width), BF16), pltpu.VMEM((keys, width), BF16), pltpu.VMEM((keys, width), BF16)]
    scratch.append(step.w.sems(len(step.parts)))
    if query:
        in_specs.append(whole(tokens))
        args.append(d1)
        scratch.append(pltpu.VMEM((tokens, width), BF16))
        out_specs = [whole(tokens), whole(6 * RANK)]
        out_shape = [jax.ShapeDtypeStruct((tokens, width), F32), jax.ShapeDtypeStruct((6 * RANK, width), BF16)]
    elif step.last:
        rest = keys - block_rows
        out_specs = [whole(block_rows), whole(rest), by_head, whole(4 * RANK)]
        out_shape = [
            jax.ShapeDtypeStruct((block_rows, width), F32),
            jax.ShapeDtypeStruct((rest, width), BF16),
            jax.ShapeDtypeStruct((tokens, width), BF16),
            jax.ShapeDtypeStruct((4 * RANK, width), BF16),
        ]
    else:
        out_specs = [whole(keys), dqt_spec, whole(4 * RANK)]
        out_shape = [
            jax.ShapeDtypeStruct((keys, width), BF16),
            jax.ShapeDtypeStruct((pairs, PAIR, tokens), F32),
            jax.ShapeDtypeStruct((4 * RANK, width), F32),
        ]
    return pl.pallas_call(
        functools.partial(back_step_kernel, step, len(xs)),
        grid_spec=pltpu.PrefetchScalarGridSpec(
            num_scalar_prefetch=1, grid=(pairs // PER,), in_specs=in_specs + step.w.specs(), out_specs=out_specs, scratch_shapes=scratch
        ),
        out_shape=out_shape,
        name=step.name,
        compiler_params=params(60),
        cost_estimate=cost(keys / 24),
    )(scalars, *args, *step.w.arrays)


ROWS = 64


def normalize_rows(u_ref, norm_ref, low_ref, std_ref):
    def body(rows):
        values = u_ref[rows, :]
        centered = values - jnp.mean(values, -1, keepdims=True)
        inv_std = lax.rsqrt(jnp.mean(centered * centered, -1, keepdims=True) + NORM_EPS)
        normed = centered * inv_std
        norm_ref[rows, :] = normed
        low_ref[rows, :] = normed.astype(BF16)
        std_ref[rows, :] = inv_std

    each(u_ref.shape[0], ROWS, body)


def normalize_back(grads, normed, inv_std):
    return inv_std * (grads - jnp.mean(grads, -1, keepdims=True) - normed * jnp.mean(grads * normed, -1, keepdims=True))


def mid_kernel(w, part, query, sc_ref, o_ref, x_ref, a_ref, b_ref, aq_ref, bq_ref, *refs):
    pieces, refs = refs[: len(w.arrays)], refs[len(w.arrays) :]
    if query:
        norm_ref, low_ref, std_ref, r_ref, q_ref, w_ref, u_ref, sems = refs
    else:
        norm_ref, low_ref, std_ref, r_ref, w_ref, u_ref, sems = refs
    width = x_ref.shape[1]
    first = w.bring(pieces, sc_ref[1], part, w_ref.at[0], sems.at[0])
    start_all(first)
    if query:
        second = w.bring(pieces, sc_ref[1], 2, w_ref.at[1], sems.at[1])
        start_all(second)
    o = o_ref[...]
    hidden = low_rank(o, a_ref[0, 0, 0])
    r_ref[:, :RANK] = hidden
    wait_all(first)

    def body(cols):
        u_ref[:, cols] = x_ref[:, cols].astype(F32) + nn(o, w_ref[0, :, cols]) + nn(hidden, b_ref[0, 0, 0, :, cols])

    each(width, COLS, body)
    normalize_rows(u_ref, norm_ref, low_ref, std_ref)
    if query:
        low = low_ref[...]
        hidden_q = low_rank(low, aq_ref[0, 0, 0])
        r_ref[:, RANK:] = hidden_q
        wait_all(second)
        project_into(q_ref, low, w_ref.at[1], hidden_q, lambda cols: bq_ref[0, 0, 0, :, cols])


def mid(name, scalars, outs, residual, part, proj, query, proj_down, proj_up, w):
    rows, width = outs.shape
    shapes = [
        jax.ShapeDtypeStruct((rows, width), F32),
        jax.ShapeDtypeStruct((rows, width), BF16),
        jax.ShapeDtypeStruct((rows, 1), F32),
        jax.ShapeDtypeStruct((rows, 2 * RANK if query else RANK), BF16),
    ]
    if query:
        shapes.append(jax.ShapeDtypeStruct((rows, width), BF16))
    spec, spec_q = adapter_spec(proj, 1, width), adapter_spec(3, 1, width)
    return pl.pallas_call(
        functools.partial(mid_kernel, w, part, query),
        grid_spec=pltpu.PrefetchScalarGridSpec(
            num_scalar_prefetch=1,
            grid=(1,),
            in_specs=[WHOLE, WHOLE, spec, spec, spec_q, spec_q, *w.specs()],
            out_specs=[WHOLE] * len(shapes),
            scratch_shapes=[pltpu.VMEM((2, width, width), BF16), pltpu.VMEM((rows, width), F32), w.sems(2)],
        ),
        out_shape=shapes,
        name=name,
        compiler_params=params(60),
        cost_estimate=cost(1),
    )(scalars, outs, residual, proj_down, proj_up, proj_down, proj_up, *w.arrays)


def gelu_kernel(sc_ref, x_ref, a_ref, b_ref, w_in, g_ref, slope_ref, r_ref, w_ref, low, sems):
    at = pl.program_id(0)
    run = g_ref.shape[1]

    def column(step):
        cols = pl.ds(pl.multiple_of(step * run, run), run)
        return pltpu.make_async_copy(w_in.at[:, cols], w_ref.at[:, cols], sems.at[step])

    @pl.when(at == 0)
    def _():
        for step in range(w_in.shape[1] // run):
            column(step).start()
        low[...] = low_rank(x_ref[...], a_ref[0, 0])
        r_ref[...] = low[...]

    column(at).wait()

    def body(cols):
        across = pl.ds(pl.multiple_of(at * run, run) + cols.start, COLS)
        pre = nn(x_ref[...], w_ref[:, across]) + nn(low[...], b_ref[0, 0, :, cols])
        phi = 0.5 * (1.0 + lax.erf(pre * 0.7071067811865476))
        g_ref[:, cols] = (pre * phi).astype(BF16)
        slope_ref[:, cols] = (phi + pre * jnp.exp(-0.5 * pre * pre) * 0.3989422804014327).astype(BF16)

    each(run, COLS, body)


def gelu_up(scalars, x, down, up, w):
    rows, width = x.shape
    wide = up.shape[3]
    by_column = pl.BlockSpec((rows, width), lambda c, s: (0, c))
    return pl.pallas_call(
        gelu_kernel,
        grid_spec=pltpu.PrefetchScalarGridSpec(
            num_scalar_prefetch=1,
            grid=(wide // width,),
            in_specs=[
                pl.BlockSpec((rows, width), lambda c, s: (0, 0)),
                mlp_adapter_spec(width),
                pl.BlockSpec((1, 1, RANK, width), lambda c, s: (0, s[2], 0, c)),
                ANY,
            ],
            out_specs=[by_column, by_column, pl.BlockSpec((rows, RANK), lambda c, s: (0, 0))],
            scratch_shapes=[pltpu.VMEM((width, wide), BF16), pltpu.VMEM((rows, RANK), BF16), pltpu.SemaphoreType.DMA((wide // width,))],
        ),
        out_shape=[
            jax.ShapeDtypeStruct((rows, wide), BF16),
            jax.ShapeDtypeStruct((rows, wide), BF16),
            jax.ShapeDtypeStruct((rows, RANK), BF16),
        ],
        name="gelu_up",
        compiler_params=params(60),
        cost_estimate=cost(15),
    )(scalars, x, down, up, *w.arrays)


FC_ROWS = {"da1": 0, "db1": 16, "da2": 80, "db2": 144, "da_co": 160, "db_co": 176, "pick": 192}
FC_TOTAL = 208


def mlp_kernel(w_up, w_down, w_mid, sc_ref, g_in, slope_in, h2_in, h2_low_in, std2_ref, cot_in, r1_ref, rco_ref, oc_in,
               a1_ref, b1_ref, a2_ref, b2_ref, a7_ref, b7_ref, *refs):
    ups, refs = refs[: len(w_up.arrays)], refs[len(w_up.arrays) :]
    downs, refs = refs[: len(w_down.arrays)], refs[len(w_down.arrays) :]
    mids, refs = refs[: len(w_mid.arrays)], refs[len(w_mid.arrays) :]
    y_ref, d2_ref, doc_ref, gac_ref, grads_ref, w1, w2, wco, u, low, dpre, sem1, sem2, sem3, *local = refs
    g_ref, slope_ref, h2_ref, h2_low_ref, cot_ref, oc_ref, sem4 = local
    rows, width = h2_ref.shape
    wide = g_ref.shape[1]
    own = sc_ref[1]
    pairs = ((g_in, g_ref), (h2_in, h2_ref), (cot_in, cot_ref), (slope_in, slope_ref), (h2_low_in, h2_low_ref), (oc_in, oc_ref))
    inputs = [pltpu.make_async_copy(source, target, sem4.at[at]) for at, (source, target) in enumerate(pairs)]
    inputs[0].start()
    copies2 = w_down.bring(downs, own, 0, w2, sem2.at[0])
    copies1 = w_up.bring(ups, own, 0, w1, sem1.at[0])
    copies3 = w_mid.bring(mids, own, 1, wco, sem3.at[0])
    start_all(copies2)
    start_all(inputs[1:])
    start_all(copies1)
    start_all(copies3)
    inputs[0].wait()
    g = g_ref[...]
    r2 = low_rank(g, a2_ref[0, 0])
    wait_all(copies2)
    inputs[1].wait()

    def second(cols):
        u[:, cols] = h2_ref[:, cols] + nn(g_ref[...], w2[:, cols]) + nn(r2, b2_ref[0, 0, :, cols])

    each(width, COLS, second)

    def third(at):
        values = u[at, :]
        centered = values - jnp.mean(values, -1, keepdims=True)
        inv_std = lax.rsqrt(jnp.mean(centered * centered, -1, keepdims=True) + NORM_EPS)
        normed = centered * inv_std
        y_ref[at, :] = normed.astype(BF16)
        d3 = normalize_back(cot_ref[at, :].astype(F32), normed, inv_std)
        u[at, :] = d3
        low[at, :] = d3.astype(BF16)

    inputs[2].wait()
    each(rows, ROWS, third)
    wait_all(inputs[3:])
    d3_low = low[...]
    grads_ref[pl.ds(FC_ROWS["db2"], RANK), :] = tn(r2, d3_low).astype(BF16)
    dr2 = low_rank(d3_low, b2_ref[0, 0])
    r1 = r1_ref[...]
    run = 2 * COLS
    runs = width // run

    def slopes(at, carry):
        cols = pl.ds(pl.multiple_of(at * run, run), run)
        down_rows = nt(low[...], w2[cols, :]) + nn(dr2, a2_ref[0, 0, :, cols])
        part = (down_rows * slope_ref[:, cols].astype(F32)).astype(BF16)
        dpre[:, cols] = part
        row = pl.multiple_of((at // runs) * RANK, RANK)
        place = pl.ds(pl.multiple_of((at % runs) * run, run), run)
        grads_ref[pl.ds(FC_ROWS["da2"] + row, RANK), place] = tn(dr2, g_ref[:, cols]).astype(BF16)
        grads_ref[pl.ds(FC_ROWS["db1"] + row, RANK), place] = tn(r1, part).astype(BF16)
        return carry

    lax.fori_loop(0, wide // run, slopes, 0, unroll=2)
    dr1 = low_rank(dpre[...], b1_ref[0, 0])
    grads_ref[pl.ds(FC_ROWS["da1"], RANK), :] = tn(dr1, h2_low_ref[...]).astype(BF16)
    wait_all(copies1)

    def first(cols):
        u[:, cols] += nt(dpre[...], w1[cols, :]) + nn(dr1, a1_ref[0, 0, :, cols])

    each(width, COLS, first)

    def norm(at):
        d2 = normalize_back(u[at, :], h2_ref[at, :], std2_ref[at, :])
        d2_ref[at, :] = d2
        low[at, :] = d2.astype(BF16)

    each(rows, ROWS, norm)
    wait_all(copies3)
    d2_low = low[...]
    grads_ref[pl.ds(FC_ROWS["db_co"], RANK), :] = tn(rco_ref[...], d2_low).astype(BF16)
    drc = low_rank(d2_low, b7_ref[0, 0, 0])
    grads_ref[pl.ds(FC_ROWS["da_co"], RANK), :] = tn(drc, oc_ref[...]).astype(BF16)

    def cross(cols):
        doc_ref[:, cols] = (nt(low[...], wco[cols, :]) + nn(drc, a7_ref[0, 0, 0, :, cols])).astype(BF16)

    each(width, COLS, cross)
    slope_rows(gac_ref, doc_ref, oc_ref)
    mine = jnp.where(sc_ref[0] == 0, sc_ref[2], 0).astype(F32)
    grads_ref[pl.ds(FC_ROWS["pick"], 16), :] = jnp.full((16, width), mine, F32).astype(BF16)


def mlp(scalars, g, slope, h2, h2_low, std2, cot, r1, rco, oc, fc1_down, fc1_up, fc2_down, fc2_up, proj_down, proj_up, w_up, w_down, w_mid):
    rows, width = h2.shape
    wide = g.shape[1]
    return pl.pallas_call(
        functools.partial(mlp_kernel, w_up, w_down, w_mid),
        grid_spec=pltpu.PrefetchScalarGridSpec(
            num_scalar_prefetch=1,
            grid=(1,),
            in_specs=[
                *[ANY] * 4, WHOLE, ANY, WHOLE, WHOLE, ANY,
                mlp_adapter_spec(width),
                mlp_adapter_spec(wide),
                mlp_adapter_spec(wide),
                mlp_adapter_spec(width),
                adapter_spec(7, 1, width),
                adapter_spec(7, 1, width),
                *w_up.specs(),
                *w_down.specs(),
                *w_mid.specs(),
            ],
            out_specs=[WHOLE] * 5,
            scratch_shapes=[
                pltpu.VMEM((width, wide), BF16),
                pltpu.VMEM((wide, width), BF16),
                pltpu.VMEM((width, width), BF16),
                pltpu.VMEM((rows, width), F32),
                pltpu.VMEM((rows, width), BF16),
                pltpu.VMEM((rows, wide), BF16),
                w_up.sems(1),
                w_down.sems(1),
                w_mid.sems(1),
                pltpu.VMEM((rows, wide), BF16),
                pltpu.VMEM((rows, wide), BF16),
                pltpu.VMEM((rows, width), F32),
                pltpu.VMEM((rows, width), BF16),
                pltpu.VMEM((rows, width), BF16),
                pltpu.VMEM((rows, width), BF16),
                pltpu.SemaphoreType.DMA((6,)),
            ],
        ),
        out_shape=[
            jax.ShapeDtypeStruct((rows, width), BF16),
            jax.ShapeDtypeStruct((rows, width), F32),
            jax.ShapeDtypeStruct((rows, width), BF16),
            jax.ShapeDtypeStruct((width // PAIR, PAIR + AUG, 2 * rows), BF16),
            jax.ShapeDtypeStruct((FC_TOTAL, width), BF16),
        ],
        name="mlp",
        compiler_params=params(60),
        cost_estimate=cost(33),
    )(scalars, g, slope, h2, h2_low, std2, cot, r1, rco, oc, fc1_down, fc1_up, fc2_down, fc2_up, proj_down, proj_up,
      *w_up.arrays, *w_down.arrays, *w_mid.arrays)


def mid_back_kernel(w, sc_ref, dqc_ref, d2_ref, h1_ref, h1_low_ref, std1_ref, r_ref, o_ref, aq_ref, bq_ref, a_ref, b_ref, *refs):
    pieces, refs = refs[: len(w.arrays)], refs[len(w.arrays) :]
    d1_ref, do_ref, ga_ref, grads_ref, w_ref, low, sems = refs
    rows, width = d2_ref.shape
    first = w.bring(pieces, sc_ref[1], 2, w_ref.at[1], sems.at[1])
    second = w.bring(pieces, sc_ref[1], 0, w_ref.at[0], sems.at[0])
    start_all(first)
    start_all(second)
    dqc = dqc_ref[...]
    drq = low_rank(dqc, bq_ref[0, 0, 0])
    grads_ref[0:RANK, :] = tn(drq, h1_low_ref[...]).astype(BF16)
    grads_ref[2 * RANK : 3 * RANK, :] = tn(r_ref[:, RANK:], dqc).astype(BF16)
    wait_all(first)

    def query(cols):
        d1_ref[:, cols] = d2_ref[:, cols] + nt(dqc_ref[...], w_ref[1, cols, :]) + nn(drq, aq_ref[0, 0, 0, :, cols])

    each(width, COLS, query)

    def norm(at):
        d1 = normalize_back(d1_ref[at, :], h1_ref[at, :], std1_ref[at, :])
        d1_ref[at, :] = d1
        low[at, :] = d1.astype(BF16)

    each(rows, ROWS, norm)
    wait_all(second)
    d1_low = low[...]
    dr = low_rank(d1_low, b_ref[0, 0, 0])
    grads_ref[RANK : 2 * RANK, :] = tn(dr, o_ref[...]).astype(BF16)
    grads_ref[3 * RANK :, :] = tn(r_ref[:, :RANK], d1_low).astype(BF16)

    def out(cols):
        do_ref[:, cols] = (nt(low[...], w_ref[0, cols, :]) + nn(dr, a_ref[0, 0, 0, :, cols])).astype(BF16)

    each(width, COLS, out)

    slope_rows(ga_ref, do_ref, o_ref)


def mid_back(scalars, dqc, d2, h1, h1_low, std1, r, o, proj_down, proj_up, w):
    rows, width = d2.shape
    spec, spec_q = adapter_spec(6, 1, width), adapter_spec(3, 1, width)
    return pl.pallas_call(
        functools.partial(mid_back_kernel, w),
        grid_spec=pltpu.PrefetchScalarGridSpec(
            num_scalar_prefetch=1,
            grid=(1,),
            in_specs=[*[WHOLE] * 7, spec_q, spec_q, spec, spec, *w.specs()],
            out_specs=[WHOLE] * 4,
            scratch_shapes=[pltpu.VMEM((2, width, width), BF16), pltpu.VMEM((rows, width), BF16), w.sems(2)],
        ),
        out_shape=[
            jax.ShapeDtypeStruct((rows, width), F32),
            jax.ShapeDtypeStruct((rows, width), BF16),
            jax.ShapeDtypeStruct((width // PAIR, PAIR + AUG, 2 * rows), BF16),
            jax.ShapeDtypeStruct((4 * RANK, width), BF16),
        ],
        name="mid_back",
        compiler_params=params(60),
        cost_estimate=cost(1),
    )(scalars, dqc, d2, h1, h1_low, std1, r, o, proj_down, proj_up, proj_down, proj_up, *w.arrays)


def add_picked(picks_ref, sequences, out, source):
    adapters, view = out
    for adapter in range(adapters):
        view(adapter)[...] = jnp.zeros(view(adapter).shape, F32)
    for at in range(sequences):
        target = view(picks_ref[at])
        target[...] += source(at).astype(F32)


def fc_total_kernel(picks_ref, g_ref, a1_ref, b1_ref, a2_ref, b2_ref):
    sequences, _, width = g_ref.shape
    adapters = a1_ref.shape[1]

    def put(out_ref, col, row):
        def view(adapter):
            return out_ref.at[0, adapter, :, pl.ds(col, width)]

        add_picked(picks_ref, sequences, (adapters, view), lambda at: g_ref[at, pl.ds(row, RANK), :])

    for out_ref, name in ((a1_ref, "da1"), (b1_ref, "db1"), (a2_ref, "da2"), (b2_ref, "db2")):
        for at in range(out_ref.shape[3] // width):
            put(out_ref, at * width, FC_ROWS[name] + at * RANK)


def fc_total(picks, gathered, shapes):
    return pl.pallas_call(
        fc_total_kernel,
        grid_spec=pltpu.PrefetchScalarGridSpec(
            num_scalar_prefetch=1, grid=(1,), in_specs=[WHOLE], out_specs=[WHOLE] * 4
        ),
        out_shape=[jax.ShapeDtypeStruct(s, F32) for s in shapes],
        name="fc_total",
        compiler_params=params(60),
        cost_estimate=cost(6),
    )(picks, gathered)


PROJ_ROWS = {
    0: (2, 0, 48),
    1: (2, 16, 64),
    2: (2, 32, 80),
    3: (1, 0, 32),
    4: (1, 64, 96),
    5: (1, 80, 112),
    6: (1, 16, 48),
    7: (0, FC_ROWS["da_co"], FC_ROWS["db_co"]),
}


def proj_total_kernel(projs, first_source, count, sources, picks_ref, *refs):
    g_refs, (down_ref, up_ref) = refs[:sources], refs[-2:]
    adapters = down_ref.shape[2]
    for at, proj in enumerate(projs):
        source, down_row, up_row = PROJ_ROWS[proj]
        g_ref = g_refs[source - first_source]

        @pl.when(pl.program_id(0) == at)
        def _(g_ref=g_ref, down_row=down_row, up_row=up_row):
            for out_ref, row in ((down_ref, down_row), (up_ref, up_row)):
                add_picked(
                    picks_ref, g_ref.shape[0], (adapters, lambda adapter, out_ref=out_ref: out_ref.at[0, 0, adapter]),
                    lambda at, row=row: g_ref[at, pl.ds(row, RANK), :],
                )


def proj_total(picks, gathered, projs, so_far, shape):
    first = projs[0]
    block = pl.BlockSpec((1, 1, *shape[2:]), lambda p, s: (0, p + first, 0, 0, 0))
    rest = [] if so_far is None else list(so_far)
    first_source = min(PROJ_ROWS[proj][0] for proj in projs)
    return pl.pallas_call(
        functools.partial(proj_total_kernel, tuple(projs), first_source, len(rest), len(gathered)),
        grid_spec=pltpu.PrefetchScalarGridSpec(
            num_scalar_prefetch=1,
            grid=(len(projs),),
            in_specs=[WHOLE] * len(gathered) + [ANY] * len(rest),
            out_specs=[block] * 2,
        ),
        out_shape=[jax.ShapeDtypeStruct(shape, F32)] * 2,
        input_output_aliases={1 + len(gathered) + at: at for at in range(len(rest))},
        name=f"proj_total_{first}",
        compiler_params=params(60),
        cost_estimate=cost(1.4 * len(projs)),
    )(picks, *gathered, *rest)


class Gathering:
    def __init__(self, shard, parts, across, sibling, together):
        self.shard, self.parts, self.across, self.sibling, self.together = shard, parts, across, sibling, together
        self.half = shard.shape[0] // 2

    def begin(self):
        self.x, self.y = self.across(self.shard, 1), self.across(self.shard, 2)
        self.own = self.sibling(self.shard)

    def forward(self):
        self.xy, self.yx = self.across(self.x[: self.half], 2), self.across(self.y[self.half :], 1)
        if self.together:
            self.near = [self.sibling(jnp.concatenate([self.x, self.y], axis=0))]
        else:
            self.near = [self.sibling(self.x), self.sibling(self.y)]

    def share(self):
        self.far = self.sibling(jnp.concatenate([self.xy, self.yx], axis=0))

    def result(self):
        rows, half = self.shard.shape[0], self.half
        arrays = [self.shard, self.own, self.x, self.y, *self.near, self.xy, self.yx, self.far]
        layout = [[(0, True, who, 0, rows)] for who in (0, 1, 2, 4)]
        if self.together:
            layout += [[(0, True, 3, 0, rows), (rows, True, 5, 0, rows)]]
        else:
            layout += [[(0, True, 3, 0, rows)], [(0, True, 5, 0, rows)]]
        layout += [[(0, True, 6, 0, half)], [(0, True, 6, half, rows - half)]]
        layout += [[(0, True, 7, 0, half), (half, True, 7, half, rows - half)]]
        return Gathered(arrays, layout, rows // self.parts)


class Whole:
    def __init__(self, shard, parts, shards, gather):
        self.shard, self.parts, self.shards, self.gather = shard, parts, shards, gather
        self.x = self.y = self.own = self.xy = self.yx = self.far = shard
        self.near = []

    def begin(self):
        self.whole = self.gather(self.shard)

    def forward(self):
        pass

    def share(self):
        pass

    def result(self):
        rows = self.shard.shape[0]
        return Gathered([self.whole], [[(at * rows, False, at, 0, rows) for at in range(self.shards)]], rows // self.parts)


def make_shards(mesh):
    chips, span = mesh.shape["chip"], mesh.shape["sp"]
    plane = ("chip", "core")

    def tie(*values):
        return lax.optimization_barrier(values)

    def turn(values, by):
        return lax.ppermute(values, "sp", [(i, (i + by) % span) for i in range(span)])

    def swap(values, bit):
        return lax.ppermute(values, "sp", [(i, i ^ bit) for i in range(span)])

    def across(values, bit):
        return lax.ppermute(values, "chip", [(i, i ^ bit) for i in range(chips)])

    def sibling(values):
        return lax.ppermute(values, "core", [(0, 1), (1, 0)])

    def gathering(shard, parts, steps, together=False):
        if chips == 4 and steps:
            return Gathering(shard, parts, across, sibling, together)
        return Whole(shard, parts, 2 * chips, lambda v: lax.all_gather(v, plane, axis=0, tiled=True))

    def shards(
        inputs,
        segments,
        enc_states,
        adapter_pick,
        qkv_weights,
        out_weights,
        mlp_in,
        mlp_out,
        proj_down,
        proj_up,
        fc1_down,
        fc1_up,
        fc2_down,
        fc2_up,
        cotangent,
    ):
        x_low = inputs[0]
        memory = enc_states[0]
        tokens, width = x_low.shape
        mem_rows = memory.shape[0]
        own = lax.axis_index("chip") * 2 + lax.axis_index("core")
        scalars = jnp.stack([lax.axis_index("sp"), own, adapter_pick[0]]).astype(jnp.int32)
        tables = (proj_down, proj_up)

        a = gathering(qkv_weights[0, :3].reshape(-1, width), 3, True)
        b_shard = jnp.concatenate([out_weights[0].reshape(-1, width), qkv_weights[0, 3:].reshape(-1, width)], axis=0)
        b = gathering(b_shard, 5, True, True)
        c, d = gathering(mlp_in[0], 1, False), gathering(mlp_out[0], 1, True, True)

        seg_row = jnp.pad(segments.astype(BF16), ((0, 15), (0, width - tokens)))
        ext = [jnp.concatenate([x_low, seg_row], axis=0)]
        a.begin()
        ext.append(turn(ext[0], 1))
        a.x, a.y, a.own, ext[1] = tie(a.x, a.y, a.own, ext[1])
        a.forward()
        ext.append(turn(ext[1], 1))
        a.xy, a.yx, b.shard, *a.near = tie(a.xy, a.yx, b.shard, *a.near)
        a.share()
        b.begin()
        a.far, ext[2] = tie(a.far, ext[2])
        while len(ext) < span:
            ext.append(turn(ext[-1], 1))
        w_a = a.result()

        state, ks, vs, rs, augs = None, [], [], [], []
        q = o = None
        for at in range(0, span, 2):
            step = Step(f"self_{at}", w_a, (0, 1, 2) if at == 0 else (1, 2), (at, at + 1), at == 0, at == span - 2, True)
            if at:
                ext[at], ext[at + 1], state[1] = tie(ext[at], ext[at + 1], state[1])
            q, k, v, r, aug, out = attend_step(step, scalars, [[ext[at]], [ext[at + 1]]], tokens, tokens, tables, q, state)
            ks, vs, rs, augs = ks + k, vs + v, rs + r, augs + aug
            if at < span - 2:
                state = out if at == 0 else [state[0], *out]
            else:
                o, qa = out
            if at == 0:
                state[1], b.x, b.y, b.own, ext[-1], on, c.shard = tie(state[1], b.x, b.y, b.own, ext[-1], memory, c.shard)
                b.forward()
                c.begin()
                mems = [memory, turn(on, 1), *[None] * (span - 3), turn(on, -1)]
        o, mems[1], mems[-1], b.xy, b.yx, *b.near = tie(o, mems[1], mems[-1], b.xy, b.yx, *b.near)
        b.share()
        for by in range(2, span - 1):
            mems[by] = turn(mems[by - 1], 1)
        w_b = b.result()
        h1, h1_low, std1, r_mid, qc = mid("mid", scalars, o, x_low, 0, 6, True, *tables, w_b)
        qc, d.shard, *mems[1:] = tie(qc, d.shard, *mems[1:])
        d.begin()
        step = Step("cross", w_b, (3, 4), (0,), True, True, False)
        _, (kc,), (vc,), (r_mem,), (free_aug,), (oc, qca) = attend_step(step, scalars, [mems], tokens, mem_rows, tables, qc, None)
        h2, h2_low, std2, r_co = mid("mid_cross", scalars, oc, h1, 1, 7, False, *tables, w_b)
        h2_low, d.x, d.y, d.own = tie(h2_low, d.x, d.y, d.own)
        d.forward()
        w_c = c.result()
        g, slope, r_fc1 = gelu_up(scalars, h2_low, fc1_down, fc1_up, w_c)
        g, d.xy, d.yx, *d.near = tie(g, d.xy, d.yx, *d.near)
        d.share()
        w_d = d.result()
        y, d2, doc, gac, fc_grads = mlp(
            scalars, g, slope, h2, h2_low, std2, cotangent[0], r_fc1, r_co, oc,
            fc1_down, fc1_up, fc2_down, fc2_up, *tables, w_c, w_d, w_b,
        )
        g0 = lax.psum(fc_grads, "sp")

        step = Step("cross_back", w_b, (3, 4), (0,), True, True, False)
        dmem, parts, dqc, cross_grads = back_step(step, scalars, qca, gac, qc, doc, kc, vc, free_aug, r_mem, mems, mem_rows, tables, None, None)

        def mem_part(slot):
            return parts[(slot - 1) * mem_rows : slot * mem_rows]

        def added(slot, arrived):
            return (mem_part(slot).astype(F32) + arrived.astype(F32)).astype(BF16)

        middle = span // 2
        lower, upper = turn(mem_part(middle), -1), turn(mem_part(middle + 1), 1)
        d1, do, ga, mid_grads = mid_back(scalars, dqc, d2, h1, h1_low, std1, r_mid, o, *tables, w_b)
        ga, g0 = tie(ga, g0)
        g0, g1 = tie(g0, jnp.concatenate([mid_grads, cross_grads], axis=0))
        g1 = lax.psum(g1, "sp")
        g0 = g0[None]

        def doubled(values, bit):
            return jnp.concatenate([values, across(values, bit)], axis=0)

        bits = [1 << at for at in range(chips.bit_length() - 1)]
        state, moving, waiting, at_bit = None, None, [], 0
        for at in reversed(range(span)):
            step = Step(f"self_back_{at}", w_a, (0, 1, 2) if at == 0 else (1, 2), (at,), at == span - 1, at == 0, True)
            out = back_step(step, scalars, qa, ga, q, do, ks[at], vs[at], augs[at], rs[at], [ext[at]], tokens, tables, state, d1)
            if at == 0:
                dx, g2 = out
                g2, g0, g1, moving = tie(g2, g0, g1, moving)
            else:
                part, *state = out
                if at == span - 1:
                    part, state[0], lower, upper = tie(part, state[0], lower, upper)
                    for slot in range(middle - 1, 1, -1):
                        lower = turn(added(slot, lower), -1)
                    for slot in range(middle + 2, span):
                        upper = turn(added(slot, upper), 1)
                    lower = added(1, lower)
                    moving = turn(part, -1)
                elif at == 1:
                    waiting.append(part)
                    state[0], moving, lower, *waiting = tie(state[0], moving, lower, *waiting)
                    while len(waiting) > 1:
                        part = (waiting.pop(0).astype(F32) + moving.astype(F32)).astype(BF16)
                        part, state[0] = tie(part, state[0])
                        moving = turn(part, -1)
                else:
                    waiting.append(part)
                if at == span - 2:
                    g0, state[0], lower = tie(g0, state[0], lower)
                    lower = turn(lower, -1)
                if at >= span - 2 and at_bit < len(bits):
                    g0 = doubled(g0, bits[at_bit])
                    at_bit += 1
        while at_bit < len(bits):
            g0 = doubled(g0, bits[at_bit])
            at_bit += 1

        g0 = jnp.concatenate([g0, sibling(g0)], axis=0)
        g1 = doubled(g1[None], bits[0])
        g2 = (g2.astype(F32) + swap(g2, 1).astype(F32)).astype(BF16)
        g2, g1, g0 = tie(g2, g1, g0)
        for bit in bits[1:]:
            g1 = doubled(g1, bit)
        picks = g0[:, FC_ROWS["pick"], 0].astype(jnp.int32)
        fcs = fc_total(picks, g0, (fc1_down.shape, fc1_up.shape, fc2_down.shape, fc2_up.shape))
        bit = 2
        while bit < span:
            g2 = (g2.astype(F32) + swap(g2, bit).astype(F32)).astype(BF16)
            bit *= 2
        g2, g1, picks, moving, *fcs = tie(g2, g1, picks, moving, *fcs)
        moving = turn((waiting[0].astype(F32) + moving.astype(F32)).astype(BF16), -1)
        g1 = jnp.concatenate([g1, sibling(g1)], axis=0)
        g2 = doubled(g2[None], bits[0])
        g2, g1, picks = tie(g2, g1, picks)
        projs = proj_total(picks, (g0, g1), range(3, 8), None, proj_down.shape)
        for bit in bits[1:]:
            g2 = doubled(g2, bit)
        g2, moving, *projs = tie(g2, moving, *projs)
        g2 = jnp.concatenate([g2, sibling(g2)], axis=0)
        projs = list(proj_total(picks, (g2,), range(3), projs, proj_down.shape))
        dx = dx + moving.astype(F32)
        dmem = dmem + lower.astype(F32) + upper.astype(F32)
        return (y[None], dx[None], dmem[None], *projs, *fcs)

    return shards


def solution(mesh):
    count = mesh.shape["fsdp"]
    fine = Mesh(mesh.devices.reshape(count // 2, 2, mesh.shape["sp"]), ("chip", "core", "sp"))
    fsdp = ("chip", "core")
    row = P(fsdp, "sp", None)
    return jax.shard_map(
        make_shards(fine),
        mesh=fine,
        in_specs=(
            row,
            P(fsdp, "sp"),
            row,
            P(fsdp),
            P(None, None, fsdp, None),
            P(None, None, fsdp, None),
            P(None, fsdp, None),
            P(None, fsdp, None),
            P(),
            P(),
            P(),
            P(),
            P(),
            P(),
            row,
        ),
        out_specs=(row, row, row, P(), P(), P(), P(), P(), P()),
        check_vma=False,
    )
```
